32 devices in a mesh: wide: 8 (over y, x, core), narrow: 4 (over z).
Axes of the slice: x: 2, y: 2, z: 4, core: 2. Of those that a mesh axis runs over, the one named last changes fastest.
Arguments:
- tokens_in: bfloat16 [640, 24576], P('narrow', 'wide'), may hold values from -6 to 6
- ln1_gain: bfloat16 [640], P('narrow'), may hold values from 0.25 to 1.75
- ln1_shift: bfloat16 [640], P('narrow'), may hold values from -3 to 3
- w_qkv: bfloat16 [3, 640, 640], P(None, 'wide', 'narrow'), may hold values from -0.25 to 0.25
- qv_bias: bfloat16 [2, 640], P(None, 'narrow'), may hold values from -1 to 1
- w_out: bfloat16 [640, 640], P('narrow', 'wide'), may hold values from -1.25 to 1.25
- out_bias: bfloat16 [640], P('narrow'), may hold values from -3 to 3
- ln2_gain: bfloat16 [640], P('narrow'), may hold values from 0.25 to 1.75
- ln2_shift: bfloat16 [640], P('narrow'), may hold values from -3 to 3
- w_up: bfloat16 [640, 5120], P('narrow', 'wide'), may hold values from -0.25 to 0.25
- up_bias: bfloat16 [5120], P('wide'), may hold values from -3 to 3
- w_down: bfloat16 [5120, 640], P('wide', 'narrow'), may hold values from -0.078125 to 0.078125
- down_bias: bfloat16 [640], P('narrow'), may hold values from -3 to 3
- segment_ids: int32 [24576], P('wide'), may hold values from 0 to 191, never falling along the last dimension, each value on 1 to 256 neighbouring positions
- out_grad: bfloat16 [640, 24576], P('narrow', 'wide'), may hold values from -6 to 6
- predicted: int32 [24576], P('wide'), may hold values from 0 to 3
- labels: int32 [24576], P('wide'), may hold values from 0 to 4
Outputs:
- layer_out: bfloat16 [640, 24576], P('narrow', 'wide')
- tokens_grad: float32 [640, 24576], P('narrow', 'wide')
- ln1_gain_grad: float32 [640], P('narrow')
- ln1_shift_grad: float32 [640], P('narrow')
- w_qkv_grad: float32 [3, 640, 640], P(None, 'wide', 'narrow')
- qv_bias_grad: float32 [2, 640], P(None, 'narrow')
- w_out_grad: float32 [640, 640], P('narrow', 'wide')
- out_bias_grad: float32 [640], P('narrow')
- ln2_gain_grad: float32 [640], P('narrow')
- ln2_shift_grad: float32 [640], P('narrow')
- w_up_grad: float32 [640, 5120], P('narrow', 'wide')
- up_bias_grad: float32 [5120], P('wide')
- w_down_grad: float32 [5120, 640], P('wide', 'narrow')
- down_bias_grad: float32 [640], P('narrow')
- tallies: int32 [2, 4], replicated
- accuracy: float32 [], replicated
The draws below stay inside these ranges and needn't reach their ends.
Inputs may be any that keep to these rules, and one draw needn't show every extreme that they name: `segment_ids`: segment numbers never fall along the tokens, and one segment holds at most 256 tokens. `labels`: the value 4 marks a token that is not scored.
All inputs are finite; a program needn't handle non-finite values.
Results may differ from the reference program's by a relative error of at most 0.012.
Values may be sent and summed in bfloat16 or wider, within the bound.
No kernel may reach another device: no remote copies, remote signals or barrier semaphores. Data moves between devices by JAX's collectives and lax.ppermute only.
A program may use at most 256 MiB of HBM per device.

```python
import math
import jax
import jax.numpy as jnp
import numpy as np
from jax import lax

D = 640
HEADS = 20
HEAD_DIM = 32
FF = 5120
SEQ = 1024
CLASSES = 4
TOKENS = 24576


def plant(drawn, stream_key, low, top_value):
    longest = drawn.shape.index(max(drawn.shape))
    spots = []
    for shift in (0, 1):
        where = [jax.random.randint(jax.random.fold_in(stream_key, axis), (), 0, length) for axis, length in enumerate(drawn.shape)]
        where[longest] = (where[longest] + shift) % drawn.shape[longest]
        spots.append(tuple(where))
    return drawn.at[spots[0]].set(low).at[spots[1]].set(top_value)


def block_scale(stream_key, extent, pieces, smallest, top_value):
    def one(position, shards_of):
        heights = jax.random.uniform(jax.random.fold_in(jax.random.fold_in(stream_key, 6), position), (shards_of,), jnp.float32, smallest / len(pieces), top_value / len(pieces))
        return jnp.repeat(jnp.exp(heights), extent[position] // shards_of).reshape((-1,) + (1,) * (len(extent) - position - 1))

    level = one(*pieces[0])
    for cut in pieces[1:]:
        level = level * one(*cut)
    return level


def length_profile(count, total, limit, lean):
    weights = [(1 << 20) // math.isqrt(rank ** lean) + 1 for rank in range(2, count + 1)]
    surplus, counts = total - limit - (count - 1), [1] * (count - 1)
    while surplus > 0:
        free = [i for i in range(count - 1) if counts[i] < limit]
        mass, budget = sum([weights[i] for i in free]), surplus
        for i in free:
            more = min(limit - counts[i], max(1, budget * weights[i] // mass), surplus)
            counts[i] = counts[i] + more
            surplus = surplus - more
    return np.array([limit] + counts)


def uneven(own_key, count, total, most, skew):
    if count == 2:
        one = jax.random.randint(own_key, (), max(1, total - most), min(most, total - 1) + 1)
        return jnp.stack([one, total - one])
    lengths = jnp.asarray(length_profile(count, total, most, skew), jnp.int32)
    pairs = (count - 1) // 2
    source_of, sink = lengths[1:1 + 2 * pairs:2], lengths[2:2 + 2 * pairs:2]
    margin = jnp.minimum(source_of - 1, most - sink)
    shifted = jax.random.randint(jax.random.fold_in(own_key, 1), (pairs,), 0, 1 << 20) % (margin + 1)
    lengths = lengths.at[1:1 + 2 * pairs:2].set(source_of - shifted).at[2:2 + 2 * pairs:2].set(sink + shifted)
    return lengths[jax.random.permutation(jax.random.fold_in(own_key, 2), count)]


def noise(stream_key, shape, deviation, bound, split=(), kind=jnp.bfloat16):
    level = block_scale(stream_key, shape, split, -0.22, 0.18) if split else 1.0
    drawn = jax.random.normal(stream_key, shape, jnp.float32) * deviation * level
    return jnp.minimum(jnp.maximum(drawn, -bound), bound).astype(kind)


def setup_inputs(seed: int = 0) -> dict:
    arg_keys = jax.random.split(jax.random.key(seed), 18)
    return {
        "tokens_in": noise(arg_keys[0], (D, TOKENS), 1.0, 6.0, ((0, 4), (1, 8))),
        "ln1_gain": jnp.clip(1.0 + 0.15 * jax.random.normal(arg_keys[1], (D,), jnp.float32), 0.25, 1.75).astype(jnp.bfloat16),
        "ln1_shift": noise(arg_keys[2], (D,), 0.3, 3.0, ((0, 4),)),
        "w_qkv": noise(arg_keys[3], (3, D, D), D ** -0.5, 0.25, ((1, 8), (2, 4))),
        "qv_bias": noise(arg_keys[4], (2, D), 0.1, 1.0, ((1, 4),)),
        "w_out": noise(arg_keys[5], (D, D), (D // 32) ** -0.5, 1.25, ((0, 4), (1, 8))),
        "out_bias": noise(arg_keys[6], (D,), 0.3, 3.0, ((0, 4),)),
        "ln2_gain": jnp.clip(1.0 + 0.15 * jax.random.normal(arg_keys[7], (D,), jnp.float32), 0.25, 1.75).astype(jnp.bfloat16),
        "ln2_shift": noise(arg_keys[8], (D,), 0.3, 3.0, ((0, 4),)),
        "w_up": noise(arg_keys[9], (D, FF), D ** -0.5, 0.25, ((0, 4), (1, 8))),
        "up_bias": noise(arg_keys[10], (FF,), 0.3, 3.0, ((0, 8),)),
        "w_down": noise(arg_keys[11], (FF, D), FF ** -0.5, 0.078125, ((0, 8), (1, 4))),
        "down_bias": noise(arg_keys[12], (D,), 0.3, 3.0, ((0, 4),)),
        "segment_ids": jnp.searchsorted(jnp.cumsum(uneven(arg_keys[13], TOKENS // (SEQ // 8), TOKENS, SEQ // 4, 0)), jnp.arange(TOKENS), side="right").astype(jnp.int32),
        "out_grad": noise(arg_keys[14], (D, TOKENS), 1.0, 6.0, ((0, 4), (1, 8))),
        "predicted": plant(jax.random.randint(arg_keys[15], (TOKENS,), 0, CLASSES), jax.random.fold_in(arg_keys[15], 1), 0, CLASSES - 1).astype(jnp.int32),
        "labels": plant(jax.random.randint(arg_keys[16], (TOKENS,), 0, CLASSES + 1), jax.random.fold_in(arg_keys[16], 1), 0, CLASSES).astype(jnp.int32),
    }


@jax.custom_vjp
def low(v):
    return lax.optimization_barrier(v.astype(jnp.bfloat16)).astype(jnp.float32)

@jax.custom_vjp
def low_back(v):
    return v

def low_keep(v):
    return (low(v), None)

def low_pass(kept, grad):
    return (grad,)

def back_keep(v):
    return (v, None)

def back_low(kept, grad):
    return (low(grad),)
low.defvjp(low_keep, low_pass)
low_back.defvjp(back_keep, back_low)
EPS = 1e-05

def layer_norm(inputs, gain_vec, shift_vec):
    centre = lax.optimization_barrier(jnp.mean(inputs, axis=-1, keepdims=True))
    spread = lax.optimization_barrier(jnp.mean(jnp.square(inputs - centre), axis=-1, keepdims=True))
    return (inputs - centre) * lax.rsqrt(spread + EPS) * gain_vec + shift_vec

def matmul(left_op, right_op):
    return jnp.dot(left_op, right_op, precision=lax.Precision.HIGHEST)

def attend_group(block_in):
    queries, key_rows, value_rows, segments = block_in
    raw_scores = jnp.einsum('gqhd,gkhd->ghqk', queries, key_rows, precision=lax.Precision.HIGHEST)
    scores = low_back(raw_scores) * HEAD_DIM ** (-0.5)
    same_doc = segments[:, :, None] == segments[:, None, :]
    scores = jnp.where(same_doc[:, None], scores, -1e+30)
    attn_probs = low(jax.nn.softmax(scores, axis=-1))
    return jnp.einsum('ghqk,gkhd->gqhd', attn_probs, value_rows, precision=lax.Precision.HIGHEST)

def forward(tokens, ln1_gain, ln1_shift, w_qkv, qv_bias, w_out, out_bias, ln2_gain, ln2_shift, w_up, up_bias, w_down, down_bias, segment_ids):
    normed = low(layer_norm(tokens, ln1_gain, ln1_shift))
    queries = low(low_back(matmul(normed, w_qkv[0]) + qv_bias[0]))
    key_rows = low(low_back(matmul(normed, w_qkv[1])))
    value_rows = low(low_back(matmul(normed, w_qkv[2]) + qv_bias[1]))
    groups = TOKENS // (2 * SEQ)
    grid_shape = (groups, 2, SEQ, HEADS, HEAD_DIM)
    attended = lax.map(jax.checkpoint(attend_group), (queries.reshape(grid_shape), key_rows.reshape(grid_shape), value_rows.reshape(grid_shape), segment_ids.reshape(groups, 2, SEQ)))
    attended = low(low_back(attended.reshape(TOKENS, D)))
    branch = low_back(matmul(attended, w_out) + out_bias)
    middle = tokens + branch
    normed_two = low(layer_norm(middle, ln2_gain, ln2_shift))
    hidden = low_back(matmul(normed_two, w_up) + up_bias)
    activated = low(jax.nn.gelu(hidden, approximate=False))
    ffn_out = low_back(matmul(activated, w_down) + down_bias)
    return middle + ffn_out

def reference(tokens_in, ln1_gain, ln1_shift, w_qkv, qv_bias, w_out, out_bias, ln2_gain, ln2_shift, w_up, up_bias, w_down, down_bias, segment_ids, out_grad, predicted, labels):
    floats = tuple((array.astype(jnp.float32) for array in (tokens_in.T, ln1_gain, ln1_shift, w_qkv, qv_bias, w_out, out_bias, ln2_gain, ln2_shift, w_up, up_bias, w_down, down_bias)))

    def apply_layer(*params):
        return forward(*params, segment_ids)
    layer_val, pullback = jax.vjp(apply_layer, *floats)
    gradients = pullback(out_grad.T.astype(jnp.float32))
    class_ids = jnp.arange(CLASSES, dtype=jnp.int32)
    label_hits = labels[:, None] == class_ids
    correct = lax.optimization_barrier(jnp.sum(((predicted[:, None] == class_ids) & label_hits).astype(jnp.int32), axis=0))
    scored = lax.optimization_barrier(jnp.sum(label_hits.astype(jnp.int32), axis=0))
    tallies = jnp.stack([correct, scored])
    accuracy = jnp.sum(correct).astype(jnp.float32) / jnp.maximum(jnp.sum(scored), 1).astype(jnp.float32)
    return (layer_val.astype(jnp.bfloat16).T, gradients[0].T, gradients[1], gradients[2], gradients[3], gradients[4], gradients[5], gradients[6], gradients[7], gradients[8], gradients[9], gradients[10], gradients[11], gradients[12], tallies, accuracy)
```

```python
import functools

import jax
import jax.numpy as jnp
from jax import lax
from jax.experimental import pallas as pl
from jax.experimental.pallas import tpu as pltpu
from jax.sharding import PartitionSpec as P

HEAD_DIM = 32
SEQ = 1024
CLASSES = 4
LONGEST = 256
EPS = 1e-05
QT = 256
KT = 128
GROUP = 4
LANES = 128
LOG2E = 1.4426950408889634
SCALE = HEAD_DIM**-0.5
MASKED = -1e30
VMEM_LIMIT = 56 * 1024 * 1024
bf16, f32 = jnp.bfloat16, jnp.float32

NN = (((1,), (0,)), ((), ()))
NT = (((1,), (1,)), ((), ()))
TN = (((0,), (0,)), ((), ()))

PHI_P = 0.33
PHI_C = (
    0.1328227541618569,
    0.117797452145417,
    0.18652846971894854,
    -0.09893620415601319,
    0.3406397450924515,
    -0.22542553879715763,
    0.046573313873415075,
)


def mm(left, right, dims=NN):
    return lax.dot_general(left, right, dims, preferred_element_type=f32)


def normal_cdf(u):
    bell = jnp.exp(-0.5 * (u * u))
    t = 1.0 / (1.0 + PHI_P * jnp.abs(u))
    tail = jnp.full_like(t, PHI_C[-1])
    for c in PHI_C[-2::-1]:
        tail = tail * t + c
    tail = tail * t * bell
    return jnp.where(u >= 0, 1.0 - tail, tail), bell * 0.3989422804014327


def head_only(block, h, axis):
    index = lax.broadcasted_iota(jnp.int32, block.shape, axis)
    keep = (index >= h * HEAD_DIM) & (index < (h + 1) * HEAD_DIM)
    return jnp.where(keep, block, jnp.zeros_like(block))


def key_bias(segk_ref, segq_ref, start, window):
    segk = segk_ref[pl.ds(start, window), :]
    segk = jnp.concatenate([segk] * (QT // LANES), axis=1)
    return jnp.where(segk == segq_ref[0:1, :], 0.0, MASKED).astype(f32)


def attend_forward(start_ref, small_ref, q_ref, k_ref, vt_ref, segk_ref, segq_ref, att_ref, lse_ref):
    tile = pl.program_id(1)

    def run(window):
        start = pl.multiple_of(start_ref[tile] * KT, KT)
        keys = k_ref[pl.ds(start, window), :]
        bias = key_bias(segk_ref, segq_ref, start, window)
        q = q_ref[...]
        for h in range(GROUP):
            rows = slice(h * HEAD_DIM, (h + 1) * HEAD_DIM)
            scores = mm(keys, head_only(q, h, 0)) + bias
            top = jnp.max(scores, axis=0, keepdims=True)
            probs = jnp.exp2((scores - top) * (SCALE * LOG2E))
            total = jnp.sum(probs, axis=0, keepdims=True)
            out = mm(vt_ref[rows, pl.ds(start, window)], probs.astype(bf16))
            att_ref[rows, :] = (out / total).astype(bf16)
            lse_ref[h : h + 1, :] = top * (SCALE * LOG2E) + jnp.log2(total)

    @pl.when(small_ref[tile] == 1)
    def _():
        run(4 * KT)

    @pl.when(small_ref[tile] == 0)
    def _():
        run(6 * KT)


def attend_backward(
    start_ref, small_ref, qt_ref, q_ref, kt_ref, k_ref, v_ref, dot_ref, do_ref, att_ref, lse_ref,
    segk_ref, segq_ref, dqt_ref, dk_ref, dv_ref, dk_sum, dv_sum,
):
    tile = pl.program_id(1)

    @pl.when(tile == 0)
    def _():
        dk_sum[...] = jnp.zeros_like(dk_sum)
        dv_sum[...] = jnp.zeros_like(dv_sum)

    def run(window):
        start = pl.multiple_of(start_ref[tile] * KT, KT)
        at = pl.ds(start, window)
        keys, values = k_ref[at, :], v_ref[at, :]
        bias = key_bias(segk_ref, segq_ref, start, window)
        qt, q, dot, do = qt_ref[...], q_ref[...], dot_ref[...], do_ref[...]
        inner = dot.astype(f32) * att_ref[...].astype(f32)
        dk = jnp.zeros((window, LANES), f32)
        dv = jnp.zeros((window, LANES), f32)
        for h in range(GROUP):
            rows = slice(h * HEAD_DIM, (h + 1) * HEAD_DIM)
            delta = jnp.sum(inner[rows, :], axis=0, keepdims=True)
            scores = mm(keys, head_only(qt, h, 0)) * (SCALE * LOG2E)
            probs = jnp.exp2((scores - lse_ref[h : h + 1, :]) + bias)
            dv = dv + mm(probs.astype(bf16), head_only(do, h, 1))
            grad_probs = mm(values, head_only(dot, h, 0))
            grad_scores = (probs * (grad_probs - delta)).astype(bf16)
            dk = dk + mm(grad_scores, head_only(q, h, 1))
            dq = mm(kt_ref[rows, at], grad_scores)
            dqt_ref[rows, :] = (dq * SCALE).astype(bf16)
        dk_sum[at, :] += dk
        dv_sum[at, :] += dv

    @pl.when(small_ref[tile] == 1)
    def _():
        run(4 * KT)

    @pl.when(small_ref[tile] == 0)
    def _():
        run(6 * KT)

    @pl.when(tile == pl.num_programs(1) - 1)
    def _():
        dk_ref[...] = (dk_sum[...] * SCALE).astype(bf16)
        dv_ref[...] = dv_sum[...].astype(bf16)


def attention_specs(span, D):
    spec = pl.BlockSpec
    return {
        "q_cols": spec((LANES, QT), lambda g, j, *_: (g, j)),
        "q_rows": spec((QT, LANES), lambda g, j, *_: (j, g)),
        "k_cols": spec((LANES, span), lambda g, j, *_: (g, 0)),
        "k_rows": spec((span, LANES), lambda g, j, *_: (0, g)),
        "lse": spec((8, QT), lambda g, j, *_: (g, j)),
        "segk": spec((span, LANES), lambda g, j, *_: (0, 0)),
        "segq": spec((8, QT), lambda g, j, *_: (0, j)),
    }


def run_forward(starts, small, qt, k, vt, segk, segq):
    D, rows = qt.shape
    span = k.shape[0]
    s = attention_specs(span, D)
    groups = D // LANES
    return pl.pallas_call(
        attend_forward,
        grid_spec=pltpu.PrefetchScalarGridSpec(
            num_scalar_prefetch=2,
            grid=(groups, rows // QT),
            in_specs=[s["q_cols"], s["k_rows"], s["k_cols"], s["segk"], s["segq"]],
            out_specs=[s["q_cols"], s["lse"]],
        ),
        out_shape=[
            jax.ShapeDtypeStruct((D, rows), bf16),
            jax.ShapeDtypeStruct((groups * 8, rows), f32),
        ],
        compiler_params=pltpu.CompilerParams(vmem_limit_bytes=VMEM_LIMIT),
        cost_estimate=pl.CostEstimate(flops=2 * 10**10, bytes_accessed=10**7, transcendentals=10**7),
        name="attend_forward",
    )(starts, small, qt, k, vt, segk, segq)


def run_backward(starts, small, qt, q, kt, k, v, dot, do, att, lse, segk, segq):
    D, rows = qt.shape
    span = k.shape[0]
    s = attention_specs(span, D)
    return pl.pallas_call(
        attend_backward,
        grid_spec=pltpu.PrefetchScalarGridSpec(
            num_scalar_prefetch=2,
            grid=(D // LANES, rows // QT),
            in_specs=[
                s["q_cols"], s["q_rows"], s["k_cols"], s["k_rows"], s["k_rows"], s["q_cols"], s["q_rows"],
                s["q_cols"], s["lse"], s["segk"], s["segq"],
            ],
            out_specs=[s["q_cols"], s["k_rows"], s["k_rows"]],
            scratch_shapes=[pltpu.VMEM((span, LANES), f32), pltpu.VMEM((span, LANES), f32)],
        ),
        out_shape=[
            jax.ShapeDtypeStruct((D, rows), bf16),
            jax.ShapeDtypeStruct((span, D), bf16),
            jax.ShapeDtypeStruct((span, D), bf16),
        ],
        compiler_params=pltpu.CompilerParams(vmem_limit_bytes=VMEM_LIMIT),
        cost_estimate=pl.CostEstimate(flops=4 * 10**10, bytes_accessed=2 * 10**7, transcendentals=10**7),
        name="attend_backward",
    )(starts, small, qt, q, kt, k, v, dot, do, att, lse, segk, segq)


def feed_forward(first, *refs):
    n2_ref, g_ref, up_ref, dt_ref, ub_ref = refs[:5]
    refs = refs[5:]
    if not first:
        out_in, gn_in = refs[:2]
        refs = refs[2:]
    out_ref, gn_ref, dup_ref, ddt_ref, dub_ref, up_t, down, dup_sum, ddt_sum = refs
    step = pl.program_id(0) * pl.num_programs(1) + pl.program_id(1)
    last = pl.num_programs(0) * pl.num_programs(1) - 1

    @pl.when(step == 0)
    def _():
        up_t[...] = up_ref[...].T
        down[...] = dt_ref[...].T
        dup_sum[...] = jnp.zeros_like(dup_sum)
        ddt_sum[...] = jnp.zeros_like(ddt_sum)
        dub_ref[...] = jnp.zeros_like(dub_ref)

    n2, g = n2_ref[0], g_ref[0]
    hidden = mm(up_t[...], n2) + ub_ref[...]
    grad_act = mm(down[...], g)
    cdf, pdf = normal_cdf(hidden)
    act = (hidden * cdf).astype(bf16)
    grad_hidden = (grad_act * (cdf + hidden * pdf)).astype(bf16)
    out = mm(dt_ref[...], act)
    gn = mm(up_ref[...], grad_hidden)
    if first:
        out_ref[0], gn_ref[0] = out, gn
    else:
        out_ref[0] = out_in[0] + out
        gn_ref[0] = gn_in[0] + gn
    dup_sum[...] += mm(n2, grad_hidden, NT)
    ddt_sum[...] += mm(g, act, NT)
    wide_sum = grad_hidden.astype(f32)
    dub_ref[...] += sum(wide_sum[:, i : i + LANES] for i in range(0, wide_sum.shape[1], LANES))

    @pl.when(step == last)
    def _():
        dup_ref[...] = dup_sum[...].astype(bf16)
        ddt_ref[...] = ddt_sum[...].astype(bf16)


def run_feed_forward(n2, g, up, dt, ub, sums):
    pair, D, rows = n2.shape
    F = up.shape[1]
    tile = QT
    first = sums is None
    whole = lambda shape: pl.BlockSpec(shape, lambda i, j: (0,) * len(shape))
    cols = pl.BlockSpec((1, D, tile), lambda i, j: (i, 0, j))
    sums = () if first else tuple(sums)
    return pl.pallas_call(
        functools.partial(feed_forward, first),
        grid=(pair, rows // tile),
        in_specs=[cols, cols, whole((D, F)), whole((D, F)), whole((F, 1))] + [cols] * len(sums),
        out_specs=[cols, cols, whole((D, F)), whole((D, F)), whole((F, LANES))],
        out_shape=[
            jax.ShapeDtypeStruct((pair, D, rows), f32),
            jax.ShapeDtypeStruct((pair, D, rows), f32),
            jax.ShapeDtypeStruct((D, F), bf16),
            jax.ShapeDtypeStruct((D, F), bf16),
            jax.ShapeDtypeStruct((F, LANES), f32),
        ],
        scratch_shapes=[
            pltpu.VMEM((F, D), bf16),
            pltpu.VMEM((F, D), bf16),
            pltpu.VMEM((D, F), f32),
            pltpu.VMEM((D, F), f32),
        ],
        input_output_aliases={} if first else {5: 0, 6: 1},
        compiler_params=pltpu.CompilerParams(vmem_limit_bytes=VMEM_LIMIT),
        cost_estimate=pl.CostEstimate(
            flops=12 * pair * rows * D * F, bytes_accessed=2 * 10**7, transcendentals=10**6
        ),
        name="feed_forward",
    )(n2, g, up, dt, ub, *sums)


def norm_parts(cols):
    centre = jnp.mean(cols, axis=0, keepdims=True)
    shifted = cols - centre
    spread = jnp.mean(jnp.square(shifted), axis=0, keepdims=True)
    scale = lax.rsqrt(spread + EPS)
    return shifted * scale, scale


def norm_back(grad, xhat, scale, gain):
    e = grad * gain
    mean_e = jnp.mean(e, axis=0, keepdims=True)
    mean_ex = jnp.mean(e * xhat, axis=0, keepdims=True)
    return scale * (e - mean_e - xhat * mean_ex)


def z_rotate(x, k):
    n = lax.axis_size("narrow")
    return lax.ppermute(x, "narrow", [(i, (i + k) % n) for i in range(n)])


def z_gather(x):
    n, me = lax.axis_size("narrow"), lax.axis_index("narrow")
    stack = jnp.stack([x] + [z_rotate(x, k) for k in range(1, n)])
    return [lax.dynamic_index_in_dim(stack, lax.rem(me - j + n, n), 0, False) for j in range(n)]


def z_scatter_sum(pieces):
    n, me = lax.axis_size("narrow"), lax.axis_index("narrow")
    total = lax.dynamic_index_in_dim(pieces, me, 0, False).astype(f32)
    for k in range(1, n):
        piece = lax.dynamic_index_in_dim(pieces, lax.rem(me + k, n), 0, False)
        total = total + z_rotate(piece, k).astype(f32)
    return total


def swap(x, mask):
    n = lax.axis_size("wide")
    return lax.ppermute(x, "wide", [(i, i ^ mask) for i in range(n)])


def wide_sum(x):
    bit = 1
    while bit < lax.axis_size("wide"):
        x = x + swap(x, bit)
        bit *= 2
    return x


CORE, X, Y = 1, 2, 4


def high_bits():
    bits, bit = [], 8
    while bit < lax.axis_size("wide"):
        bits.append(bit)
        bit *= 2
    return bits


def shards(
    tokens_in,
    ln1_gain,
    ln1_shift,
    w_qkv,
    qv_bias,
    w_out,
    out_bias,
    ln2_gain,
    ln2_shift,
    w_up,
    up_bias,
    w_down,
    down_bias,
    segment_ids,
    out_grad,
    predicted,
    labels,
):
    nn, me = lax.axis_size("narrow"), lax.axis_index("narrow")
    nw, mw = lax.axis_size("wide"), lax.axis_index("wide")
    part, tok = tokens_in.shape
    D = part * nn
    quarter = tok // nn
    halo = LONGEST
    span = quarter + 2 * halo
    high = high_bits()

    padded = jnp.pad(tokens_in, ((0, 0), (halo, halo)))
    blocks = jnp.stack([padded[:, j * quarter : j * quarter + span] for j in range(nn)])
    x_low = lax.all_to_all(blocks, "narrow", 0, 0, tiled=True).reshape(D, span)

    vectors = jnp.stack(
        [ln1_gain, ln1_shift, qv_bias[0], qv_bias[1], out_bias, ln2_gain, ln2_shift, down_bias]
    )
    vectors = jnp.concatenate(z_gather(vectors), axis=1).astype(f32)[:, :, None]
    gain_one, shift_one, q_bias, v_bias, bias_out, gain_two, shift_two, bias_down = vectors

    dw = w_qkv.shape[1]
    attn_piece = jnp.concatenate([w_qkv, w_out.T[None]], axis=0)
    attn_own = jnp.concatenate(z_gather(attn_piece), axis=2)[None]
    order = [0]
    for bit in high:
        attn_own = jnp.concatenate([attn_own, swap(attn_own, bit)], axis=0)
        order = order + [m ^ bit for m in order]
    from_x, from_y = swap(attn_own, X), swap(attn_own, Y)
    from_xy = jnp.concatenate([swap(from_y[:, :2], X), swap(from_x[:, 2:], Y)], axis=1)
    attn_half = jnp.concatenate([attn_own, from_x, from_y, from_xy], axis=0)
    order = [m ^ b for b in (0, X, Y, X | Y) for m in order]
    attn_all = jnp.concatenate([attn_half, swap(attn_half, CORE)], axis=0)
    order = order + [m ^ CORE for m in order]
    place = jnp.array([order.index(m) for m in range(nw)], jnp.int32)
    attn_all = jnp.concatenate(
        [lax.dynamic_index_in_dim(attn_all, place[mw ^ w], 0, True) for w in range(nw)], axis=0
    )
    attn_whole = attn_all.transpose(1, 0, 2, 3).reshape(4, D, D)
    wq, wk, wv, wo_t = attn_whole

    up_own = jnp.concatenate(z_gather(w_up), axis=0)
    dt_own = jnp.concatenate(z_gather(w_down.T), axis=0)
    ub_own = up_bias.astype(f32)[None]
    for bit in high:
        up_own = jnp.concatenate([up_own, swap(up_own, bit)], axis=1)
        dt_own = jnp.concatenate([dt_own, swap(dt_own, bit)], axis=1)
        ub_own = jnp.concatenate([ub_own, swap(ub_own, bit)], axis=1)
    up_x, dt_x, up_y, dt_y = swap(up_own, X), swap(dt_own, X), swap(up_own, Y), swap(dt_own, Y)
    up_xy, dt_xy = swap(up_y, X), swap(dt_x, Y)
    ub_x, ub_y, ub_xy = swap(ub_own, X), swap(ub_own, Y), swap(ub_own, X | Y)

    grad_blocks = jnp.stack([out_grad[:, j * quarter : (j + 1) * quarter] for j in range(nn)])
    grad_cols = lax.all_to_all(grad_blocks, "narrow", 0, 0, tiled=True).reshape(D, quarter)
    grad_pair = jnp.stack([grad_cols, swap(grad_cols, CORE)])

    position = jnp.arange(tok, dtype=jnp.int32)
    chunk = segment_ids * (tok // SEQ) + position // SEQ
    big = jnp.int32(2**30)
    chunk = jnp.concatenate([jnp.full((halo,), -1, jnp.int32), chunk, jnp.full((halo,), big, jnp.int32)])
    chunk = lax.dynamic_slice_in_dim(chunk, me * quarter, span, 0)
    chunk_own = chunk[halo : halo + quarter]
    tiles = quarter // QT
    edges = chunk_own.reshape(tiles, QT)
    low = jnp.sum((chunk[None] < edges[:, :1]).astype(jnp.int32), axis=1) // KT
    top = (jnp.sum((chunk[None] <= edges[:, -1:]).astype(jnp.int32), axis=1) + KT - 1) // KT
    small = (top - low <= 4).astype(jnp.int32)
    starts = jnp.minimum(low, span // KT - jnp.where(small == 1, 4, 6))
    segk = jnp.broadcast_to(chunk[:, None], (span, LANES))
    segq = jnp.broadcast_to(chunk_own[None], (8, quarter))

    x_cols = x_low.astype(f32)
    xhat_one, scale_one = norm_parts(x_cols)
    normed = (xhat_one * gain_one + shift_one).astype(bf16)
    own = slice(halo, halo + quarter)
    normed_own = normed[:, own]
    qt = (mm(wq, normed_own, TN) + q_bias).astype(bf16)
    kt = mm(wk, normed, TN).astype(bf16)
    vt = (mm(wv, normed, TN) + v_bias).astype(bf16)
    q, k, v = qt.T, kt.T, vt.T
    att, lse = run_forward(starts, small, qt, k, vt, segk, segq)
    branch = mm(wo_t, att)
    middle = x_cols[:, own] + (branch + bias_out)
    xhat_two, scale_two = norm_parts(middle)
    normed_two = (xhat_two * gain_two + shift_two).astype(bf16)

    pair = jnp.stack([normed_two, swap(normed_two, CORE)])
    sums, grads = None, []
    for up, dt, ub in (
        (up_own, dt_own, ub_own),
        (up_x, dt_x, ub_x),
        (up_y, dt_y, ub_y),
        (up_xy, dt_xy, ub_xy),
    ):
        *sums, dup, ddt, dub = run_feed_forward(pair, grad_pair, up, dt, ub.reshape(-1, 1), sums)
        grads.append((dup, ddt, jnp.sum(dub, axis=1)))
    out_sum, gn_sum = sums
    ffn_out = out_sum[0] + swap(out_sum[1].astype(bf16), CORE).astype(f32)
    grad_normed_two = gn_sum[0] + swap(gn_sum[1].astype(bf16), CORE).astype(f32)

    layer = (middle + (ffn_out + bias_down)).astype(bf16)
    layer_out = lax.all_to_all(layer.reshape(nn, part, quarter), "narrow", 0, 0, tiled=True)
    layer_out = layer_out.transpose(1, 0, 2).reshape(part, tok)

    (up_g, dt_g, ub_g), (up_gx, dt_gx, ub_gx), (up_gy, dt_gy, ub_gy), (up_gxy, dt_gxy, ub_gxy) = grads
    add = lambda *terms: sum(t.astype(f32) for t in terms)
    up_gy = add(up_gy, swap(up_gxy, X)).astype(bf16)
    dt_gx = add(dt_gx, swap(dt_gxy, Y)).astype(bf16)
    up_g = add(up_g, swap(up_gx, X), swap(up_gy, Y))
    dt_g = add(dt_g, swap(dt_gx, X), swap(dt_gy, Y))
    ub_g = ub_g + swap(ub_gx, X) + swap(ub_gy, Y) + swap(ub_gxy, X | Y)
    for bit in reversed(high):
        half = up_g.shape[1] // 2
        up_g = up_g[:, :half] + swap(up_g[:, half:].astype(bf16), bit).astype(f32)
        dt_g = dt_g[:, :half] + swap(dt_g[:, half:].astype(bf16), bit).astype(f32)
        ub_g = ub_g[:half] + swap(ub_g[half:], bit)
    up_grad = z_scatter_sum(up_g.astype(bf16).reshape(nn, part, -1))
    down_grad = z_scatter_sum(dt_g.astype(bf16).reshape(nn, part, -1)).T
    up_bias_grad = ub_g + sum(z_rotate(ub_g, r) for r in range(1, nn))

    grad_rows = grad_cols.astype(f32)
    grad_mid = grad_rows + norm_back(grad_normed_two, xhat_two, scale_two, gain_two)
    gain_two_grad = jnp.sum(grad_normed_two * xhat_two, axis=1)
    shift_two_grad = jnp.sum(grad_normed_two, axis=1)
    grad_branch = grad_mid.astype(bf16)
    out_bias_part = jnp.sum(grad_branch.astype(f32), axis=1)
    down_bias_part = jnp.sum(grad_rows, axis=1)
    grad_wo_t = mm(grad_branch, att, NT)
    grad_att = mm(wo_t, grad_branch, TN).astype(bf16)
    dqt, dk, dv = run_backward(
        starts, small, qt, q, kt, k, v, grad_att, grad_att.T, att, lse, segk, segq
    )
    grad_wq = mm(normed_own, dqt, NT)
    grad_wk = mm(normed, dk)
    grad_wv = mm(normed, dv)
    q_bias_part = jnp.sum(dqt.astype(f32), axis=1)
    v_bias_part = jnp.sum(dv.astype(f32), axis=0)
    grad_normed = mm(wk, dk, NT) + mm(wv, dv, NT) + jnp.pad(mm(wq, dqt), ((0, 0), (halo, halo)))
    gain_one_grad = jnp.sum(grad_normed * xhat_one, axis=1)
    shift_one_grad = jnp.sum(grad_normed, axis=1)
    grad_in = norm_back(grad_normed, xhat_one, scale_one, gain_one)
    grad_in = grad_in + jnp.pad(grad_mid, ((0, 0), (halo, halo)))
    grad_in = grad_in.astype(bf16).reshape(nn, part, span)
    grad_in = lax.all_to_all(grad_in, "narrow", 0, 0, tiled=True).astype(f32)
    tokens_grad = sum(
        jnp.pad(grad_in[j], ((0, 0), (j * quarter, tok - (j + 1) * quarter))) for j in range(nn)
    )[:, halo : halo + tok]

    attn_g = jnp.stack([grad_wq, grad_wk, grad_wv, grad_wo_t]).astype(bf16)
    attn_g = attn_g.reshape(4, nw, dw, D).transpose(1, 0, 2, 3)
    pick = lambda masks: jnp.concatenate(
        [lax.dynamic_index_in_dim(attn_g, mw ^ m, 0, True) for m in masks], axis=0
    )
    masks = [0]
    for bit in high:
        masks = masks + [m ^ bit for m in masks]
    count = len(masks)
    masks = [m ^ b for b in (0, X, Y, X | Y) for m in masks]
    half = add(pick(masks), swap(pick([m ^ CORE for m in masks]), CORE)).astype(bf16)
    g0, gx, gy, gxy = (half[i * count : (i + 1) * count] for i in range(4))
    gy_low = add(gy[:, :2], swap(gxy[:, :2], X)).astype(bf16)
    gx_high = add(gx[:, 2:], swap(gxy[:, 2:], Y)).astype(bf16)
    gx = jnp.concatenate([gx[:, :2], gx_high], axis=1)
    gy = jnp.concatenate([gy_low, gy[:, 2:]], axis=1)
    g0 = add(g0, swap(gx, X), swap(gy, Y))
    for bit in reversed(high):
        cut = g0.shape[0] // 2
        g0 = g0[:cut] + swap(g0[cut:].astype(bf16), bit).astype(f32)
    g0 = g0[0].astype(bf16).reshape(4, dw, nn, part).transpose(2, 0, 1, 3)
    attn_grad = z_scatter_sum(g0)
    qkv_grad = attn_grad[:3]
    out_weight_grad = attn_grad[3].T

    vector_rows = jnp.stack(
        [
            gain_one_grad,
            shift_one_grad,
            q_bias_part,
            v_bias_part,
            out_bias_part,
            gain_two_grad,
            shift_two_grad,
            down_bias_part,
        ]
    )
    vector_rows = z_scatter_sum(vector_rows.reshape(8, nn, part).transpose(1, 0, 2))
    class_ids = jnp.arange(CLASSES, dtype=jnp.int32)
    label_hits = labels[:, None] == class_ids
    counts = jnp.stack(
        [
            jnp.sum(((predicted[:, None] == class_ids) & label_hits).astype(f32), axis=0),
            jnp.sum(label_hits.astype(f32), axis=0),
        ]
    )
    counts = wide_sum(counts)
    vec = wide_sum(vector_rows)
    tallies = counts.astype(jnp.int32)
    accuracy = jnp.sum(counts[0]) / jnp.maximum(jnp.sum(counts[1]), 1.0)
    return (
        layer_out,
        tokens_grad,
        vec[0],
        vec[1],
        qkv_grad,
        vec[2:4],
        out_weight_grad,
        vec[4],
        vec[5],
        vec[6],
        up_grad,
        up_bias_grad,
        down_grad,
        vec[7],
        tallies,
        accuracy,
    )


def solution(mesh):
    return jax.shard_map(
        shards,
        mesh=mesh,
        in_specs=(
            P("narrow", "wide"),
            P("narrow"),
            P("narrow"),
            P(None, "wide", "narrow"),
            P(None, "narrow"),
            P("narrow", "wide"),
            P("narrow"),
            P("narrow"),
            P("narrow"),
            P("narrow", "wide"),
            P("wide"),
            P("wide", "narrow"),
            P("narrow"),
            P("wide"),
            P("narrow", "wide"),
            P("wide"),
            P("wide"),
        ),
        out_specs=(
            P("narrow", "wide"),
            P("narrow", "wide"),
            P("narrow"),
            P("narrow"),
            P(None, "wide", "narrow"),
            P(None, "narrow"),
            P("narrow", "wide"),
            P("narrow"),
            P("narrow"),
            P("narrow"),
            P("narrow", "wide"),
            P("wide"),
            P("wide", "narrow"),
            P("narrow"),
            P(),
            P(),
        ),
        check_vma=False,
    )
```

```python
import functools

import jax
import jax.numpy as jnp
from jax import lax
from jax.experimental import pallas as pl
from jax.experimental.pallas import tpu as pltpu
from jax.sharding import PartitionSpec as P

HEAD_DIM = 32
SEQ = 1024
CLASSES = 4
LONGEST = 256
EPS = 1e-05
QT = 256
KT = 128
GROUP = 4
LANES = 128
LOG2E = 1.4426950408889634
SCALE = HEAD_DIM**-0.5
MASKED = -1e30
VMEM_LIMIT = 56 * 1024 * 1024
VEC_BLOCK, VEC_AT = 2, 64
VEC_LAST = VEC_BLOCK * 128 + VEC_AT + 7
bf16, f32 = jnp.bfloat16, jnp.float32

NN = (((1,), (0,)), ((), ()))
NT = (((1,), (1,)), ((), ()))
TN = (((0,), (0,)), ((), ()))

PHI_P = 0.33
PHI_C = (
    0.1328227541618569,
    0.117797452145417,
    0.18652846971894854,
    -0.09893620415601319,
    0.3406397450924515,
    -0.22542553879715763,
    0.046573313873415075,
)


def mm(left, right, dims=NN):
    return lax.dot_general(left, right, dims, preferred_element_type=f32)


def normal_cdf(u):
    bell = jnp.exp(-0.5 * (u * u))
    t = 1.0 / (1.0 + PHI_P * jnp.abs(u))
    tail = jnp.full_like(t, PHI_C[-1])
    for c in PHI_C[-2::-1]:
        tail = tail * t + c
    tail = tail * t * bell
    return jnp.where(u >= 0, 1.0 - tail, tail), bell * 0.3989422804014327


def head_only(block, h, axis):
    index = lax.broadcasted_iota(jnp.int32, block.shape, axis)
    keep = (index >= h * HEAD_DIM) & (index < (h + 1) * HEAD_DIM)
    return jnp.where(keep, block, jnp.zeros_like(block))


def key_bias(segk_ref, segq_ref, start, window):
    segk = segk_ref[pl.ds(start, window), :]
    segk = jnp.concatenate([segk] * (QT // LANES), axis=1)
    return jnp.where(segk == segq_ref[0:1, :], 0.0, MASKED).astype(f32)


def attend_forward(start_ref, small_ref, q_ref, k_ref, vt_ref, segk_ref, segq_ref, *refs):
    att_ref, lse_ref = refs[-2:]
    tile = pl.program_id(1)

    def run(window):
        start = pl.multiple_of(start_ref[tile] * KT, KT)
        keys = k_ref[pl.ds(start, window), :]
        bias = key_bias(segk_ref, segq_ref, start, window)
        q = q_ref[...]
        for h in range(GROUP):
            rows = slice(h * HEAD_DIM, (h + 1) * HEAD_DIM)
            scores = mm(keys, head_only(q, h, 0)) + bias
            top = jnp.max(scores, axis=0, keepdims=True)
            probs = jnp.exp2((scores - top) * (SCALE * LOG2E))
            total = jnp.sum(probs, axis=0, keepdims=True)
            out = mm(vt_ref[rows, pl.ds(start, window)], probs.astype(bf16))
            att_ref[rows, :] = (out / total).astype(bf16)
            lse_ref[h : h + 1, :] = top * (SCALE * LOG2E) + jnp.log2(total)

    @pl.when(small_ref[tile] == 1)
    def _():
        run(4 * KT)

    @pl.when(small_ref[tile] == 0)
    def _():
        run(6 * KT)


def attend_backward(
    start_ref, small_ref, qt_ref, kt_ref, k_ref, v_ref, dot_ref, att_ref, lse_ref, segk_ref, segq_ref, *refs
):
    dqt_ref, dk_ref, dv_ref, dk_sum, dv_sum = refs[-5:]
    tile = pl.program_id(1)

    @pl.when(tile == 0)
    def _():
        dk_sum[...] = jnp.zeros_like(dk_sum)
        dv_sum[...] = jnp.zeros_like(dv_sum)

    def run(window):
        start = pl.multiple_of(start_ref[tile] * KT, KT)
        at = pl.ds(start, window)
        keys, values = k_ref[at, :], v_ref[at, :]
        bias = key_bias(segk_ref, segq_ref, start, window)
        qt, dot = qt_ref[...], dot_ref[...]
        q, do = qt.T, dot.T
        inner = dot.astype(f32) * att_ref[...].astype(f32)
        dk = jnp.zeros((window, LANES), f32)
        dv = jnp.zeros((window, LANES), f32)
        for h in range(GROUP):
            rows = slice(h * HEAD_DIM, (h + 1) * HEAD_DIM)
            delta = jnp.sum(inner[rows, :], axis=0, keepdims=True)
            scores = mm(keys, head_only(qt, h, 0)) * (SCALE * LOG2E)
            probs = jnp.exp2((scores - lse_ref[h : h + 1, :]) + bias)
            dv = dv + mm(probs.astype(bf16), head_only(do, h, 1))
            grad_probs = mm(values, head_only(dot, h, 0))
            grad_scores = (probs * (grad_probs - delta)).astype(bf16)
            dk = dk + mm(grad_scores, head_only(q, h, 1))
            dq = mm(kt_ref[rows, at], grad_scores)
            dqt_ref[rows, :] = (dq * SCALE).astype(bf16)
        dk_sum[at, :] += dk
        dv_sum[at, :] += dv

    @pl.when(small_ref[tile] == 1)
    def _():
        run(4 * KT)

    @pl.when(small_ref[tile] == 0)
    def _():
        run(6 * KT)

    @pl.when(tile == pl.num_programs(1) - 1)
    def _():
        dk_ref[...] = (dk_sum[...] * SCALE).astype(bf16)
        dv_ref[...] = dv_sum[...].astype(bf16)


def attention_specs(span, begin):
    spec = pl.BlockSpec
    return {
        "q_cols": spec((LANES, QT), lambda g, j, *_: (g + begin, j)),
        "k_cols": spec((LANES, span), lambda g, j, *_: (g + begin, 0)),
        "k_rows": spec((span, LANES), lambda g, j, *_: (0, g + begin)),
        "lse": spec((8, QT), lambda g, j, *_: (g + begin, j)),
        "segk": spec((span, LANES), lambda g, j, *_: (0, 0)),
        "segq": spec((8, QT), lambda g, j, *_: (0, j)),
    }


def run_forward(starts, small, qt, k, vt, segk, segq, span_of_groups, outs=()):
    D, rows = qt.shape
    span = k.shape[0]
    begin, end = span_of_groups
    s = attention_specs(span, begin)
    groups = D // LANES
    outs = tuple(outs)
    return pl.pallas_call(
        attend_forward,
        grid_spec=pltpu.PrefetchScalarGridSpec(
            num_scalar_prefetch=2,
            grid=(end - begin, rows // QT),
            in_specs=[s["q_cols"], s["k_rows"], s["k_cols"], s["segk"], s["segq"]]
            + [pl.BlockSpec(memory_space=pl.ANY)] * len(outs),
            out_specs=[s["q_cols"], s["lse"]],
        ),
        input_output_aliases={7: 0, 8: 1} if outs else {},
        out_shape=[
            jax.ShapeDtypeStruct((D, rows), bf16),
            jax.ShapeDtypeStruct((groups * 8, rows), f32),
        ],
        compiler_params=pltpu.CompilerParams(vmem_limit_bytes=VMEM_LIMIT),
        cost_estimate=pl.CostEstimate(flops=10**8, bytes_accessed=10**6, transcendentals=0),
        name="attend_forward",
    )(starts, small, qt, k, vt, segk, segq, *outs)


def run_backward(starts, small, qt, kt, k, v, dot, att, lse, segk, segq, span_of_groups, outs=()):
    D, rows = qt.shape
    span = k.shape[0]
    begin, end = span_of_groups
    s = attention_specs(span, begin)
    outs = tuple(outs)
    return pl.pallas_call(
        attend_backward,
        grid_spec=pltpu.PrefetchScalarGridSpec(
            num_scalar_prefetch=2,
            grid=(end - begin, rows // QT),
            in_specs=[
                s["q_cols"], s["k_cols"], s["k_rows"], s["k_rows"], s["q_cols"], s["q_cols"],
                s["lse"], s["segk"], s["segq"],
            ]
            + [pl.BlockSpec(memory_space=pl.ANY)] * len(outs),
            out_specs=[s["q_cols"], s["k_rows"], s["k_rows"]],
            scratch_shapes=[pltpu.VMEM((span, LANES), f32), pltpu.VMEM((span, LANES), f32)],
        ),
        out_shape=[
            jax.ShapeDtypeStruct((D, rows), bf16),
            jax.ShapeDtypeStruct((span, D), bf16),
            jax.ShapeDtypeStruct((span, D), bf16),
        ],
        input_output_aliases={11: 0, 12: 1, 13: 2} if outs else {},
        compiler_params=pltpu.CompilerParams(vmem_limit_bytes=VMEM_LIMIT),
        cost_estimate=pl.CostEstimate(flops=10**8, bytes_accessed=10**6, transcendentals=0),
        name="attend_backward",
    )(starts, small, qt, kt, k, v, dot, att, lse, segk, segq, *outs)


def norm_parts(cols):
    centre = jnp.mean(cols, axis=0, keepdims=True)
    shifted = cols - centre
    spread = jnp.mean(jnp.square(shifted), axis=0, keepdims=True)
    scale = lax.rsqrt(spread + EPS)
    return shifted * scale, scale


def norm_back(grad, xhat, scale, gain):
    e = grad * gain
    mean_e = jnp.mean(e, axis=0, keepdims=True)
    mean_ex = jnp.mean(e * xhat, axis=0, keepdims=True)
    return scale * (e - mean_e - xhat * mean_ex)


VECTORS = ("gain_one", "shift_one", "q_bias", "v_bias", "bias_out", "gain_two", "shift_two", "bias_down")


def vector(vec_ref, name):
    i = VEC_AT + VECTORS.index(name)
    return vec_ref[:, i : i + 1].astype(f32)


def fold(x):
    return sum(x[:, i : i + LANES] for i in range(0, x.shape[1], LANES))


def whole(shape, block=None):
    return pl.BlockSpec(shape, lambda *_: (0,) * len(shape) if block is None else block)


def kernel_params(flops, nbytes):
    return {
        "compiler_params": pltpu.CompilerParams(vmem_limit_bytes=VMEM_LIMIT),
        "cost_estimate": pl.CostEstimate(flops=flops, bytes_accessed=nbytes, transcendentals=0),
    }


def project(split, xa_ref, xb_ref, w_ref, vec_ref, x_ref, n_ref, qt_ref, kt_ref, vt_ref, k_ref, v_ref, wt):
    i = pl.program_id(0)

    @pl.when(i == 0)
    def _():
        for c in range(3):
            wt[c] = w_ref[c].T

    x = jnp.where(i < split, xa_ref[...], xb_ref[...])
    x_ref[...] = x
    xhat, _ = norm_parts(x.astype(f32))
    normed = (xhat * vector(vec_ref, "gain_one") + vector(vec_ref, "shift_one")).astype(bf16)
    n_ref[...] = normed
    kt = mm(wt[1], normed).astype(bf16)
    vt = (mm(wt[2], normed) + vector(vec_ref, "v_bias")).astype(bf16)
    kt_ref[...], vt_ref[...] = kt, vt
    k_ref[...], v_ref[...] = kt.T, vt.T

    @pl.when((i >= 1) & (i < pl.num_programs(0) - 1))
    def _():
        qt_ref[...] = (mm(wt[0], normed) + vector(vec_ref, "q_bias")).astype(bf16)


def run_project(xa, xb, w, vec, split):
    D, span = xa.shape[0], split * QT + xb.shape[1]
    steps = span // QT
    first = pl.BlockSpec((D, QT), lambda i: (0, jnp.minimum(i, split - 1)))
    second = pl.BlockSpec((D, QT), lambda i: (0, jnp.maximum(i - split, 0)))
    cols = pl.BlockSpec((D, QT), lambda i: (0, i))
    rows = pl.BlockSpec((QT, D), lambda i: (i, 0))
    own = pl.BlockSpec((D, QT), lambda i: (0, jnp.clip(i - 1, 0, steps - 3)))
    shape = jax.ShapeDtypeStruct
    return pl.pallas_call(
        functools.partial(project, split),
        grid=(steps,),
        in_specs=[first, second, whole((3, D, D)), whole((D, LANES), (0, VEC_BLOCK))],
        out_specs=[cols, cols, own, cols, cols, rows, rows],
        out_shape=[
            shape((D, span), bf16),
            shape((D, span), bf16),
            shape((D, span - 2 * QT), bf16),
            shape((D, span), bf16),
            shape((D, span), bf16),
            shape((span, D), bf16),
            shape((span, D), bf16),
        ],
        scratch_shapes=[pltpu.VMEM((3, D, D), bf16)],
        name="project",
        **kernel_params(10**8, 10**6),
    )(xa, xb, w, vec)


def project_back(
    x_ref, n_ref, dqt_ref, dk_ref, dv_ref, w_ref, mid_ref, vec_ref,
    grad_ref, gw_ref, sums_ref, vb_ref, gw_sum,
):
    i = pl.program_id(0)
    last = pl.num_programs(0) - 1
    own = (i >= 1) & (i < last)

    @pl.when(i == 0)
    def _():
        gw_sum[...] = jnp.zeros_like(gw_sum)
        sums_ref[...] = jnp.zeros_like(sums_ref)
        vb_ref[...] = jnp.zeros_like(vb_ref)

    normed, dk, dv = n_ref[...], dk_ref[...], dv_ref[...]
    dqt = jnp.where(own, dqt_ref[...], jnp.zeros_like(dqt_ref))
    gw_sum[0] += mm(normed, dqt, NT)
    gw_sum[1] += mm(normed, dk)
    gw_sum[2] += mm(normed, dv)
    grad = mm(w_ref[1], dk, NT) + mm(w_ref[2], dv, NT) + mm(w_ref[0], dqt)
    xhat, scale = norm_parts(x_ref[...].astype(f32))
    sums_ref[0] += fold(grad * xhat)
    sums_ref[1] += fold(grad)
    sums_ref[2] += fold(dqt.astype(f32))
    vb_ref[...] += jnp.sum(dv.astype(f32).reshape(-1, 8, dv.shape[1]), axis=0)
    grad_in = norm_back(grad, xhat, scale, vector(vec_ref, "gain_one"))
    grad_ref[...] = (grad_in + jnp.where(own, mid_ref[...], 0.0)).astype(bf16)

    @pl.when(i == last)
    def _():
        gw_ref[...] = gw_sum[...].astype(bf16)


def run_project_back(x, normed, dqt, dk, dv, w, grad_mid, vec):
    D, span = x.shape
    steps = span // QT
    cols = pl.BlockSpec((D, QT), lambda i: (0, i))
    rows = pl.BlockSpec((QT, D), lambda i: (i, 0))
    own = pl.BlockSpec((D, QT), lambda i: (0, jnp.clip(i - 1, 0, steps - 3)))
    shape = jax.ShapeDtypeStruct
    return pl.pallas_call(
        project_back,
        grid=(steps,),
        in_specs=[cols, cols, own, rows, rows, whole((3, D, D)), own, whole((D, LANES), (0, VEC_BLOCK))],
        out_specs=[cols, whole((3, D, D)), whole((3, D, LANES)), whole((8, D))],
        out_shape=[
            shape((D, span), bf16),
            shape((3, D, D), bf16),
            shape((3, D, LANES), f32),
            shape((8, D), f32),
        ],
        scratch_shapes=[pltpu.VMEM((3, D, D), f32)],
        name="project_back",
        **kernel_params(10**8, 10**6),
    )(x, normed, dqt, dk, dv, w, grad_mid, vec)


def branch(att_ref, wo_ref, x_ref, vec_ref, mid_ref, n_ref):
    out = mm(wo_ref[0], att_ref[...]) + vector(vec_ref, "bias_out")
    middle = x_ref[...].astype(f32) + out
    mid_ref[...] = middle
    xhat, _ = norm_parts(middle)
    n_ref[...] = (xhat * vector(vec_ref, "gain_two") + vector(vec_ref, "shift_two")).astype(bf16)


def run_branch(att, w, x, vec):
    D, rows = att.shape
    cols = pl.BlockSpec((D, QT), lambda i: (0, i))
    return pl.pallas_call(
        branch,
        grid=(rows // QT,),
        in_specs=[
            cols,
            whole((1, D, D), (3, 0, 0)),
            pl.BlockSpec((D, QT), lambda i: (0, i + LONGEST // QT)),
            whole((D, LANES), (0, VEC_BLOCK)),
        ],
        out_specs=[cols, cols],
        out_shape=[jax.ShapeDtypeStruct((D, rows), f32), jax.ShapeDtypeStruct((D, rows), bf16)],
        name="branch",
        **kernel_params(10**8, 10**6),
    )(att, w, x, vec)


def branch_back(
    gn_ref, got_ref, mid_ref, g_ref, att_ref, wo_ref, vec_ref,
    gmid_ref, gatt_ref, gwo_ref, sums_ref, wo, gwo_sum,
):
    i = pl.program_id(0)

    @pl.when(i == 0)
    def _():
        wo[...] = wo_ref[0].T
        gwo_sum[...] = jnp.zeros_like(gwo_sum)
        sums_ref[...] = jnp.zeros_like(sums_ref)

    grad = gn_ref[0] + got_ref[...].astype(f32)
    xhat, scale = norm_parts(mid_ref[...])
    g = g_ref[...].astype(f32)
    grad_mid = g + norm_back(grad, xhat, scale, vector(vec_ref, "gain_two"))
    gmid_ref[...] = grad_mid
    low = grad_mid.astype(bf16)
    gatt_ref[...] = mm(wo[...], low).astype(bf16)
    gwo_sum[...] += mm(low, att_ref[...], NT)
    sums_ref[0] += fold(low.astype(f32))
    sums_ref[1] += fold(grad * xhat)
    sums_ref[2] += fold(grad)
    sums_ref[3] += fold(g)

    @pl.when(i == pl.num_programs(0) - 1)
    def _():
        gwo_ref[...] = gwo_sum[...].astype(bf16)


def run_branch_back(gn, got, middle, g, att, w, vec):
    D, rows = att.shape
    cols = pl.BlockSpec((D, QT), lambda i: (0, i))
    shape = jax.ShapeDtypeStruct
    return pl.pallas_call(
        branch_back,
        grid=(rows // QT,),
        in_specs=[
            pl.BlockSpec((1, D, QT), lambda i: (0, 0, i)),
            cols, cols, cols, cols,
            whole((1, D, D), (3, 0, 0)),
            whole((D, LANES), (0, VEC_BLOCK)),
        ],
        out_specs=[cols, cols, whole((D, D)), whole((4, D, LANES))],
        out_shape=[
            shape((D, rows), f32),
            shape((D, rows), bf16),
            shape((D, D), bf16),
            shape((4, D, LANES), f32),
        ],
        scratch_shapes=[pltpu.VMEM((D, D), bf16), pltpu.VMEM((D, D), f32)],
        name="branch_back",
        **kernel_params(10**8, 10**6),
    )(gn, got, middle, g, att, w, vec)


def feed_forward(first, final, parts, *refs):
    n2_own, n2_other, g_own, g_other, ub_ref = refs[:5]
    pieces, refs = refs[5 : 5 + parts], refs[5 + parts :]
    if not first:
        out_in, gn_in = refs[:2]
        refs = refs[2:]
    out_ref, gn_ref, dup_ref, ddt_ref, dub_ref = refs[:5]
    refs = refs[5:]
    if final:
        out_low, gn_low = refs[:2]
        refs = refs[2:]
    up_t, down, dup_sum, ddt_sum, ub_col = refs
    F = up_t.shape[0]
    up = pieces[0][:, :F]
    dt = pieces[0][:, F:] if parts == 1 else pieces[1][...]
    step = pl.program_id(0)
    half = pl.num_programs(0) // 2

    @pl.when(step == 0)
    def _():
        up_t[...] = up.T
        down[...] = dt.T
        dup_sum[...] = jnp.zeros_like(dup_sum)
        ddt_sum[...] = jnp.zeros_like(ddt_sum)
        dub_ref[...] = jnp.zeros_like(dub_ref)
        bias = ub_ref[...].astype(f32).T[:, 0:1]
        ub_col[...] = jnp.broadcast_to(bias, ub_col.shape)

    n2 = jnp.where(step < half, n2_own[...], n2_other[...])
    g = jnp.where(step < half, g_own[...], g_other[...])
    hidden = mm(up_t[...], n2) + jnp.concatenate([ub_col[...]] * (QT // LANES), axis=1)
    grad_act = mm(down[...], g)
    cdf, pdf = normal_cdf(hidden)
    act = (hidden * cdf).astype(bf16)
    grad_hidden = (grad_act * (cdf + hidden * pdf)).astype(bf16)
    out = mm(dt, act)
    gn = mm(up, grad_hidden)
    if not first:
        out = out + out_in[0]
        gn = gn + gn_in[0]
    out_ref[0], gn_ref[0] = out, gn
    if final:
        out_low[...], gn_low[...] = out.astype(bf16), gn.astype(bf16)
    dup_sum[...] += mm(n2, grad_hidden, NT)
    ddt_sum[...] += mm(g, act, NT)
    dub_ref[...] += fold(grad_hidden.astype(f32))

    @pl.when(step == 2 * half - 1)
    def _():
        dup_ref[...] = dup_sum[...].astype(bf16)
        ddt_ref[...] = ddt_sum[...].astype(bf16)


def run_feed_forward(n2, g, ud, ub, sums, final=False):
    D, rows = n2[0].shape
    F = sum(piece.shape[1] for piece in ud) // 2
    first = sums is None
    tiles = rows // QT
    own = pl.BlockSpec((D, QT), lambda i: (0, jnp.minimum(i, tiles - 1)))
    other = pl.BlockSpec((D, QT), lambda i: (0, jnp.maximum(i - tiles, 0)))
    both = pl.BlockSpec((1, D, QT), lambda i: (i // tiles, 0, i % tiles))
    sums = () if first else tuple(sums)
    shape = jax.ShapeDtypeStruct
    return pl.pallas_call(
        functools.partial(feed_forward, first, final, len(ud)),
        grid=(2 * tiles,),
        in_specs=[own, other, own, other, whole(ub.shape)]
        + [whole(piece.shape) for piece in ud]
        + [both] * len(sums),
        out_specs=[both, both, whole((D, F)), whole((D, F)), whole((F, LANES))] + [other] * (2 * final),
        out_shape=[
            shape((2, D, rows), f32),
            shape((2, D, rows), f32),
            shape((D, F), bf16),
            shape((D, F), bf16),
            shape((F, LANES), f32),
        ]
        + [shape((D, rows), bf16)] * (2 * final),
        scratch_shapes=[
            pltpu.VMEM((F, D), bf16),
            pltpu.VMEM((F, D), bf16),
            pltpu.VMEM((D, F), f32),
            pltpu.VMEM((D, F), f32),
            pltpu.VMEM((F, LANES), f32),
        ],
        input_output_aliases={} if first else {5 + len(ud): 0, 6 + len(ud): 1},
        name="feed_forward",
        **kernel_params(10**8, 10**6),
    )(n2[0], n2[1], g[0], g[1], ub, *ud, *sums)


def z_rotate(x, k):
    n = lax.axis_size("narrow")
    return lax.ppermute(x, "narrow", [(i, (i + k) % n) for i in range(n)])


def z_gather(x):
    n, me = lax.axis_size("narrow"), lax.axis_index("narrow")
    stack = jnp.stack([x] + [z_rotate(x, k) for k in range(1, n)])
    return [lax.dynamic_index_in_dim(stack, lax.rem(me - j + n, n), 0, False) for j in range(n)]


def z_scatter_sum(pieces):
    n, me = lax.axis_size("narrow"), lax.axis_index("narrow")
    total = lax.dynamic_index_in_dim(pieces, me, 0, False).astype(f32)
    for k in range(1, n):
        piece = lax.dynamic_index_in_dim(pieces, lax.rem(me + k, n), 0, False)
        total = total + z_rotate(piece, k).astype(f32)
    return total


def swap(x, mask):
    n = lax.axis_size("wide")
    return lax.ppermute(x, "wide", [(i, i ^ mask) for i in range(n)])


def wide_sum(x):
    bit = 1
    while bit < lax.axis_size("wide"):
        x = x + swap(x, bit)
        bit *= 2
    return x


CORE, X, Y = 1, 2, 4


def after(deps, *values):
    n = len(values)
    tied = pl.pallas_call(
        lambda *refs: None,
        in_specs=[pl.BlockSpec(memory_space=pl.ANY)] * (n + len(deps)),
        out_specs=[pl.BlockSpec(memory_space=pl.ANY)] * n,
        out_shape=[jax.ShapeDtypeStruct(v.shape, v.dtype) for v in values],
        input_output_aliases={i: i for i in range(n)},
        name="tie",
    )(*values, *deps)
    return tied if n > 1 else tied[0]


def high_bits():
    bits, bit = [], 8
    while bit < lax.axis_size("wide"):
        bits.append(bit)
        bit *= 2
    return bits


def shards(
    tokens_in,
    ln1_gain,
    ln1_shift,
    w_qkv,
    qv_bias,
    w_out,
    out_bias,
    ln2_gain,
    ln2_shift,
    w_up,
    up_bias,
    w_down,
    down_bias,
    segment_ids,
    out_grad,
    predicted,
    labels,
):
    nn, me = lax.axis_size("narrow"), lax.axis_index("narrow")
    nw, mw = lax.axis_size("wide"), lax.axis_index("wide")
    part, tok = tokens_in.shape
    D = part * nn
    quarter = tok // nn
    halo = LONGEST
    span = quarter + 2 * halo
    high = high_bits()
    dw = w_qkv.shape[1]
    across = lambda x: lax.all_to_all(x, "narrow", 0, 0, tiled=True)

    position = jnp.arange(tok, dtype=jnp.int32)
    chunk = segment_ids * (tok // SEQ) + position // SEQ
    big = jnp.int32(2**30)
    chunk = jnp.concatenate([jnp.full((halo,), -1, jnp.int32), chunk, jnp.full((halo,), big, jnp.int32)])
    chunk = lax.dynamic_slice_in_dim(chunk, me * quarter, span, 0)
    chunk_own = chunk[halo : halo + quarter]
    tiles = quarter // QT
    edges = chunk_own.reshape(tiles, QT)
    low = jnp.sum((chunk[None] < edges[:, :1]).astype(jnp.int32), axis=1) // KT
    top = (jnp.sum((chunk[None] <= edges[:, -1:]).astype(jnp.int32), axis=1) + KT - 1) // KT
    small = (top - low <= 4).astype(jnp.int32)
    starts = jnp.minimum(low, span // KT - jnp.where(small == 1, 4, 6))
    segk = jnp.broadcast_to(chunk[:, None], (span, LANES))
    segq = jnp.broadcast_to(chunk_own[None], (8, quarter))

    piece = [w_qkv.reshape(3 * dw, part).T, w_out]
    piece += [jnp.zeros((part, VEC_BLOCK * LANES + VEC_AT - 4 * dw), bf16)]
    piece += [
        jnp.stack([ln1_gain, ln1_shift, qv_bias[0], qv_bias[1], out_bias, ln2_gain, ln2_shift, down_bias]).T
    ]
    piece = jnp.concatenate(piece, axis=1)
    piece = jnp.pad(piece, ((0, 0), (0, -piece.shape[1] % LANES)))
    padded = jnp.pad(tokens_in, ((0, 0), (halo, halo)))
    cut = 2 * QT
    first_cols = [jnp.concatenate([padded[:, j * quarter : j * quarter + cut], piece], axis=1) for j in range(nn)]
    other_cols = [padded[:, j * quarter + cut : j * quarter + span] for j in range(nn)]
    x_a = across(jnp.stack(first_cols)).reshape(D, -1)
    vec = x_a[:, cut:]
    other_cols = after((starts, small, segk, segq), jnp.stack(other_cols))
    x_b = across(other_cols).reshape(D, span - cut)

    units = up_bias.shape[0]
    attn_own = vec[:, : 4 * dw].T
    bias_rows = jnp.pad(up_bias[None], ((0, 15), (0, D - units)))
    attn_own = jnp.concatenate([attn_own, bias_rows], axis=0)[None]
    for bit in high:
        attn_own = jnp.concatenate([attn_own, swap(attn_own, bit)], axis=0)
    from_x, from_y = swap(attn_own, X), swap(attn_own, Y)
    from_xy = jnp.concatenate([swap(from_y[:, : 2 * dw], X), swap(from_x[:, 2 * dw :], Y)], axis=1)
    attn_half = jnp.concatenate([attn_own, from_x, from_y, from_xy], axis=0)
    count = attn_own.shape[0]
    ub_own, ub_x, ub_y, ub_xy = (
        jnp.concatenate([attn_half[i * count + j, 4 * dw :, :units] for j in range(count)], axis=1)
        for i in range(4)
    )
    attn_half = attn_half[:, : 4 * dw].reshape(-1, 4, dw, D)
    attn_all = jnp.concatenate([attn_half, swap(attn_half, CORE)], axis=0)
    bits = high + [X, Y, CORE]
    place = lambda m: sum(((m // bit) % 2) << i for i, bit in enumerate(bits))
    attn_all = jnp.concatenate(
        [lax.dynamic_index_in_dim(attn_all, place(mw ^ w), 0, True) for w in range(nw)], axis=0
    )
    w_attn = attn_all.transpose(1, 0, 2, 3).reshape(4, D, D)

    x_low, normed, qt, kt, vt, k, v = run_project(x_a, x_b, w_attn, vec, cut // QT)
    groups = D // LANES
    att_a, lse_a = run_forward(starts, small, qt, k, vt, segk, segq, (0, 2))

    ud_piece = jnp.concatenate([w_up, w_down.T], axis=1)
    ud_piece = after((x_b, attn_half), jnp.stack([ud_piece] * nn))
    ud_own = after((att_a,), across(ud_piece).reshape(D, -1))
    for bit in high:
        got = swap(ud_own, bit)
        f = ud_own.shape[1] // 2
        ud_own = jnp.concatenate([ud_own[:, :f], got[:, :f], ud_own[:, f:], got[:, f:]], axis=1)
    F = ud_own.shape[1] // 2
    ud_x, ud_y = swap(ud_own, X), swap(ud_own, Y)
    ud_xy = swap(ud_y[:, :F], X), swap(ud_x[:, F:], Y)

    grad_blocks = jnp.stack([out_grad[:, j * quarter : (j + 1) * quarter] for j in range(nn)])
    grad_blocks = after((ud_own,), grad_blocks)
    grad_cols = across(grad_blocks).reshape(D, quarter)
    grad_pair = grad_cols, swap(grad_cols, CORE)

    att_a = after((ud_own,), att_a)
    att, lse = run_forward(starts, small, qt, k, vt, segk, segq, (2, groups), (att_a, lse_a))
    middle, normed_two = run_branch(att, w_attn, x_low, vec)

    n2_pair = normed_two, swap(normed_two, CORE)
    ffn = lambda ud, ub, sums, final=False: run_feed_forward(n2_pair, grad_pair, ud, ub, sums, final)
    *sums, up_gx, dt_gx, ub_gx = ffn((ud_x,), ub_x, None)
    *sums, up_gy, dt_gy, ub_gy = ffn((ud_y,), ub_y, sums)
    up_got_x = swap(up_gx, X)
    *sums, up_gxy, dt_gxy, ub_gxy = ffn(ud_xy, ub_xy, sums)
    dt_got_y = swap(dt_gy, Y)
    up_got_xy, dt_got_xy = swap(up_gxy, X), swap(dt_gxy, Y)
    *sums, ud_own = after((up_got_x, dt_got_y), *sums, ud_own)
    out_sum, gn_sum, up_g, dt_g, ub_g, out_other, gn_other = ffn((ud_own,), ub_own, sums, True)
    ub_parts = jnp.stack([jnp.sum(u, axis=1) for u in (ub_g, ub_gx, ub_gy, ub_gxy)])
    gn_got, out_got = swap(gn_other, CORE), swap(out_other, CORE)

    layer = (middle + (out_sum[0] + out_got.astype(f32) + vec[:, VEC_LAST : VEC_LAST + 1].astype(f32))).astype(bf16)
    layer_out = across(layer.reshape(nn, part, quarter)).transpose(1, 0, 2).reshape(part, tok)

    add = lambda *terms: sum(t.astype(f32) for t in terms)
    up_gy = add(up_gy, up_got_xy).astype(bf16)
    dt_gx = add(dt_gx, dt_got_xy).astype(bf16)
    up_got_y, dt_got_x = swap(up_gy, Y), swap(dt_gx, X)

    grad_mid, grad_att, grad_wo_t, sums_two = run_branch_back(
        gn_sum, gn_got, middle, grad_cols, att, w_attn, vec
    )
    back_in = starts, small, qt, kt, k, v, grad_att, att, lse, segk, segq
    back_a = run_backward(*back_in, (0, 3))
    up_got_y, dt_got_x = after((back_a[0],), up_got_y, dt_got_x)
    up_g = add(up_g, up_got_x, up_got_y)
    dt_g = add(dt_g, dt_got_x, dt_got_y)
    for bit in reversed(high):
        half = up_g.shape[1] // 2
        up_g = up_g[:, :half] + swap(up_g[:, half:].astype(bf16), bit).astype(f32)
        dt_g = dt_g[:, :half] + swap(dt_g[:, half:].astype(bf16), bit).astype(f32)
    ud_g = jnp.concatenate([up_g, dt_g], axis=1).astype(bf16)
    ud_grad = across(ud_g.reshape(nn, part, -1))
    dqt_a = after((ud_g, layer_out), back_a[0])
    dqt, dk, dv = run_backward(*back_in, (3, groups), (dqt_a, *back_a[1:]))
    grad_in, grad_w, sums_one, vb_rows = run_project_back(x_low, normed, dqt, dk, dv, w_attn, grad_mid, vec)
    sums_one, sums_two = jnp.sum(sums_one, axis=2), jnp.sum(sums_two, axis=2)
    vector_rows = jnp.concatenate(
        [sums_one, jnp.sum(vb_rows, axis=0, keepdims=True), sums_two, jnp.pad(ub_parts, ((0, 0), (0, D - F)))]
    )
    vector_rows = vector_rows + sum(z_rotate(vector_rows, r) for r in range(1, nn))
    ud_grad = jnp.sum(ud_grad.reshape(nn, part, -1).astype(f32), axis=0)
    units = ud_grad.shape[1] // 2
    up_grad, down_grad = ud_grad[:, :units], ud_grad[:, units:].T
    grad_in = across(grad_in.reshape(nn, part, span)).astype(f32)
    tokens_grad = sum(
        jnp.pad(grad_in[j], ((0, 0), (j * quarter, tok - (j + 1) * quarter))) for j in range(nn)
    )[:, halo : halo + tok]

    attn_g = jnp.concatenate([grad_w, grad_wo_t[None]])
    attn_g = attn_g.reshape(4, nw, dw, D).transpose(1, 0, 2, 3)
    pick = lambda masks: jnp.concatenate(
        [lax.dynamic_index_in_dim(attn_g, mw ^ m, 0, True) for m in masks], axis=0
    )
    masks = [0]
    for bit in high:
        masks = masks + [m ^ bit for m in masks]
    masks = [m ^ b for b in (0, X, Y, X | Y) for m in masks]
    half = add(pick(masks), swap(pick([m ^ CORE for m in masks]), CORE)).astype(bf16)
    g0, gx, gy, gxy = (half[i * count : (i + 1) * count] for i in range(4))
    gy_low = add(gy[:, :2], swap(gxy[:, :2], X)).astype(bf16)
    gx_high = add(gx[:, 2:], swap(gxy[:, 2:], Y)).astype(bf16)
    gx = jnp.concatenate([gx[:, :2], gx_high], axis=1)
    gy = jnp.concatenate([gy_low, gy[:, 2:]], axis=1)
    g0 = add(g0, swap(gx, X), swap(gy, Y))
    for bit in reversed(high):
        cut = g0.shape[0] // 2
        g0 = g0[:cut] + swap(g0[cut:].astype(bf16), bit).astype(f32)
    g0 = g0[0].astype(bf16).reshape(4 * dw, D).T.reshape(nn, part, 4 * dw)
    attn_grad = jnp.sum(across(g0).reshape(nn, part, 4 * dw).astype(f32), axis=0)
    qkv_grad = attn_grad[:, : 3 * dw].T.reshape(3, dw, part)
    out_weight_grad = attn_grad[:, 3 * dw :]

    class_ids = jnp.arange(CLASSES, dtype=jnp.int32)
    label_hits = labels[:, None] == class_ids
    counts = jnp.stack(
        [
            jnp.sum(((predicted[:, None] == class_ids) & label_hits).astype(f32), axis=0),
            jnp.sum(label_hits.astype(f32), axis=0),
        ]
    )
    sums = lax.dynamic_slice_in_dim(vector_rows[:8], me * part, part, 1)
    ub_parts = vector_rows[8:, :F]
    ub_g = ub_parts[0] + swap(ub_parts[1], X) + swap(ub_parts[2], Y) + swap(ub_parts[3], X | Y)
    for bit in reversed(high):
        cut = ub_g.shape[0] // 2
        ub_g = ub_g[:cut] + swap(ub_g[cut:], bit)
    counts = jnp.pad(counts.reshape(1, -1), ((0, 0), (0, part - counts.size)))
    sums = wide_sum(jnp.concatenate([sums, counts]))
    gain_one_g, shift_one_g, q_bias_g, v_bias_g, out_bias_g, gain_two_g, shift_two_g, down_bias_g = sums[:8]
    counts = sums[8, : 2 * CLASSES].reshape(2, CLASSES)
    tallies = counts.astype(jnp.int32)
    accuracy = jnp.sum(counts[0]) / jnp.maximum(jnp.sum(counts[1]), 1.0)
    return (
        layer_out,
        tokens_grad,
        gain_one_g,
        shift_one_g,
        qkv_grad,
        jnp.stack([q_bias_g, v_bias_g]),
        out_weight_grad,
        out_bias_g,
        gain_two_g,
        shift_two_g,
        up_grad,
        ub_g,
        down_grad,
        down_bias_g,
        tallies,
        accuracy,
    )


def solution(mesh):
    return jax.shard_map(
        shards,
        mesh=mesh,
        in_specs=(
            P("narrow", "wide"),
            P("narrow"),
            P("narrow"),
            P(None, "wide", "narrow"),
            P(None, "narrow"),
            P("narrow", "wide"),
            P("narrow"),
            P("narrow"),
            P("narrow"),
            P("narrow", "wide"),
            P("wide"),
            P("wide", "narrow"),
            P("narrow"),
            P("wide"),
            P("narrow", "wide"),
            P("wide"),
            P("wide"),
        ),
        out_specs=(
            P("narrow", "wide"),
            P("narrow", "wide"),
            P("narrow"),
            P("narrow"),
            P(None, "wide", "narrow"),
            P(None, "narrow"),
            P("narrow", "wide"),
            P("narrow"),
            P("narrow"),
            P("narrow"),
            P("narrow", "wide"),
            P("wide"),
            P("wide", "narrow"),
            P("narrow"),
            P(),
            P(),
        ),
        check_vma=False,
    )
```

```python
import functools

import jax
import jax.numpy as jnp
from jax import lax
from jax.experimental import pallas as pl
from jax.experimental.pallas import tpu as pltpu
from jax.sharding import PartitionSpec as P

HEAD_DIM = 32
SEQ = 1024
CLASSES = 4
LONGEST = 256
EPS = 1e-05
QT = 256
KT = 128
GROUP = 4
LANES = 128
LOG2E = 1.4426950408889634
SCALE = HEAD_DIM**-0.5
MASKED = -1e30
VMEM_LIMIT = 58 * 1024 * 1024
VEC_BLOCK, VEC_AT = 2, 64
VEC_LAST = VEC_BLOCK * 128 + VEC_AT + 7
bf16, f32 = jnp.bfloat16, jnp.float32

NN = (((1,), (0,)), ((), ()))
NT = (((1,), (1,)), ((), ()))
TN = (((0,), (0,)), ((), ()))

PHI_P = 0.33
PHI_C = (
    0.1328227541618569,
    0.117797452145417,
    0.18652846971894854,
    -0.09893620415601319,
    0.3406397450924515,
    -0.22542553879715763,
    0.046573313873415075,
)


def mm(left, right, dims=NN):
    return lax.dot_general(left, right, dims, preferred_element_type=f32)


def normal_cdf(u):
    bell = jnp.exp(-0.5 * (u * u))
    t = 1.0 / (1.0 + PHI_P * jnp.abs(u))
    tail = jnp.full_like(t, PHI_C[-1])
    for c in PHI_C[-2::-1]:
        tail = tail * t + c
    tail = tail * t * bell
    return jnp.where(u >= 0, 1.0 - tail, tail), bell * 0.3989422804014327


def head_only(block, h, axis):
    index = lax.broadcasted_iota(jnp.int32, block.shape, axis)
    keep = (index >= h * HEAD_DIM) & (index < (h + 1) * HEAD_DIM)
    return jnp.where(keep, block, jnp.zeros_like(block))


def key_bias(segk_ref, segq_ref, start, window):
    segk = segk_ref[pl.ds(start, window), :]
    segk = jnp.concatenate([segk] * (QT // LANES), axis=1)
    return jnp.where(segk == segq_ref[0:1, :], 0.0, MASKED).astype(f32)


def attend_forward(start_ref, small_ref, q_ref, k_ref, vt_ref, segk_ref, segq_ref, *refs):
    att_ref, lse_ref = refs[-2:]
    tile = pl.program_id(1)

    def run(window):
        start = pl.multiple_of(start_ref[tile] * KT, KT)
        keys = k_ref[pl.ds(start, window), :]
        bias = key_bias(segk_ref, segq_ref, start, window)
        q = q_ref[...]
        for h in range(GROUP):
            rows = slice(h * HEAD_DIM, (h + 1) * HEAD_DIM)
            scores = mm(keys, head_only(q, h, 0)) + bias
            top = jnp.max(scores, axis=0, keepdims=True)
            probs = jnp.exp2((scores - top) * (SCALE * LOG2E))
            total = jnp.sum(probs, axis=0, keepdims=True)
            out = mm(vt_ref[rows, pl.ds(start, window)], probs.astype(bf16))
            att_ref[rows, :] = (out / total).astype(bf16)
            lse_ref[h : h + 1, :] = top * (SCALE * LOG2E) + jnp.log2(total)

    @pl.when(small_ref[tile] == 1)
    def _():
        run(4 * KT)

    @pl.when(small_ref[tile] == 0)
    def _():
        run(6 * KT)


def attend_backward(
    start_ref, small_ref, qt_ref, kt_ref, k_ref, v_ref, dot_ref, att_ref, lse_ref, segk_ref, segq_ref, *refs
):
    dqt_ref, dk_ref, dv_ref, dk_sum, dv_sum = refs[-5:]
    tile = pl.program_id(1)

    @pl.when(tile == 0)
    def _():
        dk_sum[...] = jnp.zeros_like(dk_sum)
        dv_sum[...] = jnp.zeros_like(dv_sum)

    def run(window):
        start = pl.multiple_of(start_ref[tile] * KT, KT)
        at = pl.ds(start, window)
        keys, values = k_ref[at, :], v_ref[at, :]
        bias = key_bias(segk_ref, segq_ref, start, window)
        qt, dot = qt_ref[...], dot_ref[...]
        q, do = qt.T, dot.T
        inner = dot.astype(f32) * att_ref[...].astype(f32)
        dk = jnp.zeros((window, LANES), f32)
        dv = jnp.zeros((window, LANES), f32)
        for h in range(GROUP):
            rows = slice(h * HEAD_DIM, (h + 1) * HEAD_DIM)
            delta = jnp.sum(inner[rows, :], axis=0, keepdims=True)
            scores = mm(keys, head_only(qt, h, 0)) * (SCALE * LOG2E)
            probs = jnp.exp2((scores - lse_ref[h : h + 1, :]) + bias)
            dv = dv + mm(probs.astype(bf16), head_only(do, h, 1))
            grad_probs = mm(values, head_only(dot, h, 0))
            grad_scores = (probs * (grad_probs - delta)).astype(bf16)
            dk = dk + mm(grad_scores, head_only(q, h, 1))
            dq = mm(kt_ref[rows, at], grad_scores)
            dqt_ref[rows, :] = (dq * SCALE).astype(bf16)
        dk_sum[at, :] += dk
        dv_sum[at, :] += dv

    @pl.when(small_ref[tile] == 1)
    def _():
        run(4 * KT)

    @pl.when(small_ref[tile] == 0)
    def _():
        run(6 * KT)

    @pl.when(tile == pl.num_programs(1) - 1)
    def _():
        dk_ref[...] = (dk_sum[...] * SCALE).astype(bf16)
        dv_ref[...] = dv_sum[...].astype(bf16)


def attention_specs(span, begin):
    spec = pl.BlockSpec
    return {
        "q_cols": spec((LANES, QT), lambda g, j, *_: (g + begin, j)),
        "k_cols": spec((LANES, span), lambda g, j, *_: (g + begin, 0)),
        "k_rows": spec((span, LANES), lambda g, j, *_: (0, g + begin)),
        "lse": spec((8, QT), lambda g, j, *_: (g + begin, j)),
        "segk": spec((span, LANES), lambda g, j, *_: (0, 0)),
        "segq": spec((8, QT), lambda g, j, *_: (0, j)),
    }


def run_forward(starts, small, qt, k, vt, segk, segq, span_of_groups, outs=()):
    D, rows = qt.shape
    span = k.shape[0]
    begin, end = span_of_groups
    s = attention_specs(span, begin)
    groups = D // LANES
    outs = tuple(outs)
    return pl.pallas_call(
        attend_forward,
        grid_spec=pltpu.PrefetchScalarGridSpec(
            num_scalar_prefetch=2,
            grid=(end - begin, rows // QT),
            in_specs=[s["q_cols"], s["k_rows"], s["k_cols"], s["segk"], s["segq"]]
            + [pl.BlockSpec(memory_space=pl.ANY)] * len(outs),
            out_specs=[s["q_cols"], s["lse"]],
        ),
        input_output_aliases={7: 0, 8: 1} if outs else {},
        out_shape=[
            jax.ShapeDtypeStruct((D, rows), bf16),
            jax.ShapeDtypeStruct((groups * 8, rows), f32),
        ],
        name="attend_forward",
        **kernel_params(6 * (end - begin)),
    )(starts, small, qt, k, vt, segk, segq, *outs)


def run_backward(starts, small, qt, kt, k, v, dot, att, lse, segk, segq, span_of_groups, outs=()):
    D, rows = qt.shape
    span = k.shape[0]
    begin, end = span_of_groups
    s = attention_specs(span, begin)
    outs = tuple(outs)
    return pl.pallas_call(
        attend_backward,
        grid_spec=pltpu.PrefetchScalarGridSpec(
            num_scalar_prefetch=2,
            grid=(end - begin, rows // QT),
            in_specs=[
                s["q_cols"], s["k_cols"], s["k_rows"], s["k_rows"], s["q_cols"], s["q_cols"],
                s["lse"], s["segk"], s["segq"],
            ]
            + [pl.BlockSpec(memory_space=pl.ANY)] * len(outs),
            out_specs=[s["q_cols"], s["k_rows"], s["k_rows"]],
            scratch_shapes=[pltpu.VMEM((span, LANES), f32), pltpu.VMEM((span, LANES), f32)],
        ),
        out_shape=[
            jax.ShapeDtypeStruct((D, rows), bf16),
            jax.ShapeDtypeStruct((span, D), bf16),
            jax.ShapeDtypeStruct((span, D), bf16),
        ],
        input_output_aliases={11: 0, 12: 1, 13: 2} if outs else {},
        name="attend_backward",
        **kernel_params(7 * (end - begin)),
    )(starts, small, qt, kt, k, v, dot, att, lse, segk, segq, *outs)


def norm_parts(cols):
    centre = jnp.mean(cols, axis=0, keepdims=True)
    shifted = cols - centre
    spread = jnp.mean(jnp.square(shifted), axis=0, keepdims=True)
    scale = lax.rsqrt(spread + EPS)
    return shifted * scale, scale


def norm_back(grad, xhat, scale, gain):
    e = grad * gain
    mean_e = jnp.mean(e, axis=0, keepdims=True)
    mean_ex = jnp.mean(e * xhat, axis=0, keepdims=True)
    return scale * (e - mean_e - xhat * mean_ex)


VECTORS = ("gain_one", "shift_one", "q_bias", "v_bias", "bias_out", "gain_two", "shift_two", "bias_down")


def vector(vec_ref, name):
    i = VEC_AT + VECTORS.index(name)
    return vec_ref[:, i : i + 1].astype(f32)


def fold(x):
    return sum(x[:, i : i + LANES] for i in range(0, x.shape[1], LANES))


def row_sums(parts):
    rows = [jnp.sum(part.T, axis=0, keepdims=True) for part in parts]
    return jnp.concatenate(rows + [jnp.zeros((8 - len(rows), rows[0].shape[1]), f32)], axis=0)


def whole(shape, block=None):
    return pl.BlockSpec(shape, lambda *_: (0,) * len(shape) if block is None else block)


def kernel_params(micros):
    return {
        "compiler_params": pltpu.CompilerParams(vmem_limit_bytes=VMEM_LIMIT),
        "cost_estimate": pl.CostEstimate(flops=micros * 10**9, bytes_accessed=10**6, transcendentals=0),
    }


def project(parts, count, member_ref, x_ref, vec_ref, *refs):
    pieces, refs = refs[:count], refs[count:]
    n_ref, qt_ref, kt_ref, vt_ref, k_ref, v_ref, w_ref, w, wt, in_sem, out_sem = refs
    i = pl.program_id(0)
    out = pltpu.make_async_copy(w, w_ref, out_sem)

    @pl.when(i == 0)
    def _():
        copies = []
        for piece, first, rows, c, mask in parts:
            at = pl.multiple_of((member_ref[0] ^ mask) * rows, 16)
            copy = pltpu.make_async_copy(
                pieces[piece].at[first : first + rows], w.at[c, pl.ds(at, rows)], in_sem.at[len(copies)]
            )
            copy.start()
            copies.append(copy)
        for copy in copies:
            copy.wait()
        out.start()
        for c in range(3):
            wt[c] = w[c].T

    xhat, _ = norm_parts(x_ref[...].astype(f32))
    normed = (xhat * vector(vec_ref, "gain_one") + vector(vec_ref, "shift_one")).astype(bf16)
    n_ref[...] = normed
    kt = mm(wt[1], normed).astype(bf16)
    vt = (mm(wt[2], normed) + vector(vec_ref, "v_bias")).astype(bf16)
    kt_ref[...], vt_ref[...] = kt, vt
    k_ref[...], v_ref[...] = kt.T, vt.T

    @pl.when((i >= 1) & (i < pl.num_programs(0) - 1))
    def _():
        qt_ref[...] = (mm(wt[0], normed) + vector(vec_ref, "q_bias")).astype(bf16)

    @pl.when(i == pl.num_programs(0) - 1)
    def _():
        out.wait()


def run_project(x, vec, member, pieces, parts):
    D, span = x.shape
    steps = span // QT
    cols = pl.BlockSpec((D, QT), lambda i, _: (0, i))
    rows = pl.BlockSpec((QT, D), lambda i, _: (i, 0))
    own = pl.BlockSpec((D, QT), lambda i, _: (0, jnp.clip(i - 1, 0, steps - 3)))
    anywhere = pl.BlockSpec(memory_space=pl.ANY)
    shape = jax.ShapeDtypeStruct
    return pl.pallas_call(
        functools.partial(project, parts, len(pieces)),
        grid_spec=pltpu.PrefetchScalarGridSpec(
            num_scalar_prefetch=1,
            grid=(steps,),
            in_specs=[cols, whole((D, LANES), (0, VEC_BLOCK))] + [anywhere] * len(pieces),
            out_specs=[cols, own, cols, cols, rows, rows, anywhere],
            scratch_shapes=[
                pltpu.VMEM((4, D, D), bf16),
                pltpu.VMEM((3, D, D), bf16),
                pltpu.SemaphoreType.DMA((len(parts),)),
                pltpu.SemaphoreType.DMA,
            ],
        ),
        out_shape=[
            shape((D, span), bf16),
            shape((D, span - 2 * QT), bf16),
            shape((D, span), bf16),
            shape((D, span), bf16),
            shape((span, D), bf16),
            shape((span, D), bf16),
            shape((4, D, D), bf16),
        ],
        name="project",
        **kernel_params(11),
    )(member, x, vec, *pieces)


def project_weights(masks, member_ref, n_ref, dqt_ref, dk_ref, dv_ref, gwo_ref, *refs):
    outs, (sums_ref, gw, sem) = refs[:-3], refs[-3:]
    rows = dqt_ref.shape[1]
    halo = (n_ref.shape[1] - rows) // 2
    copies = []

    def send(c):
        if not masks:
            targets = [(gw.at[c], outs[0].at[c])]
        else:
            run = outs[0].shape[2]
            targets = []
            for far in (1, 0):
                for i, mask in enumerate(masks):
                    at = pl.multiple_of((member_ref[0] ^ (mask | far * CORE)) * run, 16)
                    targets.append((gw.at[c, pl.ds(at, run)], outs[far].at[i, c]))
        for source, target in targets:
            copy = pltpu.make_async_copy(source, target, sem.at[len(copies)])
            copy.start()
            copies.append(copy)

    gw[3] = gwo_ref[...]
    send(3)
    gw[0] = mm(n_ref[:, halo : halo + rows], dqt_ref[...], NT).astype(bf16)
    send(0)
    gw[1] = mm(n_ref[...], dk_ref[...]).astype(bf16)
    send(1)
    gw[2] = mm(n_ref[...], dv_ref[...]).astype(bf16)
    send(2)
    sums_ref[...] = row_sums([fold(dqt_ref[...].astype(f32))])
    sums_ref[1:2, :] = jnp.sum(dv_ref[...].astype(f32), axis=0, keepdims=True)
    for copy in copies:
        copy.wait()


def run_project_weights(normed, dqt, dk, dv, gwo, member, masks, run):
    D = normed.shape[0]
    shape = jax.ShapeDtypeStruct
    vmem, anywhere = pl.BlockSpec(memory_space=pltpu.VMEM), pl.BlockSpec(memory_space=pl.ANY)
    outs = [shape((len(masks), 4, run, D), bf16)] * 2 if masks else [shape((4, D, D), bf16)]
    return pl.pallas_call(
        functools.partial(project_weights, masks),
        in_specs=[pl.BlockSpec(memory_space=pltpu.SMEM)] + [vmem] * 5,
        out_specs=[anywhere] * len(outs) + [vmem],
        out_shape=outs + [shape((8, D), f32)],
        scratch_shapes=[pltpu.VMEM((4, D, D), bf16), pltpu.SemaphoreType.DMA((8 * max(1, len(masks)),))],
        name="project_weights",
        **kernel_params(8),
    )(member, normed, dqt, dk, dv, gwo)


def project_back(x_ref, dqt_ref, dk_ref, dv_ref, w_ref, mid_ref, vec_ref, grad_ref, rows_ref, sums_ref):
    i = pl.program_id(0)
    own = (i >= 1) & (i < pl.num_programs(0) - 1)

    @pl.when(i == 0)
    def _():
        sums_ref[...] = jnp.zeros_like(sums_ref)

    dqt = jnp.where(own, dqt_ref[...], jnp.zeros_like(dqt_ref))
    grad = mm(w_ref[1], dk_ref[...], NT) + mm(w_ref[2], dv_ref[...], NT) + mm(w_ref[0], dqt)
    xhat, scale = norm_parts(x_ref[...].astype(f32))
    sums_ref[0] += fold(grad * xhat)
    sums_ref[1] += fold(grad)
    grad_in = norm_back(grad, xhat, scale, vector(vec_ref, "gain_one"))
    grad_ref[...] = (grad_in + jnp.where(own, mid_ref[...], 0.0)).astype(bf16)

    @pl.when(i == pl.num_programs(0) - 1)
    def _():
        rows_ref[...] = row_sums([sums_ref[0], sums_ref[1]])


def run_project_back(x, dqt, dk, dv, w, grad_mid, vec):
    D, span = x.shape
    steps = span // QT
    cols = pl.BlockSpec((D, QT), lambda i: (0, i))
    rows = pl.BlockSpec((QT, D), lambda i: (i, 0))
    own = pl.BlockSpec((D, QT), lambda i: (0, jnp.clip(i - 1, 0, steps - 3)))
    shape = jax.ShapeDtypeStruct
    return pl.pallas_call(
        project_back,
        grid=(steps,),
        in_specs=[cols, own, rows, rows, whole((3, D, D)), own, whole((D, LANES), (0, VEC_BLOCK))],
        out_specs=[cols, whole((8, D))],
        out_shape=[shape((D, span), bf16), shape((8, D), f32)],
        scratch_shapes=[pltpu.VMEM((2, D, LANES), f32)],
        name="project_back",
        **kernel_params(10),
    )(x, dqt, dk, dv, w, grad_mid, vec)


def branch(att_ref, wo_ref, x_ref, vec_ref, mid_ref, n_ref):
    out = mm(wo_ref[0], att_ref[...]) + vector(vec_ref, "bias_out")
    middle = x_ref[...].astype(f32) + out
    mid_ref[...] = middle
    xhat, _ = norm_parts(middle)
    n_ref[...] = (xhat * vector(vec_ref, "gain_two") + vector(vec_ref, "shift_two")).astype(bf16)


def run_branch(att, w, x, vec):
    D, rows = att.shape
    cols = pl.BlockSpec((D, QT), lambda i: (0, i))
    return pl.pallas_call(
        branch,
        grid=(rows // QT,),
        in_specs=[
            cols,
            whole((1, D, D), (3, 0, 0)),
            pl.BlockSpec((D, QT), lambda i: (0, i + LONGEST // QT)),
            whole((D, LANES), (0, VEC_BLOCK)),
        ],
        out_specs=[cols, cols],
        out_shape=[jax.ShapeDtypeStruct((D, rows), f32), jax.ShapeDtypeStruct((D, rows), bf16)],
        name="branch",
        **kernel_params(5),
    )(att, w, x, vec)


def branch_back(
    gn_ref, got_ref, mid_ref, g_ref, att_ref, wo_ref, vec_ref,
    gmid_ref, gatt_ref, gwo_ref, rows_ref, wo, gwo_sum, sums_ref,
):
    i = pl.program_id(0)

    @pl.when(i == 0)
    def _():
        wo[...] = wo_ref[0].T
        gwo_sum[...] = jnp.zeros_like(gwo_sum)
        sums_ref[...] = jnp.zeros_like(sums_ref)

    grad = gn_ref[...] + got_ref[...].astype(f32)
    xhat, scale = norm_parts(mid_ref[...])
    g = g_ref[...].astype(f32)
    grad_mid = g + norm_back(grad, xhat, scale, vector(vec_ref, "gain_two"))
    gmid_ref[...] = grad_mid
    low = grad_mid.astype(bf16)
    gatt_ref[...] = mm(wo[...], low).astype(bf16)
    gwo_sum[...] += mm(low, att_ref[...], NT)
    sums_ref[0] += fold(low.astype(f32))
    sums_ref[1] += fold(grad * xhat)
    sums_ref[2] += fold(grad)
    sums_ref[3] += fold(g)

    @pl.when(i == pl.num_programs(0) - 1)
    def _():
        gwo_ref[...] = gwo_sum[...].astype(bf16)
        rows_ref[...] = row_sums([sums_ref[i] for i in range(4)])


def run_branch_back(gn, got, middle, g, att, w, vec):
    D, rows = att.shape
    cols = pl.BlockSpec((D, QT), lambda i: (0, i))
    shape = jax.ShapeDtypeStruct
    return pl.pallas_call(
        branch_back,
        grid=(rows // QT,),
        in_specs=[
            cols, cols, cols, cols, cols,
            whole((1, D, D), (3, 0, 0)),
            whole((D, LANES), (0, VEC_BLOCK)),
        ],
        out_specs=[cols, cols, whole((D, D)), whole((8, D))],
        out_shape=[
            shape((D, rows), f32),
            shape((D, rows), bf16),
            shape((D, D), bf16),
            shape((8, D), f32),
        ],
        scratch_shapes=[pltpu.VMEM((D, D), bf16), pltpu.VMEM((D, D), f32), pltpu.VMEM((4, D, LANES), f32)],
        name="branch_back",
        **kernel_params(9),
    )(gn, got, middle, g, att, w, vec)


def feed_forward(first, places, *refs):
    blocks, weights = len(places), 1 + max(p[0] for place in places for p in place)
    n2_in, g_in, refs = refs[0:2], refs[2:4], refs[4:]
    weights, refs = refs[:weights], refs[weights:]
    if not first:
        sums_in, refs = refs[:4], refs[4:]
    sums_out, refs = refs[:4], refs[4:]
    dw_out, refs = refs[: 2 * blocks], refs[2 * blocks :]
    dub_out, refs = refs[:blocks], refs[blocks:]
    n2, g, up, dt, ub, up_t, down, act, gh, dw, sums, low, in_sem, out_sem = refs
    D, F = up.shape
    f, rows = F // blocks, n2.shape[2]

    arrivals = {}

    def fetch(name, source, target):
        copy = pltpu.make_async_copy(source, target, in_sem.at[len(arrivals)])
        copy.start()
        arrivals[name] = copy

    def weight(name, target, b, part):
        ref, at = places[b][part]
        fetch((name, b), weights[ref].at[:, at : at + f], target.at[:, b * f : (b + 1) * f])

    for b in range(blocks):
        weight("up", up, b, 0)
    fetch("n2", n2_in[0], n2.at[0])
    for b in range(blocks):
        weight("dt", dt, b, 1)
        ref, at = places[b][2]
        fetch(("ub", b), weights[ref].at[at : at + 16], ub.at[b])
    fetch("g", g_in[0], g.at[0])
    fetch("n2 other", n2_in[1], n2.at[1])
    fetch("g other", g_in[1], g.at[1])
    if not first:
        for i in range(4):
            fetch(("sum", i), sums_in[i], low.at[i])

    departures = []

    def send(source, target):
        copy = pltpu.make_async_copy(source, target, out_sem.at[len(departures)])
        copy.start()
        departures.append(copy)

    columns = []
    for b in range(blocks):
        arrivals["up", b].wait()
        up_t[b * f : (b + 1) * f, :] = up[:, b * f : (b + 1) * f].T
    for b in range(blocks):
        arrivals["dt", b].wait()
        down[b * f : (b + 1) * f, :] = dt[:, b * f : (b + 1) * f].T
        arrivals["ub", b].wait()
        column = ub[b, :, :f].astype(f32).T[:, 0:1]
        columns.append(jnp.broadcast_to(column, (f, LANES)))
    bias = jnp.concatenate([jnp.concatenate(columns, axis=0)] * (QT // LANES), axis=1)
    arrivals["n2"].wait()
    arrivals["g"].wait()

    chunks = [(half, at) for half in range(2) for at in range(0, rows, QT)]

    def front(chunk):
        half, at = chunk
        if half == 1 and at == 0:
            arrivals["n2 other"].wait()
            arrivals["g other"].wait()
        return mm(up_t[...], n2[half, :, at : at + QT]), mm(down[...], g[half, :, at : at + QT])

    dub = jnp.zeros((F, LANES), f32)
    ready = front(chunks[0])
    for i, (half, at) in enumerate(chunks):
        following = front(chunks[i + 1]) if i + 1 < len(chunks) else None
        hidden, grad_act = ready
        hidden = hidden + bias
        cdf, pdf = normal_cdf(hidden)
        act[half, :, at : at + QT] = (hidden * cdf).astype(bf16)
        grad_hidden = (grad_act * (cdf + hidden * pdf)).astype(bf16)
        gh[half, :, at : at + QT] = grad_hidden
        dub = dub + fold(grad_hidden.astype(f32))
        ready = following
    for b in range(blocks):
        dub_out[b][...] = row_sums([dub[b * f : (b + 1) * f]])
    for part, (left, right) in enumerate(((n2, gh), (g, act))):
        dw[part] = (mm(left[0], right[0], NT) + mm(left[1], right[1], NT)).astype(bf16)
        for b in range(blocks):
            send(dw.at[part, :, b * f : (b + 1) * f], dw_out[2 * b + part])
    if not first:
        for i in range(4):
            arrivals["sum", i].wait()
    for i, (left, right) in enumerate(((up, gh), (dt, act))):
        for half in (1, 0):
            total = mm(left[...], right[half])
            k = 2 * i + half
            if not first:
                total = total + low[k].astype(f32)
            if half == 1 or first:
                low[k] = total.astype(bf16)
                send(low.at[k], sums_out[k])
            else:
                sums[i] = total
                send(sums.at[i], sums_out[k])
    for copy in departures:
        copy.wait()


def run_feed_forward(n2, g, blocks, sums):
    D, rows = n2[0].shape
    F = D
    first = sums is None
    weights, places = [], []
    for block in blocks:
        place = []
        for array, column in block:
            found = [i for i, w in enumerate(weights) if w is array]
            if not found:
                weights.append(array)
            place.append((found[0] if found else len(weights) - 1, column))
        places.append(place)
    sums = () if first else tuple(sums)
    count = len(blocks)
    shape = jax.ShapeDtypeStruct
    anywhere = pl.BlockSpec(memory_space=pl.ANY)
    vmem = pl.BlockSpec(memory_space=pltpu.VMEM)
    own_type = bf16 if first else f32
    outs = pl.pallas_call(
        functools.partial(feed_forward, first, places),
        in_specs=[anywhere] * (4 + len(weights) + len(sums)),
        out_specs=[anywhere] * (4 + 2 * count) + [vmem] * count,
        out_shape=[shape((D, rows), t) for t in (own_type, bf16, own_type, bf16)]
        + [shape((D, F), bf16)] * (2 * count)
        + [shape((8, F), f32)] * count,
        scratch_shapes=[
            pltpu.VMEM((2, D, rows), bf16),
            pltpu.VMEM((2, D, rows), bf16),
            pltpu.VMEM((D, count * F), bf16),
            pltpu.VMEM((D, count * F), bf16),
            pltpu.VMEM((count, 16, D), bf16),
            pltpu.VMEM((count * F, D), bf16),
            pltpu.VMEM((count * F, D), bf16),
            pltpu.VMEM((2, count * F, rows), bf16),
            pltpu.VMEM((2, count * F, rows), bf16),
            pltpu.VMEM((2, D, count * F), bf16),
            pltpu.VMEM((2, D, rows), f32),
            pltpu.VMEM((4, D, rows), bf16),
            pltpu.SemaphoreType.DMA((3 * count + 8,)),
            pltpu.SemaphoreType.DMA((2 * count + 4,)),
        ],
        name="feed_forward",
        **kernel_params(28),
    )(*n2, *g, *weights, *sums)
    grads = [(*outs[4 + 2 * b : 6 + 2 * b], outs[4 + 2 * count + b]) for b in range(count)]
    return outs[:4], grads


def z_rotate(x, k):
    n = lax.axis_size("narrow")
    return lax.ppermute(x, "narrow", [(i, (i + k) % n) for i in range(n)])


def z_gather(x):
    n, me = lax.axis_size("narrow"), lax.axis_index("narrow")
    stack = jnp.stack([x] + [z_rotate(x, k) for k in range(1, n)])
    return [lax.dynamic_index_in_dim(stack, lax.rem(me - j + n, n), 0, False) for j in range(n)]


def z_scatter_sum(pieces):
    n, me = lax.axis_size("narrow"), lax.axis_index("narrow")
    total = lax.dynamic_index_in_dim(pieces, me, 0, False).astype(f32)
    for k in range(1, n):
        piece = lax.dynamic_index_in_dim(pieces, lax.rem(me + k, n), 0, False)
        total = total + z_rotate(piece, k).astype(f32)
    return total


def swap(x, mask):
    n = lax.axis_size("wide")
    return lax.ppermute(x, "wide", [(i, i ^ mask) for i in range(n)])


def wide_sum(x):
    bit = 1
    while bit < lax.axis_size("wide"):
        x = x + swap(x, bit)
        bit *= 2
    return x


CORE, X, Y = 1, 2, 4


def after(deps, *values):
    n = len(values)
    tied = pl.pallas_call(
        lambda *refs: None,
        in_specs=[pl.BlockSpec(memory_space=pl.ANY)] * (n + len(deps)),
        out_specs=[pl.BlockSpec(memory_space=pl.ANY)] * n,
        out_shape=[jax.ShapeDtypeStruct(v.shape, v.dtype) for v in values],
        input_output_aliases={i: i for i in range(n)},
        name="tie",
    )(*values, *deps)
    return tied if n > 1 else tied[0]


def high_bits():
    bits, bit = [], 8
    while bit < lax.axis_size("wide"):
        bits.append(bit)
        bit *= 2
    return bits


def shards(
    tokens_in,
    ln1_gain,
    ln1_shift,
    w_qkv,
    qv_bias,
    w_out,
    out_bias,
    ln2_gain,
    ln2_shift,
    w_up,
    up_bias,
    w_down,
    down_bias,
    segment_ids,
    out_grad,
    predicted,
    labels,
):
    nn, me = lax.axis_size("narrow"), lax.axis_index("narrow")
    nw, mw = lax.axis_size("wide"), lax.axis_index("wide")
    part, tok = tokens_in.shape
    D = part * nn
    quarter = tok // nn
    halo = LONGEST
    span = quarter + 2 * halo
    high = high_bits()
    dw = w_qkv.shape[1]
    across = lambda x: lax.all_to_all(x, "narrow", 0, 0, tiled=True)

    position = jnp.arange(tok, dtype=jnp.int32)
    chunk = segment_ids * (tok // SEQ) + position // SEQ
    big = jnp.int32(2**30)
    chunk = jnp.concatenate([jnp.full((halo,), -1, jnp.int32), chunk, jnp.full((halo,), big, jnp.int32)])
    chunk = lax.dynamic_slice_in_dim(chunk, me * quarter, span, 0)
    chunk_own = chunk[halo : halo + quarter]
    tiles = quarter // QT
    edges = chunk_own.reshape(tiles, QT)
    low = jnp.sum((chunk[None] < edges[:, :1]).astype(jnp.int32), axis=1) // KT
    top = (jnp.sum((chunk[None] <= edges[:, -1:]).astype(jnp.int32), axis=1) + KT - 1) // KT
    small = (top - low <= 4).astype(jnp.int32)
    starts = jnp.minimum(low, span // KT - jnp.where(small == 1, 4, 6))
    segk = jnp.broadcast_to(chunk[:, None], (span, LANES))
    segq = jnp.broadcast_to(chunk_own[None], (8, quarter))

    piece = [w_qkv.reshape(3 * dw, part).T, w_out]
    piece += [jnp.zeros((part, VEC_BLOCK * LANES + VEC_AT - 4 * dw), bf16)]
    piece += [
        jnp.stack([ln1_gain, ln1_shift, qv_bias[0], qv_bias[1], out_bias, ln2_gain, ln2_shift, down_bias]).T
    ]
    piece = jnp.concatenate(piece, axis=1)
    piece = jnp.pad(piece, ((0, 0), (0, -piece.shape[1] % LANES)))
    vec = across(jnp.stack([piece] * nn)).reshape(D, -1)
    up_own = across(after((vec,), jnp.stack([w_up] * nn))).reshape(D, -1)
    units = up_bias.shape[0]
    bias_rows = jnp.pad(up_bias[None], ((0, 15), (0, D - units)))
    attn_own = after((vec,), jnp.concatenate([vec[:, : 4 * dw].T, bias_rows], axis=0))
    count, height = 1, 4 * dw + 16
    for bit in high:
        attn_own = jnp.concatenate([attn_own, swap(attn_own, bit)], axis=0)
        count *= 2
    cut = attn_own.shape[0] // 2 // 16 * 16
    from_x, from_y = swap(attn_own, X), swap(attn_own, Y)
    from_xy = swap(from_y[:cut], X), swap(from_x[cut:], Y)
    grad_blocks = jnp.stack([out_grad[:, j * quarter : (j + 1) * quarter] for j in range(nn)])
    padded = jnp.pad(tokens_in, ((0, 0), (halo, halo)))
    blocks = jnp.stack([padded[:, j * quarter : j * quarter + span] for j in range(nn)])
    blocks = after((starts, small, segk, segq, up_own, *from_xy, grad_blocks), blocks)
    x_low = across(blocks).reshape(D, span)
    dt_blocks = after((x_low,), jnp.stack([w_down.T] * nn))
    dt_own = across(dt_blocks).reshape(D, -1)
    bias_of = lambda a: jnp.concatenate(
        [a[j * height + 4 * dw : (j + 1) * height, :units] for j in range(count)], axis=1
    )
    if dw % 16 == 0:
        pieces = [attn_own, from_x, from_y, *from_xy]
        pieces += [swap(piece, CORE) for piece in pieces]
        parts = []
        for far in (0, 1):
            for i, mask in enumerate((0, X, Y)):
                parts += [(i + 5 * far, c * dw, dw, c, mask | far * CORE) for c in range(4)]
            for c in range(4):
                for first, last in ((c * dw, min((c + 1) * dw, cut)), (max(c * dw, cut), (c + 1) * dw)):
                    assert last <= first or last - first == dw
                    if last > first:
                        piece, start = (3, first) if last <= cut else (4, first - cut)
                        parts.append((piece + 5 * far, start, dw, c, (X | Y) | far * CORE))
        ub_own, ub_x, ub_y = (attn_own, 4 * dw), (from_x, 4 * dw), (from_y, 4 * dw)
        ub_xy = from_xy[1], 4 * dw - cut
    else:
        from_xy = jnp.concatenate(from_xy, axis=0)
        ub_own, ub_x, ub_y, ub_xy = ((bias_of(a), 0) for a in (attn_own, from_x, from_y, from_xy))
        half = jnp.concatenate([attn_own, from_x, from_y, from_xy], axis=0)
        half = half.reshape(-1, height, D)[:, : 4 * dw].reshape(-1, 4, dw, D)
        every = jnp.concatenate([half, swap(half, CORE)], axis=0)
        bits = high + [X, Y, CORE]
        place = lambda m: sum(((m // bit) % 2) << i for i, bit in enumerate(bits))
        every = [lax.dynamic_index_in_dim(every, place(mw ^ w), 0, True) for w in range(nw)]
        pieces = [jnp.concatenate(every, axis=0).transpose(1, 0, 2, 3).reshape(4 * D, D)]
        parts = [(0, c * D, D, c, 0) for c in range(4)]
    member = jnp.reshape(mw if dw % 16 == 0 else mw * 0, (1,)).astype(jnp.int32)

    for bit in high:
        up_own = jnp.concatenate([up_own, swap(up_own, bit)], axis=1)
    F = up_own.shape[1]
    up_x, up_y = swap(up_own, X), swap(up_own, Y)
    x_low = after((up_x, up_y), x_low)
    normed, qt, kt, vt, k, v, w_attn = run_project(x_low, vec, member, pieces, parts)
    groups = D // LANES
    forward_in = starts, small, qt, k, vt, segk, segq
    att, lse = run_forward(*forward_in, (0, 1))

    dt_own = after((att,), dt_own)
    grad_cols = across(after((dt_own,), grad_blocks)).reshape(D, quarter)
    for bit in high:
        dt_own = jnp.concatenate([dt_own, swap(dt_own, bit)], axis=1)
    dt_x, dt_y = swap(dt_own, X), swap(dt_own, Y)
    up_xy = swap(up_y, X)
    att = after((up_xy,), att)
    att, lse = run_forward(*forward_in, (1, 3), (att, lse))
    dt_x = after((att,), dt_x)
    dt_xy = swap(dt_x, Y)
    att, lse = run_forward(*forward_in, (3, groups), (att, lse))
    grad_cols = after((att,), grad_cols)
    grad_pair = grad_cols, swap(grad_cols, CORE)
    middle, normed_two = run_branch(att, w_attn, x_low, vec)

    normed_two = after((dt_xy,), normed_two)
    n2_pair = normed_two, swap(normed_two, CORE)
    blocks = [((up_xy, 0), (dt_xy, 0), ub_xy), ((up_x, 0), (dt_x, 0), ub_x)]
    sums, ((up_gxy, dt_gxy, ub_gxy), (up_gx, dt_gx, ub_gx)) = run_feed_forward(n2_pair, grad_pair, blocks, None)
    up_got_xy, dt_got_xy = swap(up_gxy, X), swap(dt_gxy, Y)
    blocks = [((up_y, 0), (dt_y, 0), ub_y), ((up_own, 0), (dt_own, 0), ub_own)]
    sums, ((up_gy, dt_gy, ub_gy), (up_g, dt_g, ub_g)) = run_feed_forward(n2_pair, grad_pair, blocks, sums)
    gn_sum, gn_other, out_sum, out_other = sums
    ub_g, ub_gx, ub_gy, ub_gxy = (rows[0] for rows in (ub_g, ub_gx, ub_gy, ub_gxy))
    gn_other = after((up_got_xy, dt_got_xy), gn_other)
    gn_got, out_got = swap(gn_other, CORE), swap(out_other, CORE)

    layer = (middle + (out_sum + out_got.astype(f32) + vec[:, VEC_LAST : VEC_LAST + 1].astype(f32))).astype(bf16)
    layer_out = across(layer.reshape(nn, part, quarter)).transpose(1, 0, 2).reshape(part, tok)

    add = lambda *terms: sum(t.astype(f32) for t in terms)
    up_gy = add(up_gy, up_got_xy).astype(bf16)
    up_got = swap(up_gx, X), swap(up_gy, Y)

    gn_got = after((layer,), gn_got)
    grad_mid, grad_att, grad_wo_t, sums_two = run_branch_back(
        gn_sum, gn_got, middle, grad_cols, att, w_attn, vec
    )
    back_in = starts, small, qt, kt, k, v, grad_att, att, lse, segk, segq
    dt_gx = add(dt_gx, dt_got_xy).astype(bf16)
    dt_got = swap(dt_gx, X), swap(dt_gy, Y)
    back_a = run_backward(*back_in, (0, 2))
    up_got_x, up_got_y, dt_got_x, dt_got_y = after((back_a[0],), *up_got, *dt_got)
    up_g, dt_g = add(up_g, up_got_x, up_got_y), add(dt_g, dt_got_x, dt_got_y)
    for bit in reversed(high):
        half = up_g.shape[1] // 2
        up_g = up_g[:, :half] + swap(up_g[:, half:].astype(bf16), bit).astype(f32)
        dt_g = dt_g[:, :half] + swap(dt_g[:, half:].astype(bf16), bit).astype(f32)
    ud_g = jnp.concatenate([up_g, dt_g], axis=1).astype(bf16)
    ud_grad = across(ud_g.reshape(nn, part, -1))
    dqt_a = after((ud_g, layer_out), back_a[0])
    dqt, dk, dv = run_backward(*back_in, (2, groups), (dqt_a, *back_a[1:]))
    ub_gx, ub_gy, ub_gxy = after((back_a[1],), ub_gx, ub_gy, ub_gxy)
    ub_g = ub_g + swap(ub_gx, X) + swap(ub_gy, Y) + swap(ub_gxy, X | Y)
    for bit in reversed(high):
        cut = ub_g.shape[0] // 2
        ub_g = ub_g[:cut] + swap(ub_g[cut:], bit)
    ub_g = jnp.pad(ub_g[None], ((0, 0), (0, D - units)))
    dqt = after((ub_g,), dqt)
    masks = [0]
    for bit in high:
        masks = masks + [m ^ bit for m in masks]
    masks = [m ^ b for b in (0, X, Y, X | Y) for m in masks]
    direct = masks if dw % 16 == 0 else []
    *grad_w, qv_rows = run_project_weights(normed, dqt, dk, dv, grad_wo_t, member, direct, dw)
    if not direct:
        grad_w = grad_w[0].reshape(4, nw, dw, D).transpose(1, 0, 2, 3)
        pick = lambda masks: jnp.concatenate(
            [lax.dynamic_index_in_dim(grad_w, mw ^ m, 0, True) for m in masks], axis=0
        )
        grad_w = pick(masks), pick([m ^ CORE for m in masks])
    attn_g, got = grad_w[0], swap(grad_w[1], CORE)
    dqt = after((grad_w[1], ud_grad), dqt)
    grad_in, sums_one = run_project_back(x_low, dqt, dk, dv, w_attn, grad_mid, vec)
    got = after((grad_in,), got)
    vector_rows = jnp.concatenate([sums_one[:2], qv_rows[:2], sums_two[:4]])
    ud_grad = jnp.sum(ud_grad.reshape(nn, part, -1).astype(f32), axis=0)
    up_grad, down_grad = ud_grad[:, :units], ud_grad[:, units:].T
    grad_in = across(grad_in.reshape(nn, part, span)).astype(f32)
    tokens_grad = sum(
        jnp.pad(grad_in[j], ((0, 0), (j * quarter, tok - (j + 1) * quarter))) for j in range(nn)
    )[:, halo : halo + tok]

    half = add(attn_g, got).astype(bf16)
    g0, gx, gy, gxy = (half[i * count : (i + 1) * count] for i in range(4))
    gy_low = add(gy[:, :2], swap(gxy[:, :2], X)).astype(bf16)
    gx_high = add(gx[:, 2:], swap(gxy[:, 2:], Y)).astype(bf16)
    gx = jnp.concatenate([gx[:, :2], gx_high], axis=1)
    gy = jnp.concatenate([gy_low, gy[:, 2:]], axis=1)
    g0 = add(g0, swap(gx, X), swap(gy, Y))
    for bit in reversed(high):
        cut = g0.shape[0] // 2
        g0 = g0[:cut] + swap(g0[cut:].astype(bf16), bit).astype(f32)
    g0 = g0[0].astype(bf16).reshape(4 * dw, D).T.reshape(nn, part, 4 * dw)
    g0 = after((grad_in,), g0)
    vector_rows = after((g0,), vector_rows)
    attn_grad = jnp.sum(across(g0).reshape(nn, part, 4 * dw).astype(f32), axis=0)
    qkv_grad = attn_grad[:, : 3 * dw].T.reshape(3, dw, part)
    out_weight_grad = attn_grad[:, 3 * dw :]

    class_ids = jnp.arange(CLASSES, dtype=jnp.int32)
    label_hits = labels[:, None] == class_ids
    counts = jnp.stack(
        [
            jnp.sum(((predicted[:, None] == class_ids) & label_hits).astype(f32), axis=0),
            jnp.sum(label_hits.astype(f32), axis=0),
        ]
    )
    counts = jnp.pad(counts.reshape(1, -1), ((0, 0), (0, D - counts.size)))
    sums = wide_sum(jnp.concatenate([vector_rows, counts]))
    counts = sums[8, : 2 * CLASSES].reshape(2, CLASSES)
    sums = jnp.concatenate([sums[:8], ub_g])
    sums = sums + sum(z_rotate(sums, r) for r in range(1, nn))
    ub_g = sums[8, :units]
    sums = lax.dynamic_slice_in_dim(sums[:8], me * part, part, 1)
    gain_one_g, shift_one_g, q_bias_g, v_bias_g, out_bias_g, gain_two_g, shift_two_g, down_bias_g = sums
    tallies = counts.astype(jnp.int32)
    accuracy = jnp.sum(counts[0]) / jnp.maximum(jnp.sum(counts[1]), 1.0)
    return (
        layer_out,
        tokens_grad,
        gain_one_g,
        shift_one_g,
        qkv_grad,
        jnp.stack([q_bias_g, v_bias_g]),
        out_weight_grad,
        out_bias_g,
        gain_two_g,
        shift_two_g,
        up_grad,
        ub_g,
        down_grad,
        down_bias_g,
        tallies,
        accuracy,
    )


def solution(mesh):
    return jax.shard_map(
        shards,
        mesh=mesh,
        in_specs=(
            P("narrow", "wide"),
            P("narrow"),
            P("narrow"),
            P(None, "wide", "narrow"),
            P(None, "narrow"),
            P("narrow", "wide"),
            P("narrow"),
            P("narrow"),
            P("narrow"),
            P("narrow", "wide"),
            P("wide"),
            P("wide", "narrow"),
            P("narrow"),
            P("wide"),
            P("narrow", "wide"),
            P("wide"),
            P("wide"),
        ),
        out_specs=(
            P("narrow", "wide"),
            P("narrow", "wide"),
            P("narrow"),
            P("narrow"),
            P(None, "wide", "narrow"),
            P(None, "narrow"),
            P("narrow", "wide"),
            P("narrow"),
            P("narrow"),
            P("narrow"),
            P("narrow", "wide"),
            P("wide"),
            P("wide", "narrow"),
            P("narrow"),
            P(),
            P(),
        ),
        check_vma=False,
    )
```

```python
import functools

import jax
import jax.numpy as jnp
from jax import lax
from jax.experimental import pallas as pl
from jax.experimental.pallas import tpu as pltpu
from jax.sharding import PartitionSpec as P

HEAD_DIM = 32
SEQ = 1024
CLASSES = 4
LONGEST = 256
EPS = 1e-05
QT = 256
KT = 128
GROUP = 4
LANES = 128
LOG2E = 1.4426950408889634
SCALE = HEAD_DIM**-0.5
MASKED = -1e30
VMEM_LIMIT = 58 * 1024 * 1024
VEC_BLOCK, VEC_AT = 2, 64
VEC_LAST = VEC_BLOCK * 128 + VEC_AT + 7
bf16, f32 = jnp.bfloat16, jnp.float32

NN = (((1,), (0,)), ((), ()))
NT = (((1,), (1,)), ((), ()))
TN = (((0,), (0,)), ((), ()))

PHI_P = 0.33
PHI_C = (
    0.1328227541618569,
    0.117797452145417,
    0.18652846971894854,
    -0.09893620415601319,
    0.3406397450924515,
    -0.22542553879715763,
    0.046573313873415075,
)


def mm(left, right, dims=NN):
    return lax.dot_general(left, right, dims, preferred_element_type=f32)


def normal_cdf(u):
    bell = jnp.exp(-0.5 * (u * u))
    t = 1.0 / (1.0 + PHI_P * jnp.abs(u))
    tail = jnp.full_like(t, PHI_C[-1])
    for c in PHI_C[-2::-1]:
        tail = tail * t + c
    tail = tail * t * bell
    return jnp.where(u >= 0, 1.0 - tail, tail), bell * 0.3989422804014327


def head_only(block, h, axis):
    index = lax.broadcasted_iota(jnp.int32, block.shape, axis)
    keep = (index >= h * HEAD_DIM) & (index < (h + 1) * HEAD_DIM)
    return jnp.where(keep, block, jnp.zeros_like(block))


def key_bias(segk_ref, segq_ref, start, window):
    segk = segk_ref[pl.ds(start, window), :]
    segk = jnp.concatenate([segk] * (QT // LANES), axis=1)
    return jnp.where(segk == segq_ref[0:1, :], 0.0, MASKED).astype(f32)


def attend_forward(start_ref, small_ref, q_ref, k_ref, vt_ref, segk_ref, segq_ref, *refs):
    att_ref, lse_ref = refs[-2:]
    tile = pl.program_id(1)

    def run(window):
        start = pl.multiple_of(start_ref[tile] * KT, KT)
        keys = k_ref[pl.ds(start, window), :]
        bias = key_bias(segk_ref, segq_ref, start, window)
        q = q_ref[...]
        rows = [slice(h * HEAD_DIM, (h + 1) * HEAD_DIM) for h in range(GROUP)]
        scores = [mm(keys, head_only(q, h, 0)) for h in range(GROUP)]
        ready = []
        for h in range(GROUP):
            masked = scores[h] + bias
            top = jnp.max(masked, axis=0, keepdims=True)
            probs = jnp.exp2((masked - top) * (SCALE * LOG2E))
            total = jnp.sum(probs, axis=0, keepdims=True)
            lse_ref[h : h + 1, :] = top * (SCALE * LOG2E) + jnp.log2(total)
            ready.append((probs.astype(bf16), total))
        for h, (probs, total) in enumerate(ready):
            out = mm(vt_ref[rows[h], pl.ds(start, window)], probs)
            att_ref[rows[h], :] = (out / total).astype(bf16)

    @pl.when(small_ref[tile] == 1)
    def _():
        run(4 * KT)

    @pl.when(small_ref[tile] == 0)
    def _():
        run(6 * KT)


def attend_backward(
    start_ref, small_ref, qt_ref, kt_ref, k_ref, v_ref, dot_ref, att_ref, lse_ref, segk_ref, segq_ref, *refs
):
    dqt_ref, dk_ref, dv_ref, dk_sum, dv_sum = refs[-5:]
    tile = pl.program_id(1)

    @pl.when(tile == 0)
    def _():
        dk_sum[...] = jnp.zeros_like(dk_sum)
        dv_sum[...] = jnp.zeros_like(dv_sum)

    def run(window):
        start = pl.multiple_of(start_ref[tile] * KT, KT)
        at = pl.ds(start, window)
        keys, values = k_ref[at, :], v_ref[at, :]
        bias = key_bias(segk_ref, segq_ref, start, window)
        qt, dot = qt_ref[...], dot_ref[...]
        q, do = qt.T, dot.T
        inner = dot.astype(f32) * att_ref[...].astype(f32)
        rows = [slice(h * HEAD_DIM, (h + 1) * HEAD_DIM) for h in range(GROUP)]
        products = [(mm(keys, head_only(qt, h, 0)), mm(values, head_only(dot, h, 0))) for h in range(GROUP)]
        probs_low, grads_low = [], []
        for h, (scores, grad_probs) in enumerate(products):
            delta = jnp.sum(inner[rows[h], :], axis=0, keepdims=True)
            probs = jnp.exp2((scores * (SCALE * LOG2E) - lse_ref[h : h + 1, :]) + bias)
            probs_low.append(probs.astype(bf16))
            grads_low.append((probs * (grad_probs - delta)).astype(bf16))
        heads_of = lambda block: jnp.concatenate([head_only(block, h, 1) for h in range(GROUP)], axis=0)
        dv = mm(jnp.concatenate(probs_low, axis=1), heads_of(do))
        dk = mm(jnp.concatenate(grads_low, axis=1), heads_of(q))
        for h in range(GROUP):
            dq = mm(kt_ref[rows[h], at], grads_low[h])
            dqt_ref[rows[h], :] = (dq * SCALE).astype(bf16)
        dk_sum[at, :] += dk
        dv_sum[at, :] += dv

    @pl.when(small_ref[tile] == 1)
    def _():
        run(4 * KT)

    @pl.when(small_ref[tile] == 0)
    def _():
        run(6 * KT)

    @pl.when(tile == pl.num_programs(1) - 1)
    def _():
        dk_ref[...] = (dk_sum[...] * SCALE).astype(bf16)
        dv_ref[...] = dv_sum[...].astype(bf16)


def attention_specs(span, begin):
    spec = pl.BlockSpec
    return {
        "q_cols": spec((LANES, QT), lambda g, j, *_: (g + begin, j)),
        "k_cols": spec((LANES, span), lambda g, j, *_: (g + begin, 0)),
        "k_rows": spec((span, LANES), lambda g, j, *_: (0, g + begin)),
        "lse": spec((8, QT), lambda g, j, *_: (g + begin, j)),
        "segk": spec((span, LANES), lambda g, j, *_: (0, 0)),
        "segq": spec((8, QT), lambda g, j, *_: (0, j)),
    }


def run_forward(starts, small, qt, k, vt, segk, segq, span_of_groups, outs=()):
    D, rows = qt.shape
    span = k.shape[0]
    begin, end = span_of_groups
    s = attention_specs(span, begin)
    groups = D // LANES
    outs = tuple(outs)
    return pl.pallas_call(
        attend_forward,
        grid_spec=pltpu.PrefetchScalarGridSpec(
            num_scalar_prefetch=2,
            grid=(end - begin, rows // QT),
            in_specs=[s["q_cols"], s["k_rows"], s["k_cols"], s["segk"], s["segq"]]
            + [pl.BlockSpec(memory_space=pl.ANY)] * len(outs),
            out_specs=[s["q_cols"], s["lse"]],
        ),
        input_output_aliases={7: 0, 8: 1} if outs else {},
        out_shape=[
            jax.ShapeDtypeStruct((D, rows), bf16),
            jax.ShapeDtypeStruct((groups * 8, rows), f32),
        ],
        name="attend_forward",
        **kernel_params(4 * (end - begin)),
    )(starts, small, qt, k, vt, segk, segq, *outs)


def run_backward(starts, small, qt, kt, k, v, dot, att, lse, segk, segq, span_of_groups, outs=()):
    D, rows = qt.shape
    span = k.shape[0]
    begin, end = span_of_groups
    s = attention_specs(span, begin)
    outs = tuple(outs)
    return pl.pallas_call(
        attend_backward,
        grid_spec=pltpu.PrefetchScalarGridSpec(
            num_scalar_prefetch=2,
            grid=(end - begin, rows // QT),
            in_specs=[
                s["q_cols"], s["k_cols"], s["k_rows"], s["k_rows"], s["q_cols"], s["q_cols"],
                s["lse"], s["segk"], s["segq"],
            ]
            + [pl.BlockSpec(memory_space=pl.ANY)] * len(outs),
            out_specs=[s["q_cols"], s["k_rows"], s["k_rows"]],
            scratch_shapes=[pltpu.VMEM((span, LANES), f32), pltpu.VMEM((span, LANES), f32)],
        ),
        out_shape=[
            jax.ShapeDtypeStruct((D, rows), bf16),
            jax.ShapeDtypeStruct((span, D), bf16),
            jax.ShapeDtypeStruct((span, D), bf16),
        ],
        input_output_aliases={11: 0, 12: 1, 13: 2} if outs else {},
        name="attend_backward",
        **kernel_params(6 * (end - begin)),
    )(starts, small, qt, kt, k, v, dot, att, lse, segk, segq, *outs)


def norm_parts(cols):
    centre = jnp.mean(cols, axis=0, keepdims=True)
    shifted = cols - centre
    spread = jnp.mean(jnp.square(shifted), axis=0, keepdims=True)
    scale = lax.rsqrt(spread + EPS)
    return shifted * scale, scale


def norm_back(grad, xhat, scale, gain):
    e = grad * gain
    mean_e = jnp.mean(e, axis=0, keepdims=True)
    mean_ex = jnp.mean(e * xhat, axis=0, keepdims=True)
    return scale * (e - mean_e - xhat * mean_ex)


VECTORS = ("gain_one", "shift_one", "q_bias", "v_bias", "bias_out", "gain_two", "shift_two", "bias_down")


def vector(vec_ref, name):
    i = VEC_AT + VECTORS.index(name)
    return vec_ref[:, i : i + 1].astype(f32)


def fold(x):
    return sum(x[:, i : i + LANES] for i in range(0, x.shape[1], LANES))


def row_sums(parts):
    rows = [jnp.sum(part.T, axis=0, keepdims=True) for part in parts]
    return jnp.concatenate(rows + [jnp.zeros((8 - len(rows), rows[0].shape[1]), f32)], axis=0)


def whole(shape, block=None):
    return pl.BlockSpec(shape, lambda *_: (0,) * len(shape) if block is None else block)


def kernel_params(micros):
    return {
        "compiler_params": pltpu.CompilerParams(vmem_limit_bytes=VMEM_LIMIT),
        "cost_estimate": pl.CostEstimate(flops=micros * 10**9, bytes_accessed=10**6, transcendentals=0),
    }


def project(parts, count, member_ref, x_ref, vec_ref, *refs):
    pieces, refs = refs[:count], refs[count:]
    n_ref, qt_ref, kt_ref, vt_ref, k_ref, v_ref, w_ref, w, wt, in_sem, out_sem = refs
    i = pl.program_id(0)
    out = pltpu.make_async_copy(w, w_ref, out_sem)

    @pl.when(i == 0)
    def _():
        copies = []
        for piece, first, rows, c, mask in parts:
            at = pl.multiple_of((member_ref[0] ^ mask) * rows, 16)
            copy = pltpu.make_async_copy(
                pieces[piece].at[first : first + rows], w.at[c, pl.ds(at, rows)], in_sem.at[len(copies)]
            )
            copy.start()
            copies.append(copy)
        for copy in copies:
            copy.wait()
        out.start()
        for c in range(3):
            wt[c] = w[c].T

    xhat, _ = norm_parts(x_ref[...].astype(f32))
    normed = (xhat * vector(vec_ref, "gain_one") + vector(vec_ref, "shift_one")).astype(bf16)
    n_ref[...] = normed
    kt = mm(wt[1], normed).astype(bf16)
    vt = (mm(wt[2], normed) + vector(vec_ref, "v_bias")).astype(bf16)
    kt_ref[...], vt_ref[...] = kt, vt
    k_ref[...], v_ref[...] = kt.T, vt.T

    @pl.when((i >= 1) & (i < pl.num_programs(0) - 1))
    def _():
        qt_ref[...] = (mm(wt[0], normed) + vector(vec_ref, "q_bias")).astype(bf16)

    @pl.when(i == pl.num_programs(0) - 1)
    def _():
        out.wait()


def run_project(x, vec, member, pieces, parts):
    D, span = x.shape
    steps = span // QT
    cols = pl.BlockSpec((D, QT), lambda i, _: (0, i))
    rows = pl.BlockSpec((QT, D), lambda i, _: (i, 0))
    own = pl.BlockSpec((D, QT), lambda i, _: (0, jnp.clip(i - 1, 0, steps - 3)))
    anywhere = pl.BlockSpec(memory_space=pl.ANY)
    shape = jax.ShapeDtypeStruct
    return pl.pallas_call(
        functools.partial(project, parts, len(pieces)),
        grid_spec=pltpu.PrefetchScalarGridSpec(
            num_scalar_prefetch=1,
            grid=(steps,),
            in_specs=[cols, whole((D, LANES), (0, VEC_BLOCK))] + [anywhere] * len(pieces),
            out_specs=[cols, own, cols, cols, rows, rows, anywhere],
            scratch_shapes=[
                pltpu.VMEM((4, D, D), bf16),
                pltpu.VMEM((3, D, D), bf16),
                pltpu.SemaphoreType.DMA((len(parts),)),
                pltpu.SemaphoreType.DMA,
            ],
        ),
        out_shape=[
            shape((D, span), bf16),
            shape((D, span - 2 * QT), bf16),
            shape((D, span), bf16),
            shape((D, span), bf16),
            shape((span, D), bf16),
            shape((span, D), bf16),
            shape((4, D, D), bf16),
        ],
        name="project",
        **kernel_params(11),
    )(member, x, vec, *pieces)


def project_weights(masks, member_ref, n_ref, dqt_ref, dk_ref, dv_ref, gwo_ref, *refs):
    outs, (sums_ref, gw, sem) = refs[:-3], refs[-3:]
    rows = dqt_ref.shape[1]
    halo = (n_ref.shape[1] - rows) // 2
    copies = []

    def send(c):
        if not masks:
            targets = [(gw.at[c], outs[0].at[c])]
        else:
            run = outs[0].shape[2]
            targets = []
            for far in (1, 0):
                for i, mask in enumerate(masks):
                    at = pl.multiple_of((member_ref[0] ^ (mask | far * CORE)) * run, 16)
                    targets.append((gw.at[c, pl.ds(at, run)], outs[far].at[i, c]))
        for source, target in targets:
            copy = pltpu.make_async_copy(source, target, sem.at[len(copies)])
            copy.start()
            copies.append(copy)

    gw[3] = gwo_ref[...]
    send(3)
    gw[0] = mm(n_ref[:, halo : halo + rows], dqt_ref[...], NT).astype(bf16)
    send(0)
    gw[1] = mm(n_ref[...], dk_ref[...]).astype(bf16)
    send(1)
    gw[2] = mm(n_ref[...], dv_ref[...]).astype(bf16)
    send(2)
    sums_ref[...] = row_sums([fold(dqt_ref[...].astype(f32))])
    sums_ref[1:2, :] = jnp.sum(dv_ref[...].astype(f32), axis=0, keepdims=True)
    for copy in copies:
        copy.wait()


def run_project_weights(normed, dqt, dk, dv, gwo, member, masks, run):
    D = normed.shape[0]
    shape = jax.ShapeDtypeStruct
    vmem, anywhere = pl.BlockSpec(memory_space=pltpu.VMEM), pl.BlockSpec(memory_space=pl.ANY)
    outs = [shape((len(masks), 4, run, D), bf16)] * 2 if masks else [shape((4, D, D), bf16)]
    return pl.pallas_call(
        functools.partial(project_weights, masks),
        in_specs=[pl.BlockSpec(memory_space=pltpu.SMEM)] + [vmem] * 5,
        out_specs=[anywhere] * len(outs) + [vmem],
        out_shape=outs + [shape((8, D), f32)],
        scratch_shapes=[pltpu.VMEM((4, D, D), bf16), pltpu.SemaphoreType.DMA((8 * max(1, len(masks)),))],
        name="project_weights",
        **kernel_params(8),
    )(member, normed, dqt, dk, dv, gwo)


def project_back(x_ref, dqt_ref, dk_ref, dv_ref, w_ref, mid_ref, vec_ref, grad_ref, rows_ref, sums_ref):
    i = pl.program_id(0)
    own = (i >= 1) & (i < pl.num_programs(0) - 1)

    @pl.when(i == 0)
    def _():
        sums_ref[...] = jnp.zeros_like(sums_ref)

    dqt = jnp.where(own, dqt_ref[...], jnp.zeros_like(dqt_ref))
    grad = mm(w_ref[1], dk_ref[...], NT) + mm(w_ref[2], dv_ref[...], NT) + mm(w_ref[0], dqt)
    xhat, scale = norm_parts(x_ref[...].astype(f32))
    sums_ref[0] += fold(grad * xhat)
    sums_ref[1] += fold(grad)
    grad_in = norm_back(grad, xhat, scale, vector(vec_ref, "gain_one"))
    grad_ref[...] = (grad_in + jnp.where(own, mid_ref[...], 0.0)).astype(bf16)

    @pl.when(i == pl.num_programs(0) - 1)
    def _():
        rows_ref[...] = row_sums([sums_ref[0], sums_ref[1]])


def run_project_back(x, dqt, dk, dv, w, grad_mid, vec):
    D, span = x.shape
    steps = span // QT
    cols = pl.BlockSpec((D, QT), lambda i: (0, i))
    rows = pl.BlockSpec((QT, D), lambda i: (i, 0))
    own = pl.BlockSpec((D, QT), lambda i: (0, jnp.clip(i - 1, 0, steps - 3)))
    shape = jax.ShapeDtypeStruct
    return pl.pallas_call(
        project_back,
        grid=(steps,),
        in_specs=[cols, own, rows, rows, whole((3, D, D)), own, whole((D, LANES), (0, VEC_BLOCK))],
        out_specs=[cols, whole((8, D))],
        out_shape=[shape((D, span), bf16), shape((8, D), f32)],
        scratch_shapes=[pltpu.VMEM((2, D, LANES), f32)],
        name="project_back",
        **kernel_params(10),
    )(x, dqt, dk, dv, w, grad_mid, vec)


def branch(att_ref, wo_ref, x_ref, vec_ref, mid_ref, n_ref):
    out = mm(wo_ref[0], att_ref[...]) + vector(vec_ref, "bias_out")
    middle = x_ref[...].astype(f32) + out
    mid_ref[...] = middle
    xhat, _ = norm_parts(middle)
    n_ref[...] = (xhat * vector(vec_ref, "gain_two") + vector(vec_ref, "shift_two")).astype(bf16)


def run_branch(att, w, x, vec):
    D, rows = att.shape
    cols = pl.BlockSpec((D, QT), lambda i: (0, i))
    return pl.pallas_call(
        branch,
        grid=(rows // QT,),
        in_specs=[
            cols,
            whole((1, D, D), (3, 0, 0)),
            pl.BlockSpec((D, QT), lambda i: (0, i + LONGEST // QT)),
            whole((D, LANES), (0, VEC_BLOCK)),
        ],
        out_specs=[cols, cols],
        out_shape=[jax.ShapeDtypeStruct((D, rows), f32), jax.ShapeDtypeStruct((D, rows), bf16)],
        name="branch",
        **kernel_params(5),
    )(att, w, x, vec)


def branch_back(
    gn_ref, got_ref, mid_ref, g_ref, att_ref, wo_ref, vec_ref,
    gmid_ref, gatt_ref, gwo_ref, rows_ref, wo, gwo_sum, sums_ref,
):
    i = pl.program_id(0)

    @pl.when(i == 0)
    def _():
        wo[...] = wo_ref[0].T
        gwo_sum[...] = jnp.zeros_like(gwo_sum)
        sums_ref[...] = jnp.zeros_like(sums_ref)

    grad = gn_ref[...] + got_ref[...].astype(f32)
    xhat, scale = norm_parts(mid_ref[...])
    g = g_ref[...].astype(f32)
    grad_mid = g + norm_back(grad, xhat, scale, vector(vec_ref, "gain_two"))
    gmid_ref[...] = grad_mid
    low = grad_mid.astype(bf16)
    gatt_ref[...] = mm(wo[...], low).astype(bf16)
    gwo_sum[...] += mm(low, att_ref[...], NT)
    sums_ref[0] += fold(low.astype(f32))
    sums_ref[1] += fold(grad * xhat)
    sums_ref[2] += fold(grad)
    sums_ref[3] += fold(g)

    @pl.when(i == pl.num_programs(0) - 1)
    def _():
        gwo_ref[...] = gwo_sum[...].astype(bf16)
        rows_ref[...] = row_sums([sums_ref[i] for i in range(4)])


def run_branch_back(gn, got, middle, g, att, w, vec):
    D, rows = att.shape
    cols = pl.BlockSpec((D, QT), lambda i: (0, i))
    shape = jax.ShapeDtypeStruct
    return pl.pallas_call(
        branch_back,
        grid=(rows // QT,),
        in_specs=[
            cols, cols, cols, cols, cols,
            whole((1, D, D), (3, 0, 0)),
            whole((D, LANES), (0, VEC_BLOCK)),
        ],
        out_specs=[cols, cols, whole((D, D)), whole((8, D))],
        out_shape=[
            shape((D, rows), f32),
            shape((D, rows), bf16),
            shape((D, D), bf16),
            shape((8, D), f32),
        ],
        scratch_shapes=[pltpu.VMEM((D, D), bf16), pltpu.VMEM((D, D), f32), pltpu.VMEM((4, D, LANES), f32)],
        name="branch_back",
        **kernel_params(9),
    )(gn, got, middle, g, att, w, vec)


def feed_forward(first, final, places, *refs):
    blocks, weights = len(places), 1 + max(p[0] for place in places for p in place)
    n2_in, g_in, refs = refs[0:2], refs[2:4], refs[4:]
    weights, refs = refs[:weights], refs[weights:]
    if not first:
        sums_in, refs = refs[:4], refs[4:]
    sums_out, refs = refs[:4], refs[4:]
    dw_out, refs = refs[: 2 * blocks], refs[2 * blocks :]
    dub_out, refs = refs[:blocks], refs[blocks:]
    n2, g, up, dt, ub, up_t, down, act, gh, dw, sums, low, in_sem, out_sem = refs
    D, F = up.shape
    f, rows = F // blocks, n2.shape[2]

    arrivals = {}

    def fetch(name, source, target):
        copy = pltpu.make_async_copy(source, target, in_sem.at[len(arrivals)])
        copy.start()
        arrivals[name] = copy

    def weight(name, target, b, part):
        ref, at = places[b][part]
        fetch((name, b), weights[ref].at[:, at : at + f], target.at[:, b * f : (b + 1) * f])

    for b in range(blocks):
        weight("up", up, b, 0)
    fetch("n2", n2_in[0], n2.at[0])
    for b in range(blocks):
        weight("dt", dt, b, 1)
        ref, at = places[b][2]
        fetch(("ub", b), weights[ref].at[at : at + 16], ub.at[b])
    fetch("g", g_in[0], g.at[0])
    fetch("n2 other", n2_in[1], n2.at[1])
    fetch("g other", g_in[1], g.at[1])
    if not first:
        for i in range(4):
            fetch(("sum", i), sums_in[i], low.at[i])

    departures = []

    def send(source, target):
        copy = pltpu.make_async_copy(source, target, out_sem.at[len(departures)])
        copy.start()
        departures.append(copy)

    columns = []
    for b in range(blocks):
        arrivals["up", b].wait()
        up_t[b * f : (b + 1) * f, :] = up[:, b * f : (b + 1) * f].T
    for b in range(blocks):
        arrivals["dt", b].wait()
        down[b * f : (b + 1) * f, :] = dt[:, b * f : (b + 1) * f].T
        arrivals["ub", b].wait()
        column = ub[b, :, :f].astype(f32).T[:, 0:1]
        columns.append(jnp.broadcast_to(column, (f, LANES)))
    bias = jnp.concatenate([jnp.concatenate(columns, axis=0)] * (QT // LANES), axis=1)
    arrivals["n2"].wait()
    arrivals["g"].wait()

    chunks = [(half, at) for half in range(2) for at in range(0, rows, QT)]

    def front(chunk):
        half, at = chunk
        if half == 1 and at == 0:
            arrivals["n2 other"].wait()
            arrivals["g other"].wait()
        return mm(up_t[...], n2[half, :, at : at + QT]), mm(down[...], g[half, :, at : at + QT])

    dub = jnp.zeros((F, LANES), f32)
    ready = front(chunks[0])
    for i, (half, at) in enumerate(chunks):
        following = front(chunks[i + 1]) if i + 1 < len(chunks) else None
        hidden, grad_act = ready
        hidden = hidden + bias
        cdf, pdf = normal_cdf(hidden)
        act[half, :, at : at + QT] = (hidden * cdf).astype(bf16)
        grad_hidden = (grad_act * (cdf + hidden * pdf)).astype(bf16)
        gh[half, :, at : at + QT] = grad_hidden
        dub = dub + fold(grad_hidden.astype(f32))
        ready = following
    for b in range(blocks):
        dub_out[b][...] = row_sums([dub[b * f : (b + 1) * f]])
    for part, (left, right) in enumerate(((n2, gh), (g, act))):
        dw[part] = (mm(left[0], right[0], NT) + mm(left[1], right[1], NT)).astype(bf16)
        for b in range(blocks):
            send(dw.at[part, :, b * f : (b + 1) * f], dw_out[2 * b + part])
    if not first:
        for i in range(4):
            arrivals["sum", i].wait()
    for i, (left, right) in enumerate(((up, gh), (dt, act))):
        for half in (1, 0):
            total = mm(left[...], right[half])
            k = 2 * i + half
            if not first:
                total = total + low[k].astype(f32)
            if half == 1 or not final:
                low[k] = total.astype(bf16)
                send(low.at[k], sums_out[k])
            else:
                sums[i] = total
                send(sums.at[i], sums_out[k])
    for copy in departures:
        copy.wait()


def run_feed_forward(n2, g, blocks, sums, final=False):
    D, rows = n2[0].shape
    F = D
    first = sums is None
    weights, places = [], []
    for block in blocks:
        place = []
        for array, column in block:
            found = [i for i, w in enumerate(weights) if w is array]
            if not found:
                weights.append(array)
            place.append((found[0] if found else len(weights) - 1, column))
        places.append(place)
    sums = () if first else tuple(sums)
    count = len(blocks)
    shape = jax.ShapeDtypeStruct
    anywhere = pl.BlockSpec(memory_space=pl.ANY)
    vmem = pl.BlockSpec(memory_space=pltpu.VMEM)
    own_type = f32 if final else bf16
    outs = pl.pallas_call(
        functools.partial(feed_forward, first, final, places),
        in_specs=[anywhere] * (4 + len(weights) + len(sums)),
        out_specs=[anywhere] * (4 + 2 * count) + [vmem] * count,
        out_shape=[shape((D, rows), t) for t in (own_type, bf16, own_type, bf16)]
        + [shape((D, F), bf16)] * (2 * count)
        + [shape((8, F), f32)] * count,
        scratch_shapes=[
            pltpu.VMEM((2, D, rows), bf16),
            pltpu.VMEM((2, D, rows), bf16),
            pltpu.VMEM((D, count * F), bf16),
            pltpu.VMEM((D, count * F), bf16),
            pltpu.VMEM((count, 16, D), bf16),
            pltpu.VMEM((count * F, D), bf16),
            pltpu.VMEM((count * F, D), bf16),
            pltpu.VMEM((2, count * F, rows), bf16),
            pltpu.VMEM((2, count * F, rows), bf16),
            pltpu.VMEM((2, D, count * F), bf16),
            pltpu.VMEM((2, D, rows), f32),
            pltpu.VMEM((4, D, rows), bf16),
            pltpu.SemaphoreType.DMA((3 * count + 8,)),
            pltpu.SemaphoreType.DMA((2 * count + 4,)),
        ],
        name="feed_forward",
        **kernel_params(14 * count),
    )(*n2, *g, *weights, *sums)
    grads = [(*outs[4 + 2 * b : 6 + 2 * b], outs[4 + 2 * count + b]) for b in range(count)]
    return outs[:4], grads


def z_rotate(x, k):
    n = lax.axis_size("narrow")
    return lax.ppermute(x, "narrow", [(i, (i + k) % n) for i in range(n)])


def z_gather(x):
    n, me = lax.axis_size("narrow"), lax.axis_index("narrow")
    stack = jnp.stack([x] + [z_rotate(x, k) for k in range(1, n)])
    return [lax.dynamic_index_in_dim(stack, lax.rem(me - j + n, n), 0, False) for j in range(n)]


def z_scatter_sum(pieces):
    n, me = lax.axis_size("narrow"), lax.axis_index("narrow")
    total = lax.dynamic_index_in_dim(pieces, me, 0, False).astype(f32)
    for k in range(1, n):
        piece = lax.dynamic_index_in_dim(pieces, lax.rem(me + k, n), 0, False)
        total = total + z_rotate(piece, k).astype(f32)
    return total


def swap(x, mask):
    n = lax.axis_size("wide")
    return lax.ppermute(x, "wide", [(i, i ^ mask) for i in range(n)])


def wide_sum(x):
    bit = 1
    while bit < lax.axis_size("wide"):
        x = x + swap(x, bit)
        bit *= 2
    return x


CORE, X, Y = 1, 2, 4


def after(deps, *values):
    n = len(values)
    tied = pl.pallas_call(
        lambda *refs: None,
        in_specs=[pl.BlockSpec(memory_space=pl.ANY)] * (n + len(deps)),
        out_specs=[pl.BlockSpec(memory_space=pl.ANY)] * n,
        out_shape=[jax.ShapeDtypeStruct(v.shape, v.dtype) for v in values],
        input_output_aliases={i: i for i in range(n)},
        name="tie",
    )(*values, *deps)
    return tied if n > 1 else tied[0]


def high_bits():
    bits, bit = [], 8
    while bit < lax.axis_size("wide"):
        bits.append(bit)
        bit *= 2
    return bits


def shards(
    tokens_in,
    ln1_gain,
    ln1_shift,
    w_qkv,
    qv_bias,
    w_out,
    out_bias,
    ln2_gain,
    ln2_shift,
    w_up,
    up_bias,
    w_down,
    down_bias,
    segment_ids,
    out_grad,
    predicted,
    labels,
):
    nn, me = lax.axis_size("narrow"), lax.axis_index("narrow")
    nw, mw = lax.axis_size("wide"), lax.axis_index("wide")
    part, tok = tokens_in.shape
    D = part * nn
    quarter = tok // nn
    halo = LONGEST
    span = quarter + 2 * halo
    high = high_bits()
    dw = w_qkv.shape[1]
    across = lambda x: lax.all_to_all(x, "narrow", 0, 0, tiled=True)

    position = jnp.arange(tok, dtype=jnp.int32)
    chunk = segment_ids * (tok // SEQ) + position // SEQ
    big = jnp.int32(2**30)
    chunk = jnp.concatenate([jnp.full((halo,), -1, jnp.int32), chunk, jnp.full((halo,), big, jnp.int32)])
    chunk = lax.dynamic_slice_in_dim(chunk, me * quarter, span, 0)
    chunk_own = chunk[halo : halo + quarter]
    tiles = quarter // QT
    edges = chunk_own.reshape(tiles, QT)
    low = jnp.sum((chunk[None] < edges[:, :1]).astype(jnp.int32), axis=1) // KT
    top = (jnp.sum((chunk[None] <= edges[:, -1:]).astype(jnp.int32), axis=1) + KT - 1) // KT
    small = (top - low <= 4).astype(jnp.int32)
    starts = jnp.minimum(low, span // KT - jnp.where(small == 1, 4, 6))
    segk = jnp.broadcast_to(chunk[:, None], (span, LANES))
    segq = jnp.broadcast_to(chunk_own[None], (8, quarter))

    piece = [w_qkv.reshape(3 * dw, part).T, w_out]
    piece += [jnp.zeros((part, VEC_BLOCK * LANES + VEC_AT - 4 * dw), bf16)]
    piece += [
        jnp.stack([ln1_gain, ln1_shift, qv_bias[0], qv_bias[1], out_bias, ln2_gain, ln2_shift, down_bias]).T
    ]
    piece = jnp.concatenate(piece, axis=1)
    piece = jnp.pad(piece, ((0, 0), (0, -piece.shape[1] % LANES)))
    vec = across(jnp.stack([piece] * nn)).reshape(D, -1)
    up_own = across(after((vec,), jnp.stack([w_up] * nn))).reshape(D, -1)
    units = up_bias.shape[0]
    bias_rows = jnp.pad(up_bias[None], ((0, 15), (0, D - units)))
    attn_own = after((vec,), jnp.concatenate([vec[:, : 4 * dw].T, bias_rows], axis=0))
    count, height = 1, 4 * dw + 16
    for bit in high:
        attn_own = jnp.concatenate([attn_own, swap(attn_own, bit)], axis=0)
        count *= 2
    cut = attn_own.shape[0] // 2 // 16 * 16
    from_x, from_y = swap(attn_own, X), swap(attn_own, Y)
    from_xy = swap(from_y[:cut], X), swap(from_x[cut:], Y)
    grad_blocks = jnp.stack([out_grad[:, j * quarter : (j + 1) * quarter] for j in range(nn)])
    padded = jnp.pad(tokens_in, ((0, 0), (halo, halo)))
    blocks = jnp.stack([padded[:, j * quarter : j * quarter + span] for j in range(nn)])
    blocks = after((starts, small, segk, segq, up_own, *from_xy, grad_blocks), blocks)
    x_low = across(blocks).reshape(D, span)
    dt_blocks = after((x_low,), jnp.stack([w_down.T] * nn))
    dt_own = across(dt_blocks).reshape(D, -1)
    bias_of = lambda a: jnp.concatenate(
        [a[j * height + 4 * dw : (j + 1) * height, :units] for j in range(count)], axis=1
    )
    if dw % 16 == 0:
        pieces = [attn_own, from_x, from_y, *from_xy]
        pieces += [swap(piece, CORE) for piece in pieces]
        parts = []
        for far in (0, 1):
            for i, mask in enumerate((0, X, Y)):
                parts += [(i + 5 * far, c * dw, dw, c, mask | far * CORE) for c in range(4)]
            for c in range(4):
                for first, last in ((c * dw, min((c + 1) * dw, cut)), (max(c * dw, cut), (c + 1) * dw)):
                    assert last <= first or last - first == dw
                    if last > first:
                        piece, start = (3, first) if last <= cut else (4, first - cut)
                        parts.append((piece + 5 * far, start, dw, c, (X | Y) | far * CORE))
        ub_own, ub_x, ub_y = (attn_own, 4 * dw), (from_x, 4 * dw), (from_y, 4 * dw)
        ub_xy = from_xy[1], 4 * dw - cut
    else:
        from_xy = jnp.concatenate(from_xy, axis=0)
        ub_own, ub_x, ub_y, ub_xy = ((bias_of(a), 0) for a in (attn_own, from_x, from_y, from_xy))
        half = jnp.concatenate([attn_own, from_x, from_y, from_xy], axis=0)
        half = half.reshape(-1, height, D)[:, : 4 * dw].reshape(-1, 4, dw, D)
        every = jnp.concatenate([half, swap(half, CORE)], axis=0)
        bits = high + [X, Y, CORE]
        place = lambda m: sum(((m // bit) % 2) << i for i, bit in enumerate(bits))
        every = [lax.dynamic_index_in_dim(every, place(mw ^ w), 0, True) for w in range(nw)]
        pieces = [jnp.concatenate(every, axis=0).transpose(1, 0, 2, 3).reshape(4 * D, D)]
        parts = [(0, c * D, D, c, 0) for c in range(4)]
    member = jnp.reshape(mw if dw % 16 == 0 else mw * 0, (1,)).astype(jnp.int32)

    for bit in high:
        up_own = jnp.concatenate([up_own, swap(up_own, bit)], axis=1)
    F = up_own.shape[1]
    up_x, up_y = swap(up_own, X), swap(up_own, Y)
    x_low = after((up_x, up_y), x_low)
    normed, qt, kt, vt, k, v, w_attn = run_project(x_low, vec, member, pieces, parts)
    groups = D // LANES
    forward_in = starts, small, qt, k, vt, segk, segq
    att, lse = run_forward(*forward_in, (0, 1))

    dt_own = after((att,), dt_own)
    grad_cols = across(after((dt_own,), grad_blocks)).reshape(D, quarter)
    for bit in high:
        dt_own = jnp.concatenate([dt_own, swap(dt_own, bit)], axis=1)
    dt_x, dt_y = swap(dt_own, X), swap(dt_own, Y)
    up_xy = swap(up_y, X)
    att = after((up_xy,), att)
    att, lse = run_forward(*forward_in, (1, 3), (att, lse))
    dt_x = after((att,), dt_x)
    dt_xy = swap(dt_x, Y)
    att, lse = run_forward(*forward_in, (3, groups), (att, lse))
    grad_cols = after((att,), grad_cols)
    grad_pair = grad_cols, swap(grad_cols, CORE)
    middle, normed_two = run_branch(att, w_attn, x_low, vec)

    normed_two = after((dt_xy,), normed_two)
    n2_pair = normed_two, swap(normed_two, CORE)
    blocks = [((up_xy, 0), (dt_xy, 0), ub_xy), ((up_x, 0), (dt_x, 0), ub_x)]
    sums, ((up_gxy, dt_gxy, ub_gxy), (up_gx, dt_gx, ub_gx)) = run_feed_forward(n2_pair, grad_pair, blocks, None)
    up_got_xy, dt_got_xy = swap(up_gxy, X), swap(dt_gxy, Y)
    up_got_x = swap(up_gx, X)
    blocks = [((up_y, 0), (dt_y, 0), ub_y)]
    sums, ((up_gy, dt_gy, ub_gy),) = run_feed_forward(n2_pair, grad_pair, blocks, sums)
    add = lambda *terms: sum(t.astype(f32) for t in terms)
    dt_got_y = swap(dt_gy, Y)
    up_gy, dt_gx = add(up_gy, up_got_xy).astype(bf16), add(dt_gx, dt_got_xy).astype(bf16)
    up_got_y, dt_got_x = swap(up_gy, Y), swap(dt_gx, X)
    sums = after((up_gy, dt_gx), *sums)
    blocks = [((up_own, 0), (dt_own, 0), ub_own)]
    sums, ((up_g, dt_g, ub_g),) = run_feed_forward(n2_pair, grad_pair, blocks, sums, True)
    gn_sum, gn_other, out_sum, out_other = sums
    gn_got, out_got = swap(gn_other, CORE), swap(out_other, CORE)

    layer = (middle + (out_sum + out_got.astype(f32) + vec[:, VEC_LAST : VEC_LAST + 1].astype(f32))).astype(bf16)
    layer_out = across(layer.reshape(nn, part, quarter)).transpose(1, 0, 2).reshape(part, tok)

    gn_got = after((layer,), gn_got)
    grad_mid, grad_att, grad_wo_t, sums_two = run_branch_back(
        gn_sum, gn_got, middle, grad_cols, att, w_attn, vec
    )
    back_in = starts, small, qt, kt, k, v, grad_att, att, lse, segk, segq
    back_a = run_backward(*back_in, (0, 2))
    up_got_x, up_got_y, dt_got_x, dt_got_y = after((back_a[0],), up_got_x, up_got_y, dt_got_x, dt_got_y)
    up_g, dt_g = add(up_g, up_got_x, up_got_y), add(dt_g, dt_got_x, dt_got_y)
    for bit in reversed(high):
        half = up_g.shape[1] // 2
        up_g = up_g[:, :half] + swap(up_g[:, half:].astype(bf16), bit).astype(f32)
        dt_g = dt_g[:, :half] + swap(dt_g[:, half:].astype(bf16), bit).astype(f32)
    ud_g = jnp.concatenate([up_g, dt_g], axis=1).astype(bf16)
    ud_grad = z_scatter_sum(ud_g.reshape(nn, part, -1))
    dqt_a = after((ud_g, layer_out), back_a[0])
    dqt, dk, dv = run_backward(*back_in, (2, groups), (dqt_a, *back_a[1:]))
    masks = [0]
    for bit in high:
        masks = masks + [m ^ bit for m in masks]
    masks = [m ^ b for b in (0, X, Y, X | Y) for m in masks]
    direct = masks if dw % 16 == 0 else []
    *grad_w, qv_rows = run_project_weights(normed, dqt, dk, dv, grad_wo_t, member, direct, dw)
    if not direct:
        grad_w = grad_w[0].reshape(4, nw, dw, D).transpose(1, 0, 2, 3)
        pick = lambda masks: jnp.concatenate(
            [lax.dynamic_index_in_dim(grad_w, mw ^ m, 0, True) for m in masks], axis=0
        )
        grad_w = pick(masks), pick([m ^ CORE for m in masks])
    attn_g, got = grad_w[0], swap(grad_w[1], CORE)
    dqt = after((grad_w[1],), dqt)
    grad_in, sums_one = run_project_back(x_low, dqt, dk, dv, w_attn, grad_mid, vec)
    got = after((grad_in,), got)
    vector_rows = jnp.concatenate([sums_one[:2], qv_rows[:2], sums_two[:4]])
    up_grad, down_grad = ud_grad[:, :units], ud_grad[:, units:].T
    grad_in = across(grad_in.reshape(nn, part, span)).astype(f32)
    tokens_grad = sum(
        jnp.pad(grad_in[j], ((0, 0), (j * quarter, tok - (j + 1) * quarter))) for j in range(nn)
    )[:, halo : halo + tok]

    half = add(attn_g, got).astype(bf16)
    g0, gx, gy, gxy = (half[i * count : (i + 1) * count] for i in range(4))
    gy_low = add(gy[:, :2], swap(gxy[:, :2], X)).astype(bf16)
    gx_high = add(gx[:, 2:], swap(gxy[:, 2:], Y)).astype(bf16)
    gx = jnp.concatenate([gx[:, :2], gx_high], axis=1)
    gy = jnp.concatenate([gy_low, gy[:, 2:]], axis=1)
    ub_g, ub_gx, ub_gy, ub_gxy = (rows[0] for rows in after((gx, gy), ub_g, ub_gx, ub_gy, ub_gxy))
    ub_g = ub_g + swap(ub_gx, X) + swap(ub_gy, Y) + swap(ub_gxy, X | Y)
    for bit in reversed(high):
        cut = ub_g.shape[0] // 2
        ub_g = ub_g[:cut] + swap(ub_g[cut:], bit)
    ub_g = jnp.pad(ub_g[None], ((0, 0), (0, D - units)))
    vector_rows = after((gx, gy), vector_rows)
    g0 = add(g0, swap(gx, X), swap(gy, Y))
    for bit in reversed(high):
        cut = g0.shape[0] // 2
        g0 = g0[:cut] + swap(g0[cut:].astype(bf16), bit).astype(f32)
    g0 = g0[0].astype(bf16).reshape(4 * dw, D).T.reshape(nn, part, 4 * dw)
    attn_grad = z_scatter_sum(g0)
    qkv_grad = attn_grad[:, : 3 * dw].T.reshape(3, dw, part)
    out_weight_grad = attn_grad[:, 3 * dw :]

    class_ids = jnp.arange(CLASSES, dtype=jnp.int32)
    label_hits = labels[:, None] == class_ids
    counts = jnp.stack(
        [
            jnp.sum(((predicted[:, None] == class_ids) & label_hits).astype(f32), axis=0),
            jnp.sum(label_hits.astype(f32), axis=0),
        ]
    )
    counts = jnp.pad(counts.reshape(1, -1), ((0, 0), (0, D - counts.size)))
    sums = wide_sum(jnp.concatenate([vector_rows, counts]))
    counts = sums[8, : 2 * CLASSES].reshape(2, CLASSES)
    sums = after((g0,), jnp.concatenate([sums[:8], ub_g]))
    sums = sums + sum(z_rotate(sums, r) for r in range(1, nn))
    ub_g = sums[8, :units]
    sums = lax.dynamic_slice_in_dim(sums[:8], me * part, part, 1)
    gain_one_g, shift_one_g, q_bias_g, v_bias_g, out_bias_g, gain_two_g, shift_two_g, down_bias_g = sums
    tallies = counts.astype(jnp.int32)
    accuracy = jnp.sum(counts[0]) / jnp.maximum(jnp.sum(counts[1]), 1.0)
    return (
        layer_out,
        tokens_grad,
        gain_one_g,
        shift_one_g,
        qkv_grad,
        jnp.stack([q_bias_g, v_bias_g]),
        out_weight_grad,
        out_bias_g,
        gain_two_g,
        shift_two_g,
        up_grad,
        ub_g,
        down_grad,
        down_bias_g,
        tallies,
        accuracy,
    )


def solution(mesh):
    return jax.shard_map(
        shards,
        mesh=mesh,
        in_specs=(
            P("narrow", "wide"),
            P("narrow"),
            P("narrow"),
            P(None, "wide", "narrow"),
            P(None, "narrow"),
            P("narrow", "wide"),
            P("narrow"),
            P("narrow"),
            P("narrow"),
            P("narrow", "wide"),
            P("wide"),
            P("wide", "narrow"),
            P("narrow"),
            P("wide"),
            P("narrow", "wide"),
            P("wide"),
            P("wide"),
        ),
        out_specs=(
            P("narrow", "wide"),
            P("narrow", "wide"),
            P("narrow"),
            P("narrow"),
            P(None, "wide", "narrow"),
            P(None, "narrow"),
            P("narrow", "wide"),
            P("narrow"),
            P("narrow"),
            P("narrow"),
            P("narrow", "wide"),
            P("wide"),
            P("wide", "narrow"),
            P("narrow"),
            P(),
            P(),
        ),
        check_vma=False,
    )
```

```python
import functools

import jax
import jax.numpy as jnp
from jax import lax
from jax.experimental import pallas as pl
from jax.experimental.pallas import tpu as pltpu
from jax.sharding import PartitionSpec as P

HEAD_DIM = 32
SEQ = 1024
CLASSES = 4
LONGEST = 256
EPS = 1e-05
QT = 256
KT = 128
GROUP = 4
LANES = 128
LOG2E = 1.4426950408889634
SCALE = HEAD_DIM**-0.5
MASKED = -1e30
VMEM_LIMIT = 58 * 1024 * 1024
VEC_BLOCK, VEC_AT = 2, 64
VEC_LAST = VEC_BLOCK * 128 + VEC_AT + 7
bf16, f32 = jnp.bfloat16, jnp.float32

NN = (((1,), (0,)), ((), ()))
NT = (((1,), (1,)), ((), ()))
TN = (((0,), (0,)), ((), ()))

PHI_P = 0.33
PHI_C = (
    0.1328227541618569,
    0.117797452145417,
    0.18652846971894854,
    -0.09893620415601319,
    0.3406397450924515,
    -0.22542553879715763,
    0.046573313873415075,
)


def mm(left, right, dims=NN):
    return lax.dot_general(left, right, dims, preferred_element_type=f32)


def normal_cdf(u):
    bell = jnp.exp(-0.5 * (u * u))
    t = 1.0 / (1.0 + PHI_P * jnp.abs(u))
    tail = jnp.full_like(t, PHI_C[-1])
    for c in PHI_C[-2::-1]:
        tail = tail * t + c
    tail = tail * t * bell
    return jnp.where(u >= 0, 1.0 - tail, tail), bell * 0.3989422804014327


def head_only(block, h, axis):
    index = lax.broadcasted_iota(jnp.int32, block.shape, axis)
    keep = (index >= h * HEAD_DIM) & (index < (h + 1) * HEAD_DIM)
    return jnp.where(keep, block, jnp.zeros_like(block))


def key_bias(segk_ref, segq_ref, start, window):
    segk = segk_ref[pl.ds(start, window), :]
    segk = jnp.concatenate([segk] * (QT // LANES), axis=1)
    return jnp.where(segk == segq_ref[0:1, :], 0.0, MASKED).astype(f32)


def attend_forward(start_ref, small_ref, q_ref, k_ref, vt_ref, segk_ref, segq_ref, *refs):
    att_ref, lse_ref = refs[-2:]
    tile = pl.program_id(1)

    def run(window):
        start = pl.multiple_of(start_ref[tile] * KT, KT)
        keys = k_ref[pl.ds(start, window), :]
        bias = key_bias(segk_ref, segq_ref, start, window)
        q = q_ref[...]
        rows = [slice(h * HEAD_DIM, (h + 1) * HEAD_DIM) for h in range(GROUP)]
        scores = [mm(keys, head_only(q, h, 0)) for h in range(GROUP)]
        ready = []
        for h in range(GROUP):
            masked = scores[h] + bias
            top = jnp.max(masked, axis=0, keepdims=True)
            probs = jnp.exp2((masked - top) * (SCALE * LOG2E))
            total = jnp.sum(probs, axis=0, keepdims=True)
            lse_ref[h : h + 1, :] = top * (SCALE * LOG2E) + jnp.log2(total)
            ready.append((probs.astype(bf16), total))
        for h, (probs, total) in enumerate(ready):
            out = mm(vt_ref[rows[h], pl.ds(start, window)], probs)
            att_ref[rows[h], :] = (out / total).astype(bf16)

    @pl.when(small_ref[tile] == 1)
    def _():
        run(4 * KT)

    @pl.when(small_ref[tile] == 0)
    def _():
        run(6 * KT)


def attend_backward(
    start_ref, small_ref, qt_ref, kt_ref, k_ref, v_ref, dot_ref, att_ref, lse_ref, segk_ref, segq_ref, *refs
):
    dqt_ref, dk_ref, dv_ref, dk_sum, dv_sum = refs[-5:]
    tile = pl.program_id(1)

    @pl.when(tile == 0)
    def _():
        dk_sum[...] = jnp.zeros_like(dk_sum)
        dv_sum[...] = jnp.zeros_like(dv_sum)

    def run(window):
        start = pl.multiple_of(start_ref[tile] * KT, KT)
        at = pl.ds(start, window)
        keys, values = k_ref[at, :], v_ref[at, :]
        bias = key_bias(segk_ref, segq_ref, start, window)
        qt, dot = qt_ref[...], dot_ref[...]
        q, do = qt.T, dot.T
        inner = dot.astype(f32) * att_ref[...].astype(f32)
        rows = [slice(h * HEAD_DIM, (h + 1) * HEAD_DIM) for h in range(GROUP)]
        products = [(mm(keys, head_only(qt, h, 0)), mm(values, head_only(dot, h, 0))) for h in range(GROUP)]
        probs_low, grads_low = [], []
        for h, (scores, grad_probs) in enumerate(products):
            delta = jnp.sum(inner[rows[h], :], axis=0, keepdims=True)
            probs = jnp.exp2((scores * (SCALE * LOG2E) - lse_ref[h : h + 1, :]) + bias)
            probs_low.append(probs.astype(bf16))
            grads_low.append((probs * (grad_probs - delta)).astype(bf16))
        heads_of = lambda block: jnp.concatenate([head_only(block, h, 1) for h in range(GROUP)], axis=0)
        dv = mm(jnp.concatenate(probs_low, axis=1), heads_of(do))
        dk = mm(jnp.concatenate(grads_low, axis=1), heads_of(q))
        for h in range(GROUP):
            dq = mm(kt_ref[rows[h], at], grads_low[h])
            dqt_ref[rows[h], :] = (dq * SCALE).astype(bf16)
        dk_sum[at, :] += dk
        dv_sum[at, :] += dv

    @pl.when(small_ref[tile] == 1)
    def _():
        run(4 * KT)

    @pl.when(small_ref[tile] == 0)
    def _():
        run(6 * KT)

    @pl.when(tile == pl.num_programs(1) - 1)
    def _():
        dk_ref[...] = (dk_sum[...] * SCALE).astype(bf16)
        dv_ref[...] = dv_sum[...].astype(bf16)


def attention_specs(span, begin):
    spec = pl.BlockSpec
    return {
        "q_cols": spec((LANES, QT), lambda g, j, *_: (g + begin, j)),
        "k_cols": spec((LANES, span), lambda g, j, *_: (g + begin, 0)),
        "k_rows": spec((span, LANES), lambda g, j, *_: (0, g + begin)),
        "lse": spec((8, QT), lambda g, j, *_: (g + begin, j)),
        "segk": spec((span, LANES), lambda g, j, *_: (0, 0)),
        "segq": spec((8, QT), lambda g, j, *_: (0, j)),
    }


def run_forward(starts, small, qt, k, vt, segk, segq, span_of_groups, outs=(), first=()):
    D, rows = qt.shape
    span = k.shape[0]
    begin, end = span_of_groups
    s = attention_specs(span, begin)
    groups = D // LANES
    outs = tuple(outs)
    return pl.pallas_call(
        attend_forward,
        grid_spec=pltpu.PrefetchScalarGridSpec(
            num_scalar_prefetch=2,
            grid=(end - begin, rows // QT),
            in_specs=[s["q_cols"], s["k_rows"], s["k_cols"], s["segk"], s["segq"]]
            + [pl.BlockSpec(memory_space=pl.ANY)] * (len(outs) + len(first)),
            out_specs=[s["q_cols"], s["lse"]],
        ),
        input_output_aliases={7: 0, 8: 1} if outs else {},
        out_shape=[
            jax.ShapeDtypeStruct((D, rows), bf16),
            jax.ShapeDtypeStruct((groups * 8, rows), f32),
        ],
        name="attend_forward",
        **kernel_params(4 * (end - begin)),
    )(starts, small, qt, k, vt, segk, segq, *outs, *first)


def run_backward(starts, small, qt, kt, k, v, dot, att, lse, segk, segq, span_of_groups, outs=(), first=()):
    D, rows = qt.shape
    span = k.shape[0]
    begin, end = span_of_groups
    s = attention_specs(span, begin)
    outs = tuple(outs)
    return pl.pallas_call(
        attend_backward,
        grid_spec=pltpu.PrefetchScalarGridSpec(
            num_scalar_prefetch=2,
            grid=(end - begin, rows // QT),
            in_specs=[
                s["q_cols"], s["k_cols"], s["k_rows"], s["k_rows"], s["q_cols"], s["q_cols"],
                s["lse"], s["segk"], s["segq"],
            ]
            + [pl.BlockSpec(memory_space=pl.ANY)] * (len(outs) + len(first)),
            out_specs=[s["q_cols"], s["k_rows"], s["k_rows"]],
            scratch_shapes=[pltpu.VMEM((span, LANES), f32), pltpu.VMEM((span, LANES), f32)],
        ),
        out_shape=[
            jax.ShapeDtypeStruct((D, rows), bf16),
            jax.ShapeDtypeStruct((span, D), bf16),
            jax.ShapeDtypeStruct((span, D), bf16),
        ],
        input_output_aliases={11: 0, 12: 1, 13: 2} if outs else {},
        name="attend_backward",
        **kernel_params(6 * (end - begin)),
    )(starts, small, qt, kt, k, v, dot, att, lse, segk, segq, *outs, *first)


def norm_parts(cols):
    centre = jnp.mean(cols, axis=0, keepdims=True)
    shifted = cols - centre
    spread = jnp.mean(jnp.square(shifted), axis=0, keepdims=True)
    scale = lax.rsqrt(spread + EPS)
    return shifted * scale, scale


def norm_back(grad, xhat, scale, gain):
    e = grad * gain
    mean_e = jnp.mean(e, axis=0, keepdims=True)
    mean_ex = jnp.mean(e * xhat, axis=0, keepdims=True)
    return scale * (e - mean_e - xhat * mean_ex)


VECTORS = ("gain_one", "shift_one", "q_bias", "v_bias", "bias_out", "gain_two", "shift_two", "bias_down")


def vector(vec_ref, name):
    i = VEC_AT + VECTORS.index(name)
    return vec_ref[:, i : i + 1].astype(f32)


def fold(x):
    return sum(x[:, i : i + LANES] for i in range(0, x.shape[1], LANES))


def row_sums(parts):
    rows = [jnp.sum(part.T, axis=0, keepdims=True) for part in parts]
    return jnp.concatenate(rows + [jnp.zeros((8 - len(rows), rows[0].shape[1]), f32)], axis=0)


def whole(shape, block=None):
    return pl.BlockSpec(shape, lambda *_: (0,) * len(shape) if block is None else block)


def kernel_params(micros):
    return {
        "compiler_params": pltpu.CompilerParams(vmem_limit_bytes=VMEM_LIMIT),
        "cost_estimate": pl.CostEstimate(flops=micros * 10**9, bytes_accessed=10**6, transcendentals=0),
    }


def pack(qkv_ref, out_ref, *refs):
    vectors, (piece_ref, rows, turned) = refs[:-3], refs[-3:]
    part, dw = out_ref.shape
    rows[...] = jnp.zeros_like(rows)
    turned[...] = jnp.zeros_like(turned)
    turned[:part, :dw] = out_ref[...].astype(f32)
    for c in range(3):
        rows[c * dw : (c + 1) * dw, :part] = qkv_ref[c].astype(f32)
    rows[3 * dw : 4 * dw, :] = turned[...].T[:dw, :]
    at = VEC_BLOCK * LANES + VEC_AT
    for ref in vectors:
        count = ref.shape[0] if len(ref.shape) == 2 else 1
        rows[at : at + count, :part] = ref[...].reshape(count, part).astype(f32)
        at += count
    piece = rows[...].T[:part, :].astype(bf16)
    for n in range(piece_ref.shape[0]):
        piece_ref[n] = piece


def run_pack(w_qkv, w_out, vectors, members):
    part = w_out.shape[0]
    height, wide = (VEC_BLOCK + 1) * LANES, -(-part // LANES) * LANES
    return pl.pallas_call(
        pack,
        out_shape=jax.ShapeDtypeStruct((members, part, height), bf16),
        scratch_shapes=[pltpu.VMEM((height, wide), f32), pltpu.VMEM((wide, LANES), f32)],
        name="pack",
        **kernel_params(2),
    )(w_qkv, w_out, *vectors)


def project(parts, count, member_ref, x_ref, vec_ref, *refs):
    pieces, refs = refs[:count], refs[-11:]
    n_ref, qt_ref, kt_ref, vt_ref, k_ref, v_ref, w_ref, w, wt, in_sem, out_sem = refs
    i = pl.program_id(0)
    out = pltpu.make_async_copy(w, w_ref, out_sem)

    @pl.when(i == 0)
    def _():
        copies = []
        for piece, first, rows, c, mask in parts:
            at = pl.multiple_of((member_ref[0] ^ mask) * rows, 16)
            copy = pltpu.make_async_copy(
                pieces[piece].at[first : first + rows], w.at[c, pl.ds(at, rows)], in_sem.at[len(copies)]
            )
            copy.start()
            copies.append(copy)
        for copy in copies:
            copy.wait()
        out.start()
        for c in range(3):
            wt[c] = w[c].T

    xhat, _ = norm_parts(x_ref[...].astype(f32))
    normed = (xhat * vector(vec_ref, "gain_one") + vector(vec_ref, "shift_one")).astype(bf16)
    n_ref[...] = normed
    kt = mm(wt[1], normed).astype(bf16)
    vt = (mm(wt[2], normed) + vector(vec_ref, "v_bias")).astype(bf16)
    kt_ref[...], vt_ref[...] = kt, vt
    k_ref[...], v_ref[...] = kt.T, vt.T

    @pl.when((i >= 1) & (i < pl.num_programs(0) - 1))
    def _():
        qt_ref[...] = (mm(wt[0], normed) + vector(vec_ref, "q_bias")).astype(bf16)

    @pl.when(i == pl.num_programs(0) - 1)
    def _():
        out.wait()


def run_project(x, vec, member, pieces, parts, first):
    D, span = x.shape
    steps = span // QT
    cols = pl.BlockSpec((D, QT), lambda i, _: (0, i))
    rows = pl.BlockSpec((QT, D), lambda i, _: (i, 0))
    own = pl.BlockSpec((D, QT), lambda i, _: (0, jnp.clip(i - 1, 0, steps - 3)))
    anywhere = pl.BlockSpec(memory_space=pl.ANY)
    shape = jax.ShapeDtypeStruct
    return pl.pallas_call(
        functools.partial(project, parts, len(pieces)),
        grid_spec=pltpu.PrefetchScalarGridSpec(
            num_scalar_prefetch=1,
            grid=(steps,),
            in_specs=[cols, whole((D, LANES), (0, VEC_BLOCK))] + [anywhere] * (len(pieces) + len(first)),
            out_specs=[cols, own, cols, cols, rows, rows, anywhere],
            scratch_shapes=[
                pltpu.VMEM((4, D, D), bf16),
                pltpu.VMEM((3, D, D), bf16),
                pltpu.SemaphoreType.DMA((len(parts),)),
                pltpu.SemaphoreType.DMA,
            ],
        ),
        out_shape=[
            shape((D, span), bf16),
            shape((D, span - 2 * QT), bf16),
            shape((D, span), bf16),
            shape((D, span), bf16),
            shape((span, D), bf16),
            shape((span, D), bf16),
            shape((4, D, D), bf16),
        ],
        name="project",
        **kernel_params(11),
    )(member, x, vec, *pieces, *first)


def project_weights(masks, member_ref, n_ref, dqt_ref, dk_ref, dv_ref, gwo_ref, *refs):
    outs, (sums_ref, gw, sem) = refs[:-3], refs[-3:]
    rows = dqt_ref.shape[1]
    halo = (n_ref.shape[1] - rows) // 2
    copies = []

    def send(c):
        if not masks:
            targets = [(gw.at[c], outs[0].at[c])]
        else:
            run = outs[0].shape[2]
            targets = []
            for far in (1, 0):
                for i, mask in enumerate(masks):
                    at = pl.multiple_of((member_ref[0] ^ (mask | far * CORE)) * run, 16)
                    targets.append((gw.at[c, pl.ds(at, run)], outs[far].at[i, c]))
        for source, target in targets:
            copy = pltpu.make_async_copy(source, target, sem.at[len(copies)])
            copy.start()
            copies.append(copy)

    gw[3] = gwo_ref[...]
    send(3)
    gw[0] = mm(n_ref[:, halo : halo + rows], dqt_ref[...], NT).astype(bf16)
    send(0)
    gw[1] = mm(n_ref[...], dk_ref[...]).astype(bf16)
    send(1)
    gw[2] = mm(n_ref[...], dv_ref[...]).astype(bf16)
    send(2)
    sums_ref[...] = row_sums([fold(dqt_ref[...].astype(f32))])
    sums_ref[1:2, :] = jnp.sum(dv_ref[...].astype(f32), axis=0, keepdims=True)
    for copy in copies:
        copy.wait()


def run_project_weights(normed, dqt, dk, dv, gwo, member, masks, run):
    D = normed.shape[0]
    shape = jax.ShapeDtypeStruct
    vmem, anywhere = pl.BlockSpec(memory_space=pltpu.VMEM), pl.BlockSpec(memory_space=pl.ANY)
    outs = [shape((len(masks), 4, run, D), bf16)] * 2 if masks else [shape((4, D, D), bf16)]
    return pl.pallas_call(
        functools.partial(project_weights, masks),
        in_specs=[pl.BlockSpec(memory_space=pltpu.SMEM)] + [vmem] * 5,
        out_specs=[anywhere] * len(outs) + [vmem],
        out_shape=outs + [shape((8, D), f32)],
        scratch_shapes=[pltpu.VMEM((4, D, D), bf16), pltpu.SemaphoreType.DMA((8 * max(1, len(masks)),))],
        name="project_weights",
        **kernel_params(8),
    )(member, normed, dqt, dk, dv, gwo)


def project_back(x_ref, dqt_ref, dk_ref, dv_ref, w_ref, mid_ref, vec_ref, *refs):
    grad_ref, rows_ref, sums_ref = refs[-3:]
    i = pl.program_id(0)
    own = (i >= 1) & (i < pl.num_programs(0) - 1)

    @pl.when(i == 0)
    def _():
        sums_ref[...] = jnp.zeros_like(sums_ref)

    dqt = jnp.where(own, dqt_ref[...], jnp.zeros_like(dqt_ref))
    grad = mm(w_ref[1], dk_ref[...], NT) + mm(w_ref[2], dv_ref[...], NT) + mm(w_ref[0], dqt)
    xhat, scale = norm_parts(x_ref[...].astype(f32))
    sums_ref[0] += fold(grad * xhat)
    sums_ref[1] += fold(grad)
    grad_in = norm_back(grad, xhat, scale, vector(vec_ref, "gain_one"))
    grad_ref[...] = (grad_in + jnp.where(own, mid_ref[...], 0.0)).astype(bf16)

    @pl.when(i == pl.num_programs(0) - 1)
    def _():
        rows_ref[...] = row_sums([sums_ref[0], sums_ref[1]])


def run_project_back(x, dqt, dk, dv, w, grad_mid, vec, first):
    D, span = x.shape
    steps = span // QT
    cols = pl.BlockSpec((D, QT), lambda i: (0, i))
    rows = pl.BlockSpec((QT, D), lambda i: (i, 0))
    own = pl.BlockSpec((D, QT), lambda i: (0, jnp.clip(i - 1, 0, steps - 3)))
    shape = jax.ShapeDtypeStruct
    return pl.pallas_call(
        project_back,
        grid=(steps,),
        in_specs=[cols, own, rows, rows, whole((3, D, D)), own, whole((D, LANES), (0, VEC_BLOCK))]
        + [pl.BlockSpec(memory_space=pl.ANY)] * len(first),
        out_specs=[cols, whole((8, D))],
        out_shape=[shape((D, span), bf16), shape((8, D), f32)],
        scratch_shapes=[pltpu.VMEM((2, D, LANES), f32)],
        name="project_back",
        **kernel_params(10),
    )(x, dqt, dk, dv, w, grad_mid, vec, *first)


def branch(att_ref, wo_ref, x_ref, vec_ref, mid_ref, n_ref):
    out = mm(wo_ref[0], att_ref[...]) + vector(vec_ref, "bias_out")
    middle = x_ref[...].astype(f32) + out
    mid_ref[...] = middle
    xhat, _ = norm_parts(middle)
    n_ref[...] = (xhat * vector(vec_ref, "gain_two") + vector(vec_ref, "shift_two")).astype(bf16)


def run_branch(att, w, x, vec):
    D, rows = att.shape
    cols = pl.BlockSpec((D, QT), lambda i: (0, i))
    return pl.pallas_call(
        branch,
        grid=(rows // QT,),
        in_specs=[
            cols,
            whole((1, D, D), (3, 0, 0)),
            pl.BlockSpec((D, QT), lambda i: (0, i + LONGEST // QT)),
            whole((D, LANES), (0, VEC_BLOCK)),
        ],
        out_specs=[cols, cols],
        out_shape=[jax.ShapeDtypeStruct((D, rows), f32), jax.ShapeDtypeStruct((D, rows), bf16)],
        name="branch",
        **kernel_params(5),
    )(att, w, x, vec)


def branch_back(
    gn_ref, got_ref, mid_ref, g_ref, att_ref, wo_ref, vec_ref,
    gmid_ref, gatt_ref, gwo_ref, rows_ref, wo, gwo_sum, sums_ref,
):
    i = pl.program_id(0)

    @pl.when(i == 0)
    def _():
        wo[...] = wo_ref[0].T
        gwo_sum[...] = jnp.zeros_like(gwo_sum)
        sums_ref[...] = jnp.zeros_like(sums_ref)

    grad = gn_ref[...] + got_ref[...].astype(f32)
    xhat, scale = norm_parts(mid_ref[...])
    g = g_ref[...].astype(f32)
    grad_mid = g + norm_back(grad, xhat, scale, vector(vec_ref, "gain_two"))
    gmid_ref[...] = grad_mid
    low = grad_mid.astype(bf16)
    gatt_ref[...] = mm(wo[...], low).astype(bf16)
    gwo_sum[...] += mm(low, att_ref[...], NT)
    sums_ref[0] += fold(low.astype(f32))
    sums_ref[1] += fold(grad * xhat)
    sums_ref[2] += fold(grad)
    sums_ref[3] += fold(g)

    @pl.when(i == pl.num_programs(0) - 1)
    def _():
        gwo_ref[...] = gwo_sum[...].astype(bf16)
        rows_ref[...] = row_sums([sums_ref[i] for i in range(4)])


def run_branch_back(gn, got, middle, g, att, w, vec):
    D, rows = att.shape
    cols = pl.BlockSpec((D, QT), lambda i: (0, i))
    shape = jax.ShapeDtypeStruct
    return pl.pallas_call(
        branch_back,
        grid=(rows // QT,),
        in_specs=[
            cols, cols, cols, cols, cols,
            whole((1, D, D), (3, 0, 0)),
            whole((D, LANES), (0, VEC_BLOCK)),
        ],
        out_specs=[cols, cols, whole((D, D)), whole((8, D))],
        out_shape=[
            shape((D, rows), f32),
            shape((D, rows), bf16),
            shape((D, D), bf16),
            shape((8, D), f32),
        ],
        scratch_shapes=[pltpu.VMEM((D, D), bf16), pltpu.VMEM((D, D), f32), pltpu.VMEM((4, D, LANES), f32)],
        name="branch_back",
        **kernel_params(9),
    )(gn, got, middle, g, att, w, vec)


def feed_forward(first, final, ahead, places, *refs):
    blocks, weights = len(places), 1 + max(p[0] for place in places for p in place)
    n2_in, g_in, refs = refs[0:2], refs[2:4], refs[4:]
    weights, refs = refs[:weights], refs[weights:]
    if not first:
        sums_in, refs = refs[:4], refs[4:]
    refs = refs[ahead:]
    sums_out, refs = refs[:4], refs[4:]
    dw_out, refs = refs[: 2 * blocks], refs[2 * blocks :]
    dub_out, refs = refs[:blocks], refs[blocks:]
    n2, g, up, dt, ub, up_t, down, act, gh, dw, sums, low, in_sem, out_sem = refs
    D, F = up.shape
    f, rows = F // blocks, n2.shape[2]

    arrivals = {}

    def fetch(name, source, target):
        copy = pltpu.make_async_copy(source, target, in_sem.at[len(arrivals)])
        copy.start()
        arrivals[name] = copy

    def weight(name, target, b, part):
        ref, at = places[b][part]
        fetch((name, b), weights[ref].at[:, at : at + f], target.at[:, b * f : (b + 1) * f])

    for b in range(blocks):
        weight("up", up, b, 0)
    fetch("n2", n2_in[0], n2.at[0])
    for b in range(blocks):
        weight("dt", dt, b, 1)
        ref, at = places[b][2]
        fetch(("ub", b), weights[ref].at[at : at + 16], ub.at[b])
    fetch("g", g_in[0], g.at[0])
    fetch("n2 other", n2_in[1], n2.at[1])
    fetch("g other", g_in[1], g.at[1])
    if not first:
        for i in range(4):
            fetch(("sum", i), sums_in[i], low.at[i])

    departures = []

    def send(source, target):
        copy = pltpu.make_async_copy(source, target, out_sem.at[len(departures)])
        copy.start()
        departures.append(copy)

    columns = []
    for b in range(blocks):
        arrivals["up", b].wait()
        up_t[b * f : (b + 1) * f, :] = up[:, b * f : (b + 1) * f].T
    for b in range(blocks):
        arrivals["dt", b].wait()
        down[b * f : (b + 1) * f, :] = dt[:, b * f : (b + 1) * f].T
        arrivals["ub", b].wait()
        column = ub[b, :, :f].astype(f32).T[:, 0:1]
        columns.append(jnp.broadcast_to(column, (f, LANES)))
    bias = jnp.concatenate([jnp.concatenate(columns, axis=0)] * (QT // LANES), axis=1)
    arrivals["n2"].wait()
    arrivals["g"].wait()

    chunks = [(half, at) for half in range(2) for at in range(0, rows, QT)]

    def front(chunk):
        half, at = chunk
        if half == 1 and at == 0:
            arrivals["n2 other"].wait()
            arrivals["g other"].wait()
        return mm(up_t[...], n2[half, :, at : at + QT]), mm(down[...], g[half, :, at : at + QT])

    dub = jnp.zeros((F, LANES), f32)
    ready = front(chunks[0])
    for i, (half, at) in enumerate(chunks):
        following = front(chunks[i + 1]) if i + 1 < len(chunks) else None
        hidden, grad_act = ready
        hidden = hidden + bias
        cdf, pdf = normal_cdf(hidden)
        act[half, :, at : at + QT] = (hidden * cdf).astype(bf16)
        grad_hidden = (grad_act * (cdf + hidden * pdf)).astype(bf16)
        gh[half, :, at : at + QT] = grad_hidden
        dub = dub + fold(grad_hidden.astype(f32))
        ready = following
    for b in range(blocks):
        dub_out[b][...] = row_sums([dub[b * f : (b + 1) * f]])
    for part, (left, right) in enumerate(((n2, gh), (g, act))):
        dw[part] = (mm(left[0], right[0], NT) + mm(left[1], right[1], NT)).astype(bf16)
        for b in range(blocks):
            send(dw.at[part, :, b * f : (b + 1) * f], dw_out[2 * b + part])
    if not first:
        for i in range(4):
            arrivals["sum", i].wait()
    for i, (left, right) in enumerate(((up, gh), (dt, act))):
        for half in (1, 0):
            total = mm(left[...], right[half])
            k = 2 * i + half
            if not first:
                total = total + low[k].astype(f32)
            if half == 1 or not final:
                low[k] = total.astype(bf16)
                send(low.at[k], sums_out[k])
            else:
                sums[i] = total
                send(sums.at[i], sums_out[k])
    for copy in departures:
        copy.wait()


def run_feed_forward(n2, g, blocks, sums, final=False, ahead=()):
    D, rows = n2[0].shape
    F = D
    first = sums is None
    weights, places = [], []
    for block in blocks:
        place = []
        for array, column in block:
            found = [i for i, w in enumerate(weights) if w is array]
            if not found:
                weights.append(array)
            place.append((found[0] if found else len(weights) - 1, column))
        places.append(place)
    sums = () if first else tuple(sums)
    count = len(blocks)
    shape = jax.ShapeDtypeStruct
    anywhere = pl.BlockSpec(memory_space=pl.ANY)
    vmem = pl.BlockSpec(memory_space=pltpu.VMEM)
    own_type = f32 if final else bf16
    outs = pl.pallas_call(
        functools.partial(feed_forward, first, final, len(ahead), places),
        in_specs=[anywhere] * (4 + len(weights) + len(sums) + len(ahead)),
        out_specs=[anywhere] * (4 + 2 * count) + [vmem] * count,
        out_shape=[shape((D, rows), t) for t in (own_type, bf16, own_type, bf16)]
        + [shape((D, F), bf16)] * (2 * count)
        + [shape((8, F), f32)] * count,
        scratch_shapes=[
            pltpu.VMEM((2, D, rows), bf16),
            pltpu.VMEM((2, D, rows), bf16),
            pltpu.VMEM((D, count * F), bf16),
            pltpu.VMEM((D, count * F), bf16),
            pltpu.VMEM((count, 16, D), bf16),
            pltpu.VMEM((count * F, D), bf16),
            pltpu.VMEM((count * F, D), bf16),
            pltpu.VMEM((2, count * F, rows), bf16),
            pltpu.VMEM((2, count * F, rows), bf16),
            pltpu.VMEM((2, D, count * F), bf16),
            pltpu.VMEM((2, D, rows), f32),
            pltpu.VMEM((4, D, rows), bf16),
            pltpu.SemaphoreType.DMA((3 * count + 8,)),
            pltpu.SemaphoreType.DMA((2 * count + 4,)),
        ],
        name="feed_forward",
        **kernel_params(14 * count),
    )(*n2, *g, *weights, *sums, *ahead)
    grads = [(*outs[4 + 2 * b : 6 + 2 * b], outs[4 + 2 * count + b]) for b in range(count)]
    return outs[:4], grads


def z_rotate(x, k):
    n = lax.axis_size("narrow")
    return lax.ppermute(x, "narrow", [(i, (i + k) % n) for i in range(n)])


def z_gather(x):
    n, me = lax.axis_size("narrow"), lax.axis_index("narrow")
    stack = jnp.stack([x] + [z_rotate(x, k) for k in range(1, n)])
    return [lax.dynamic_index_in_dim(stack, lax.rem(me - j + n, n), 0, False) for j in range(n)]


def z_scatter_sum(pieces):
    n, me = lax.axis_size("narrow"), lax.axis_index("narrow")
    total = lax.dynamic_index_in_dim(pieces, me, 0, False).astype(f32)
    for k in range(1, n):
        piece = lax.dynamic_index_in_dim(pieces, lax.rem(me + k, n), 0, False)
        total = total + z_rotate(piece, k).astype(f32)
    return total


def swap(x, mask):
    n = lax.axis_size("wide")
    return lax.ppermute(x, "wide", [(i, i ^ mask) for i in range(n)])


def wide_sum(x):
    bit = 1
    while bit < lax.axis_size("wide"):
        x = x + swap(x, bit)
        bit *= 2
    return x


CORE, X, Y = 1, 2, 4


def after(deps, *values):
    n = len(values)
    tied = pl.pallas_call(
        lambda *refs: None,
        in_specs=[pl.BlockSpec(memory_space=pl.ANY)] * (n + len(deps)),
        out_specs=[pl.BlockSpec(memory_space=pl.ANY)] * n,
        out_shape=[jax.ShapeDtypeStruct(v.shape, v.dtype) for v in values],
        input_output_aliases={i: i for i in range(n)},
        name="tie",
    )(*values, *deps)
    return tied if n > 1 else tied[0]


def high_bits():
    bits, bit = [], 8
    while bit < lax.axis_size("wide"):
        bits.append(bit)
        bit *= 2
    return bits


def shards(
    tokens_in,
    ln1_gain,
    ln1_shift,
    w_qkv,
    qv_bias,
    w_out,
    out_bias,
    ln2_gain,
    ln2_shift,
    w_up,
    up_bias,
    w_down,
    down_bias,
    segment_ids,
    out_grad,
    predicted,
    labels,
):
    nn, me = lax.axis_size("narrow"), lax.axis_index("narrow")
    nw, mw = lax.axis_size("wide"), lax.axis_index("wide")
    part, tok = tokens_in.shape
    D = part * nn
    quarter = tok // nn
    halo = LONGEST
    span = quarter + 2 * halo
    high = high_bits()
    dw = w_qkv.shape[1]
    across = lambda x: lax.all_to_all(x, "narrow", 0, 0, tiled=True)

    position = jnp.arange(tok, dtype=jnp.int32)
    chunk = segment_ids * (tok // SEQ) + position // SEQ
    big = jnp.int32(2**30)
    chunk = jnp.concatenate([jnp.full((halo,), -1, jnp.int32), chunk, jnp.full((halo,), big, jnp.int32)])
    chunk = lax.dynamic_slice_in_dim(chunk, me * quarter, span, 0)
    chunk_own = chunk[halo : halo + quarter]
    tiles = quarter // QT
    edges = chunk_own.reshape(tiles, QT)
    low = jnp.sum((chunk[None] < edges[:, :1]).astype(jnp.int32), axis=1) // KT
    top = (jnp.sum((chunk[None] <= edges[:, -1:]).astype(jnp.int32), axis=1) + KT - 1) // KT
    small = (top - low <= 4).astype(jnp.int32)
    starts = jnp.minimum(low, span // KT - jnp.where(small == 1, 4, 6))
    segk = jnp.broadcast_to(chunk[:, None], (span, LANES))
    segq = jnp.broadcast_to(chunk_own[None], (8, quarter))

    vectors = [ln1_gain, ln1_shift, qv_bias, out_bias, ln2_gain, ln2_shift, down_bias]
    piece = run_pack(w_qkv, w_out, vectors, nn)
    vec = across(piece).reshape(D, -1)
    up_own = across(after((vec,), jnp.stack([w_up] * nn))).reshape(D, -1)
    units = up_bias.shape[0]
    bias_rows = jnp.pad(up_bias[None], ((0, 15), (0, D - units)))
    attn_own = after((vec,), jnp.concatenate([vec[:, : 4 * dw].T, bias_rows], axis=0))
    count, height = 1, 4 * dw + 16
    for bit in high:
        attn_own = jnp.concatenate([attn_own, swap(attn_own, bit)], axis=0)
        count *= 2
    cut = attn_own.shape[0] // 2 // 16 * 16
    from_x, from_y = swap(attn_own, X), swap(attn_own, Y)
    from_xy = swap(from_y[:cut], X), swap(from_x[cut:], Y)
    grad_blocks = jnp.stack([out_grad[:, j * quarter : (j + 1) * quarter] for j in range(nn)])
    padded = jnp.pad(tokens_in, ((0, 0), (halo, halo)))
    blocks = jnp.stack([padded[:, j * quarter : j * quarter + span] for j in range(nn)])
    blocks = after((starts, small, segk, segq, up_own, *from_xy, grad_blocks), blocks)
    x_low = across(blocks).reshape(D, span)
    dt_blocks = after((x_low,), jnp.stack([w_down.T] * nn))
    dt_own = across(dt_blocks).reshape(D, -1)
    bias_of = lambda a: jnp.concatenate(
        [a[j * height + 4 * dw : (j + 1) * height, :units] for j in range(count)], axis=1
    )
    if dw % 16 == 0:
        pieces = [attn_own, from_x, from_y, *from_xy]
        pieces += [swap(piece, CORE) for piece in pieces]
        parts = []
        for far in (0, 1):
            for i, mask in enumerate((0, X, Y)):
                parts += [(i + 5 * far, c * dw, dw, c, mask | far * CORE) for c in range(4)]
            for c in range(4):
                for first, last in ((c * dw, min((c + 1) * dw, cut)), (max(c * dw, cut), (c + 1) * dw)):
                    assert last <= first or last - first == dw
                    if last > first:
                        piece, start = (3, first) if last <= cut else (4, first - cut)
                        parts.append((piece + 5 * far, start, dw, c, (X | Y) | far * CORE))
        ub_own, ub_x, ub_y = (attn_own, 4 * dw), (from_x, 4 * dw), (from_y, 4 * dw)
        ub_xy = from_xy[1], 4 * dw - cut
    else:
        from_xy = jnp.concatenate(from_xy, axis=0)
        ub_own, ub_x, ub_y, ub_xy = ((bias_of(a), 0) for a in (attn_own, from_x, from_y, from_xy))
        half = jnp.concatenate([attn_own, from_x, from_y, from_xy], axis=0)
        half = half.reshape(-1, height, D)[:, : 4 * dw].reshape(-1, 4, dw, D)
        every = jnp.concatenate([half, swap(half, CORE)], axis=0)
        bits = high + [X, Y, CORE]
        place = lambda m: sum(((m // bit) % 2) << i for i, bit in enumerate(bits))
        every = [lax.dynamic_index_in_dim(every, place(mw ^ w), 0, True) for w in range(nw)]
        pieces = [jnp.concatenate(every, axis=0).transpose(1, 0, 2, 3).reshape(4 * D, D)]
        parts = [(0, c * D, D, c, 0) for c in range(4)]
    member = jnp.reshape(mw if dw % 16 == 0 else mw * 0, (1,)).astype(jnp.int32)

    for bit in high:
        up_own = jnp.concatenate([up_own, swap(up_own, bit)], axis=1)
    F = up_own.shape[1]
    up_x, up_y = swap(up_own, X), swap(up_own, Y)
    normed, qt, kt, vt, k, v, w_attn = run_project(x_low, vec, member, pieces, parts, (up_x, up_y))
    groups = D // LANES
    forward_in = starts, small, qt, k, vt, segk, segq
    att, lse = run_forward(*forward_in, (0, 1))

    dt_own = after((att,), dt_own)
    grad_cols = across(after((dt_own,), grad_blocks)).reshape(D, quarter)
    for bit in high:
        dt_own = jnp.concatenate([dt_own, swap(dt_own, bit)], axis=1)
    dt_x, dt_y = swap(dt_own, X), swap(dt_own, Y)
    up_xy = swap(up_y, X)
    att, lse = run_forward(*forward_in, (1, 3), (att, lse), (up_xy,))
    dt_x = after((att,), dt_x)
    dt_xy = swap(dt_x, Y)
    att, lse = run_forward(*forward_in, (3, groups), (att, lse))
    grad_cols = after((att,), grad_cols)
    grad_pair = grad_cols, swap(grad_cols, CORE)
    middle, normed_two = run_branch(att, w_attn, x_low, vec)

    normed_two = after((dt_xy,), normed_two)
    n2_pair = normed_two, swap(normed_two, CORE)
    blocks = [((up_xy, 0), (dt_xy, 0), ub_xy), ((up_x, 0), (dt_x, 0), ub_x)]
    sums, ((up_gxy, dt_gxy, ub_gxy), (up_gx, dt_gx, ub_gx)) = run_feed_forward(n2_pair, grad_pair, blocks, None)
    up_got_xy, dt_got_xy = swap(up_gxy, X), swap(dt_gxy, Y)
    up_got_x = swap(up_gx, X)
    blocks = [((up_y, 0), (dt_y, 0), ub_y)]
    sums, ((up_gy, dt_gy, ub_gy),) = run_feed_forward(n2_pair, grad_pair, blocks, sums)
    add = lambda *terms: sum(t.astype(f32) for t in terms)
    dt_got_y = swap(dt_gy, Y)
    up_gy, dt_gx = add(up_gy, up_got_xy).astype(bf16), add(dt_gx, dt_got_xy).astype(bf16)
    up_got_y, dt_got_x = swap(up_gy, Y), swap(dt_gx, X)
    blocks = [((up_own, 0), (dt_own, 0), ub_own)]
    sums, ((up_g, dt_g, ub_g),) = run_feed_forward(n2_pair, grad_pair, blocks, sums, True, (up_gy, dt_gx))
    gn_sum, gn_other, out_sum, out_other = sums
    gn_got, out_got = swap(gn_other, CORE), swap(out_other, CORE)

    layer = (middle + (out_sum + out_got.astype(f32) + vec[:, VEC_LAST : VEC_LAST + 1].astype(f32))).astype(bf16)
    layer_out = across(layer.reshape(nn, part, quarter)).transpose(1, 0, 2).reshape(part, tok)

    gn_got = after((layer,), gn_got)
    grad_mid, grad_att, grad_wo_t, sums_two = run_branch_back(
        gn_sum, gn_got, middle, grad_cols, att, w_attn, vec
    )
    back_in = starts, small, qt, kt, k, v, grad_att, att, lse, segk, segq
    back_a = run_backward(*back_in, (0, 3))
    up_got_x, up_got_y, dt_got_x, dt_got_y = after((back_a[0],), up_got_x, up_got_y, dt_got_x, dt_got_y)
    up_g, dt_g = add(up_g, up_got_x, up_got_y), add(dt_g, dt_got_x, dt_got_y)
    for bit in reversed(high):
        half = up_g.shape[1] // 2
        up_g = up_g[:, :half] + swap(up_g[:, half:].astype(bf16), bit).astype(f32)
        dt_g = dt_g[:, :half] + swap(dt_g[:, half:].astype(bf16), bit).astype(f32)
    ud_g = jnp.concatenate([up_g, dt_g], axis=1).astype(bf16)
    ud_grad = z_scatter_sum(ud_g.reshape(nn, part, -1))
    dqt, dk, dv = run_backward(*back_in, (3, groups), back_a, (ud_g, layer_out))
    masks = [0]
    for bit in high:
        masks = masks + [m ^ bit for m in masks]
    masks = [m ^ b for b in (0, X, Y, X | Y) for m in masks]
    direct = masks if dw % 16 == 0 else []
    *grad_w, qv_rows = run_project_weights(normed, dqt, dk, dv, grad_wo_t, member, direct, dw)
    if not direct:
        grad_w = grad_w[0].reshape(4, nw, dw, D).transpose(1, 0, 2, 3)
        pick = lambda masks: jnp.concatenate(
            [lax.dynamic_index_in_dim(grad_w, mw ^ m, 0, True) for m in masks], axis=0
        )
        grad_w = pick(masks), pick([m ^ CORE for m in masks])
    attn_g, got = grad_w[0], swap(grad_w[1], CORE)
    grad_in, sums_one = run_project_back(x_low, dqt, dk, dv, w_attn, grad_mid, vec, (grad_w[1],))
    got = after((grad_in,), got)
    vector_rows = jnp.concatenate([sums_one[:2], qv_rows[:2], sums_two[:4]])
    up_grad, down_grad = ud_grad[:, :units], ud_grad[:, units:].T
    grad_in = across(grad_in.reshape(nn, part, span)).astype(f32)
    tokens_grad = sum(
        jnp.pad(grad_in[j], ((0, 0), (j * quarter, tok - (j + 1) * quarter))) for j in range(nn)
    )[:, halo : halo + tok]

    half = add(attn_g, got).astype(bf16)
    g0, gx, gy, gxy = (half[i * count : (i + 1) * count] for i in range(4))
    gy_low = add(gy[:, :2], swap(gxy[:, :2], X)).astype(bf16)
    gx_high = add(gx[:, 2:], swap(gxy[:, 2:], Y)).astype(bf16)
    gx = jnp.concatenate([gx[:, :2], gx_high], axis=1)
    gy = jnp.concatenate([gy_low, gy[:, 2:]], axis=1)
    ub_g, ub_gx, ub_gy, ub_gxy = (rows[0] for rows in after((gx, gy), ub_g, ub_gx, ub_gy, ub_gxy))
    ub_g = ub_g + swap(ub_gx, X) + swap(ub_gy, Y) + swap(ub_gxy, X | Y)
    for bit in reversed(high):
        cut = ub_g.shape[0] // 2
        ub_g = ub_g[:cut] + swap(ub_g[cut:], bit)
    ub_g = jnp.pad(ub_g[None], ((0, 0), (0, D - units)))
    vector_rows = after((gx, gy), vector_rows)
    g0 = add(g0, swap(gx, X), swap(gy, Y))
    for bit in reversed(high):
        cut = g0.shape[0] // 2
        g0 = g0[:cut] + swap(g0[cut:].astype(bf16), bit).astype(f32)
    g0 = g0[0].astype(bf16).reshape(4 * dw, D).T.reshape(nn, part, 4 * dw)
    attn_grad = z_scatter_sum(g0)
    qkv_grad = attn_grad[:, : 3 * dw].T.reshape(3, dw, part)
    out_weight_grad = attn_grad[:, 3 * dw :]

    class_ids = jnp.arange(CLASSES, dtype=jnp.int32)
    label_hits = labels[:, None] == class_ids
    counts = jnp.stack(
        [
            jnp.sum(((predicted[:, None] == class_ids) & label_hits).astype(f32), axis=0),
            jnp.sum(label_hits.astype(f32), axis=0),
        ]
    )
    counts = jnp.pad(counts.reshape(1, -1), ((0, 0), (0, D - counts.size)))
    sums = wide_sum(jnp.concatenate([vector_rows, counts]))
    counts = sums[8, : 2 * CLASSES].reshape(2, CLASSES)
    sums = after((g0,), jnp.concatenate([sums[:8], ub_g]))
    sums = sums + sum(z_rotate(sums, r) for r in range(1, nn))
    ub_g = sums[8, :units]
    sums = lax.dynamic_slice_in_dim(sums[:8], me * part, part, 1)
    gain_one_g, shift_one_g, q_bias_g, v_bias_g, out_bias_g, gain_two_g, shift_two_g, down_bias_g = sums
    tallies = counts.astype(jnp.int32)
    accuracy = jnp.sum(counts[0]) / jnp.maximum(jnp.sum(counts[1]), 1.0)
    return (
        layer_out,
        tokens_grad,
        gain_one_g,
        shift_one_g,
        qkv_grad,
        jnp.stack([q_bias_g, v_bias_g]),
        out_weight_grad,
        out_bias_g,
        gain_two_g,
        shift_two_g,
        up_grad,
        ub_g,
        down_grad,
        down_bias_g,
        tallies,
        accuracy,
    )


def solution(mesh):
    return jax.shard_map(
        shards,
        mesh=mesh,
        in_specs=(
            P("narrow", "wide"),
            P("narrow"),
            P("narrow"),
            P(None, "wide", "narrow"),
            P(None, "narrow"),
            P("narrow", "wide"),
            P("narrow"),
            P("narrow"),
            P("narrow"),
            P("narrow", "wide"),
            P("wide"),
            P("wide", "narrow"),
            P("narrow"),
            P("wide"),
            P("narrow", "wide"),
            P("wide"),
            P("wide"),
        ),
        out_specs=(
            P("narrow", "wide"),
            P("narrow", "wide"),
            P("narrow"),
            P("narrow"),
            P(None, "wide", "narrow"),
            P(None, "narrow"),
            P("narrow", "wide"),
            P("narrow"),
            P("narrow"),
            P("narrow"),
            P("narrow", "wide"),
            P("wide"),
            P("wide", "narrow"),
            P("narrow"),
            P(),
            P(),
        ),
        check_vma=False,
    )
```

```python
import functools

import jax
import jax.numpy as jnp
from jax import lax
from jax.experimental import pallas as pl
from jax.experimental.pallas import tpu as pltpu
from jax.sharding import PartitionSpec as P

HEAD_DIM = 32
SEQ = 1024
CLASSES = 4
LONGEST = 256
EPS = 1e-05
QT = 256
KT = 128
GROUP = 4
LANES = 128
LOG2E = 1.4426950408889634
SCALE = HEAD_DIM**-0.5
MASKED = -1e30
VMEM_LIMIT = 58 * 1024 * 1024
VEC_BLOCK, VEC_AT = 2, 64
VEC_LAST = VEC_BLOCK * 128 + VEC_AT + 7
bf16, f32 = jnp.bfloat16, jnp.float32

NN = (((1,), (0,)), ((), ()))
NT = (((1,), (1,)), ((), ()))
TN = (((0,), (0,)), ((), ()))

PHI_P = 0.33
PHI_C = (
    0.1328227541618569,
    0.117797452145417,
    0.18652846971894854,
    -0.09893620415601319,
    0.3406397450924515,
    -0.22542553879715763,
    0.046573313873415075,
)


def mm(left, right, dims=NN):
    return lax.dot_general(left, right, dims, preferred_element_type=f32)


def normal_cdf(u):
    bell = jnp.exp(-0.5 * (u * u))
    t = 1.0 / (1.0 + PHI_P * jnp.abs(u))
    tail = jnp.full_like(t, PHI_C[-1])
    for c in PHI_C[-2::-1]:
        tail = tail * t + c
    tail = tail * t * bell
    return jnp.where(u >= 0, 1.0 - tail, tail), bell * 0.3989422804014327


def head_only(block, h, axis):
    index = lax.broadcasted_iota(jnp.int32, block.shape, axis)
    keep = (index >= h * HEAD_DIM) & (index < (h + 1) * HEAD_DIM)
    return jnp.where(keep, block, jnp.zeros_like(block))


def key_bias(segk_ref, segq_ref, start, window):
    segk = segk_ref[pl.ds(start, window), :]
    segk = jnp.concatenate([segk] * (QT // LANES), axis=1)
    return jnp.where(segk == segq_ref[0:1, :], 0.0, MASKED).astype(f32)


def attend_forward(start_ref, small_ref, q_ref, k_ref, vt_ref, segk_ref, segq_ref, *refs):
    att_ref, lse_ref = refs[-2:]
    tile = pl.program_id(1)

    def run(window):
        start = pl.multiple_of(start_ref[tile] * KT, KT)
        keys = k_ref[pl.ds(start, window), :]
        bias = key_bias(segk_ref, segq_ref, start, window)
        q = q_ref[...]
        rows = [slice(h * HEAD_DIM, (h + 1) * HEAD_DIM) for h in range(GROUP)]
        scores = [mm(keys, head_only(q, h, 0)) for h in range(GROUP)]
        ready = []
        for h in range(GROUP):
            masked = scores[h] + bias
            top = jnp.max(masked, axis=0, keepdims=True)
            probs = jnp.exp2((masked - top) * (SCALE * LOG2E))
            total = jnp.sum(probs, axis=0, keepdims=True)
            lse_ref[h : h + 1, :] = top * (SCALE * LOG2E) + jnp.log2(total)
            ready.append((probs.astype(bf16), total))
        for h, (probs, total) in enumerate(ready):
            out = mm(vt_ref[rows[h], pl.ds(start, window)], probs)
            att_ref[rows[h], :] = (out / total).astype(bf16)

    @pl.when(small_ref[tile] == 1)
    def _():
        run(4 * KT)

    @pl.when(small_ref[tile] == 0)
    def _():
        run(6 * KT)


def attend_backward(
    start_ref, small_ref, qt_ref, kt_ref, k_ref, v_ref, dot_ref, att_ref, lse_ref, segk_ref, segq_ref, *refs
):
    dqt_ref, dk_ref, dv_ref, dk_sum, dv_sum = refs[-5:]
    tile = pl.program_id(1)

    @pl.when(tile == 0)
    def _():
        dk_sum[...] = jnp.zeros_like(dk_sum)
        dv_sum[...] = jnp.zeros_like(dv_sum)

    def run(window):
        start = pl.multiple_of(start_ref[tile] * KT, KT)
        at = pl.ds(start, window)
        keys, values = k_ref[at, :], v_ref[at, :]
        bias = key_bias(segk_ref, segq_ref, start, window)
        qt, dot = qt_ref[...], dot_ref[...]
        q, do = qt.T, dot.T
        inner = dot.astype(f32) * att_ref[...].astype(f32)
        rows = [slice(h * HEAD_DIM, (h + 1) * HEAD_DIM) for h in range(GROUP)]
        products = [(mm(keys, head_only(qt, h, 0)), mm(values, head_only(dot, h, 0))) for h in range(GROUP)]
        probs_low, grads_low = [], []
        for h, (scores, grad_probs) in enumerate(products):
            delta = jnp.sum(inner[rows[h], :], axis=0, keepdims=True)
            probs = jnp.exp2((scores * (SCALE * LOG2E) - lse_ref[h : h + 1, :]) + bias)
            probs_low.append(probs.astype(bf16))
            grads_low.append((probs * (grad_probs - delta)).astype(bf16))
        heads_of = lambda block: jnp.concatenate([head_only(block, h, 1) for h in range(GROUP)], axis=0)
        dv = mm(jnp.concatenate(probs_low, axis=1), heads_of(do))
        dk = mm(jnp.concatenate(grads_low, axis=1), heads_of(q))
        for h in range(GROUP):
            dq = mm(kt_ref[rows[h], at], grads_low[h])
            dqt_ref[rows[h], :] = (dq * SCALE).astype(bf16)
        dk_sum[at, :] += dk
        dv_sum[at, :] += dv

    @pl.when(small_ref[tile] == 1)
    def _():
        run(4 * KT)

    @pl.when(small_ref[tile] == 0)
    def _():
        run(6 * KT)

    @pl.when(tile == pl.num_programs(1) - 1)
    def _():
        dk_ref[...] = (dk_sum[...] * SCALE).astype(bf16)
        dv_ref[...] = dv_sum[...].astype(bf16)


def attention_specs(span, begin):
    spec = pl.BlockSpec
    return {
        "q_cols": spec((LANES, QT), lambda g, j, *_: (g + begin, j)),
        "k_cols": spec((LANES, span), lambda g, j, *_: (g + begin, 0)),
        "k_rows": spec((span, LANES), lambda g, j, *_: (0, g + begin)),
        "lse": spec((8, QT), lambda g, j, *_: (g + begin, j)),
        "segk": spec((span, LANES), lambda g, j, *_: (0, 0)),
        "segq": spec((8, QT), lambda g, j, *_: (0, j)),
    }


def run_forward(starts, small, qt, k, vt, segk, segq, span_of_groups, outs=(), first=()):
    D, rows = qt.shape
    span = k.shape[0]
    begin, end = span_of_groups
    s = attention_specs(span, begin)
    groups = D // LANES
    outs = tuple(outs)
    return pl.pallas_call(
        attend_forward,
        grid_spec=pltpu.PrefetchScalarGridSpec(
            num_scalar_prefetch=2,
            grid=(end - begin, rows // QT),
            in_specs=[s["q_cols"], s["k_rows"], s["k_cols"], s["segk"], s["segq"]]
            + [pl.BlockSpec(memory_space=pl.ANY)] * (len(outs) + len(first)),
            out_specs=[s["q_cols"], s["lse"]],
        ),
        input_output_aliases={7: 0, 8: 1} if outs else {},
        out_shape=[
            jax.ShapeDtypeStruct((D, rows), bf16),
            jax.ShapeDtypeStruct((groups * 8, rows), f32),
        ],
        name="attend_forward",
        **kernel_params(4 * (end - begin)),
    )(starts, small, qt, k, vt, segk, segq, *outs, *first)


def run_backward(starts, small, qt, kt, k, v, dot, att, lse, segk, segq, span_of_groups, outs=(), first=()):
    D, rows = qt.shape
    span = k.shape[0]
    begin, end = span_of_groups
    s = attention_specs(span, begin)
    outs = tuple(outs)
    return pl.pallas_call(
        attend_backward,
        grid_spec=pltpu.PrefetchScalarGridSpec(
            num_scalar_prefetch=2,
            grid=(end - begin, rows // QT),
            in_specs=[
                s["q_cols"], s["k_cols"], s["k_rows"], s["k_rows"], s["q_cols"], s["q_cols"],
                s["lse"], s["segk"], s["segq"],
            ]
            + [pl.BlockSpec(memory_space=pl.ANY)] * (len(outs) + len(first)),
            out_specs=[s["q_cols"], s["k_rows"], s["k_rows"]],
            scratch_shapes=[pltpu.VMEM((span, LANES), f32), pltpu.VMEM((span, LANES), f32)],
        ),
        out_shape=[
            jax.ShapeDtypeStruct((D, rows), bf16),
            jax.ShapeDtypeStruct((span, D), bf16),
            jax.ShapeDtypeStruct((span, D), bf16),
        ],
        input_output_aliases={11: 0, 12: 1, 13: 2} if outs else {},
        name="attend_backward",
        **kernel_params(6 * (end - begin)),
    )(starts, small, qt, kt, k, v, dot, att, lse, segk, segq, *outs, *first)


def norm_parts(cols):
    centre = jnp.mean(cols, axis=0, keepdims=True)
    shifted = cols - centre
    spread = jnp.mean(jnp.square(shifted), axis=0, keepdims=True)
    scale = lax.rsqrt(spread + EPS)
    return shifted * scale, scale


def norm_back(grad, xhat, scale, gain):
    e = grad * gain
    mean_e = jnp.mean(e, axis=0, keepdims=True)
    mean_ex = jnp.mean(e * xhat, axis=0, keepdims=True)
    return scale * (e - mean_e - xhat * mean_ex)


VECTORS = ("gain_one", "shift_one", "q_bias", "v_bias", "bias_out", "gain_two", "shift_two", "bias_down")


def vector(vec_ref, name):
    i = VEC_AT + VECTORS.index(name)
    return vec_ref[:, i : i + 1].astype(f32)


def fold(x):
    return sum(x[:, i : i + LANES] for i in range(0, x.shape[1], LANES))


def row_sums(parts):
    rows = [jnp.sum(part.T, axis=0, keepdims=True) for part in parts]
    return jnp.concatenate(rows + [jnp.zeros((8 - len(rows), rows[0].shape[1]), f32)], axis=0)


def whole(shape, block=None):
    return pl.BlockSpec(shape, lambda *_: (0,) * len(shape) if block is None else block)


def kernel_params(micros):
    return {
        "compiler_params": pltpu.CompilerParams(vmem_limit_bytes=VMEM_LIMIT),
        "cost_estimate": pl.CostEstimate(flops=micros * 10**9, bytes_accessed=10**6, transcendentals=0),
    }


def pack(qkv_ref, out_ref, *refs):
    vectors, (piece_ref, rows, turned) = refs[:-3], refs[-3:]
    part, dw = out_ref.shape
    rows[...] = jnp.zeros_like(rows)
    turned[...] = jnp.zeros_like(turned)
    turned[:part, :dw] = out_ref[...].astype(f32)
    for c in range(3):
        rows[c * dw : (c + 1) * dw, :part] = qkv_ref[c].astype(f32)
    rows[3 * dw : 4 * dw, :] = turned[...].T[:dw, :]
    at = VEC_BLOCK * LANES + VEC_AT
    for ref in vectors:
        count = ref.shape[0] if len(ref.shape) == 2 else 1
        rows[at : at + count, :part] = ref[...].reshape(count, part).astype(f32)
        at += count
    piece = rows[...].T[:part, :].astype(bf16)
    for n in range(piece_ref.shape[0]):
        piece_ref[n] = piece


def run_pack(w_qkv, w_out, vectors, members):
    part = w_out.shape[0]
    height, wide = (VEC_BLOCK + 1) * LANES, -(-part // LANES) * LANES
    return pl.pallas_call(
        pack,
        out_shape=jax.ShapeDtypeStruct((members, part, height), bf16),
        scratch_shapes=[pltpu.VMEM((height, wide), f32), pltpu.VMEM((wide, LANES), f32)],
        name="pack",
        **kernel_params(2),
    )(w_qkv, w_out, *vectors)


def project(parts, count, member_ref, x_ref, vec_ref, *refs):
    pieces, refs = refs[:count], refs[-11:]
    n_ref, qt_ref, kt_ref, vt_ref, k_ref, v_ref, w_ref, w, wt, in_sem, out_sem = refs
    i = pl.program_id(0)
    out = pltpu.make_async_copy(w, w_ref, out_sem)

    @pl.when(i == 0)
    def _():
        copies = []
        for piece, first, rows, c, mask in parts:
            at = pl.multiple_of((member_ref[0] ^ mask) * rows, 16)
            copy = pltpu.make_async_copy(
                pieces[piece].at[first : first + rows], w.at[c, pl.ds(at, rows)], in_sem.at[len(copies)]
            )
            copy.start()
            copies.append(copy)
        for copy in copies:
            copy.wait()
        out.start()
        for c in range(3):
            wt[c] = w[c].T

    xhat, _ = norm_parts(x_ref[...].astype(f32))
    normed = (xhat * vector(vec_ref, "gain_one") + vector(vec_ref, "shift_one")).astype(bf16)
    n_ref[...] = normed
    kt = mm(wt[1], normed).astype(bf16)
    vt = (mm(wt[2], normed) + vector(vec_ref, "v_bias")).astype(bf16)
    kt_ref[...], vt_ref[...] = kt, vt
    k_ref[...], v_ref[...] = kt.T, vt.T

    @pl.when((i >= 1) & (i < pl.num_programs(0) - 1))
    def _():
        qt_ref[...] = (mm(wt[0], normed) + vector(vec_ref, "q_bias")).astype(bf16)

    @pl.when(i == pl.num_programs(0) - 1)
    def _():
        out.wait()


def run_project(x, vec, member, pieces, parts, first):
    D, span = x.shape
    steps = span // QT
    cols = pl.BlockSpec((D, QT), lambda i, _: (0, i))
    rows = pl.BlockSpec((QT, D), lambda i, _: (i, 0))
    own = pl.BlockSpec((D, QT), lambda i, _: (0, jnp.clip(i - 1, 0, steps - 3)))
    anywhere = pl.BlockSpec(memory_space=pl.ANY)
    shape = jax.ShapeDtypeStruct
    return pl.pallas_call(
        functools.partial(project, parts, len(pieces)),
        grid_spec=pltpu.PrefetchScalarGridSpec(
            num_scalar_prefetch=1,
            grid=(steps,),
            in_specs=[cols, whole((D, LANES), (0, VEC_BLOCK))] + [anywhere] * (len(pieces) + len(first)),
            out_specs=[cols, own, cols, cols, rows, rows, anywhere],
            scratch_shapes=[
                pltpu.VMEM((4, D, D), bf16),
                pltpu.VMEM((3, D, D), bf16),
                pltpu.SemaphoreType.DMA((len(parts),)),
                pltpu.SemaphoreType.DMA,
            ],
        ),
        out_shape=[
            shape((D, span), bf16),
            shape((D, span - 2 * QT), bf16),
            shape((D, span), bf16),
            shape((D, span), bf16),
            shape((span, D), bf16),
            shape((span, D), bf16),
            shape((4, D, D), bf16),
        ],
        name="project",
        **kernel_params(11),
    )(member, x, vec, *pieces, *first)


def project_weights(masks, ahead, member_ref, n_ref, dqt_ref, dk_ref, dv_ref, gwo_ref, *refs):
    outs, (sums_ref, gw, sem) = refs[ahead:-3], refs[-3:]
    rows = dqt_ref.shape[1]
    halo = (n_ref.shape[1] - rows) // 2
    copies = []

    def send(c):
        if not masks:
            targets = [(gw.at[c], outs[0].at[c])]
        else:
            run = outs[0].shape[2]
            targets = []
            for far in (1, 0):
                for i, mask in enumerate(masks):
                    at = pl.multiple_of((member_ref[0] ^ (mask | far * CORE)) * run, 16)
                    targets.append((gw.at[c, pl.ds(at, run)], outs[far].at[i, c]))
        for source, target in targets:
            copy = pltpu.make_async_copy(source, target, sem.at[len(copies)])
            copy.start()
            copies.append(copy)

    gw[3] = gwo_ref[...]
    send(3)
    gw[0] = mm(n_ref[:, halo : halo + rows], dqt_ref[...], NT).astype(bf16)
    send(0)
    gw[1] = mm(n_ref[...], dk_ref[...]).astype(bf16)
    send(1)
    gw[2] = mm(n_ref[...], dv_ref[...]).astype(bf16)
    send(2)
    sums_ref[...] = row_sums([fold(dqt_ref[...].astype(f32))])
    sums_ref[1:2, :] = jnp.sum(dv_ref[...].astype(f32), axis=0, keepdims=True)
    for copy in copies:
        copy.wait()


def run_project_weights(normed, dqt, dk, dv, gwo, member, masks, run, first):
    D = normed.shape[0]
    shape = jax.ShapeDtypeStruct
    vmem, anywhere = pl.BlockSpec(memory_space=pltpu.VMEM), pl.BlockSpec(memory_space=pl.ANY)
    outs = [shape((len(masks), 4, run, D), bf16)] * 2 if masks else [shape((4, D, D), bf16)]
    return pl.pallas_call(
        functools.partial(project_weights, masks, len(first)),
        in_specs=[pl.BlockSpec(memory_space=pltpu.SMEM)] + [vmem] * 5 + [anywhere] * len(first),
        out_specs=[anywhere] * len(outs) + [vmem],
        out_shape=outs + [shape((8, D), f32)],
        scratch_shapes=[pltpu.VMEM((4, D, D), bf16), pltpu.SemaphoreType.DMA((8 * max(1, len(masks)),))],
        name="project_weights",
        **kernel_params(8),
    )(member, normed, dqt, dk, dv, gwo, *first)


def project_back(x_ref, dqt_ref, dk_ref, dv_ref, w_ref, mid_ref, vec_ref, run_ref, got_ref, *refs):
    grad_ref, rows_ref, both_ref, sums_ref = refs[-4:]
    i = pl.program_id(0)
    both_ref[...] = (run_ref[...].astype(f32) + got_ref[...].astype(f32)).astype(bf16)
    own = (i >= 1) & (i < pl.num_programs(0) - 1)

    @pl.when(i == 0)
    def _():
        sums_ref[...] = jnp.zeros_like(sums_ref)

    dqt = jnp.where(own, dqt_ref[...], jnp.zeros_like(dqt_ref))
    grad = mm(w_ref[1], dk_ref[...], NT) + mm(w_ref[2], dv_ref[...], NT) + mm(w_ref[0], dqt)
    xhat, scale = norm_parts(x_ref[...].astype(f32))
    sums_ref[0] += fold(grad * xhat)
    sums_ref[1] += fold(grad)
    grad_in = norm_back(grad, xhat, scale, vector(vec_ref, "gain_one"))
    grad_ref[...] = (grad_in + jnp.where(own, mid_ref[...], 0.0)).astype(bf16)

    @pl.when(i == pl.num_programs(0) - 1)
    def _():
        rows_ref[...] = row_sums([sums_ref[0], sums_ref[1]])


def run_project_back(x, dqt, dk, dv, w, grad_mid, vec, runs, got, first):
    D, span = x.shape
    steps = span // QT
    cols = pl.BlockSpec((D, QT), lambda i: (0, i))
    rows = pl.BlockSpec((QT, D), lambda i: (i, 0))
    own = pl.BlockSpec((D, QT), lambda i: (0, jnp.clip(i - 1, 0, steps - 3)))
    fourth = pl.BlockSpec((runs.shape[0] // 4, *runs.shape[1:]), lambda i: (jnp.minimum(i, 3), 0, 0, 0))
    shape = jax.ShapeDtypeStruct
    return pl.pallas_call(
        project_back,
        grid=(steps,),
        in_specs=[cols, own, rows, rows, whole((3, D, D)), own, whole((D, LANES), (0, VEC_BLOCK)), fourth, fourth]
        + [pl.BlockSpec(memory_space=pl.ANY)] * len(first),
        out_specs=[cols, whole((8, D)), fourth],
        out_shape=[shape((D, span), bf16), shape((8, D), f32), shape(runs.shape, bf16)],
        scratch_shapes=[pltpu.VMEM((2, D, LANES), f32)],
        name="project_back",
        **kernel_params(1),
    )(x, dqt, dk, dv, w, grad_mid, vec, runs, got, *first)


def branch(att_ref, wo_ref, x_ref, vec_ref, mid_ref, n_ref):
    out = mm(wo_ref[0], att_ref[...]) + vector(vec_ref, "bias_out")
    middle = x_ref[...].astype(f32) + out
    mid_ref[...] = middle
    xhat, _ = norm_parts(middle)
    n_ref[...] = (xhat * vector(vec_ref, "gain_two") + vector(vec_ref, "shift_two")).astype(bf16)


def run_branch(att, w, x, vec):
    D, rows = att.shape
    cols = pl.BlockSpec((D, QT), lambda i: (0, i))
    return pl.pallas_call(
        branch,
        grid=(rows // QT,),
        in_specs=[
            cols,
            whole((1, D, D), (3, 0, 0)),
            pl.BlockSpec((D, QT), lambda i: (0, i + LONGEST // QT)),
            whole((D, LANES), (0, VEC_BLOCK)),
        ],
        out_specs=[cols, cols],
        out_shape=[jax.ShapeDtypeStruct((D, rows), f32), jax.ShapeDtypeStruct((D, rows), bf16)],
        name="branch",
        **kernel_params(5),
    )(att, w, x, vec)


def branch_back(
    gn_ref, got_ref, mid_ref, g_ref, att_ref, wo_ref, vec_ref,
    gmid_ref, gatt_ref, gwo_ref, rows_ref, wo, gwo_sum, sums_ref,
):
    i = pl.program_id(0)

    @pl.when(i == 0)
    def _():
        wo[...] = wo_ref[0].T
        gwo_sum[...] = jnp.zeros_like(gwo_sum)
        sums_ref[...] = jnp.zeros_like(sums_ref)

    grad = gn_ref[...] + got_ref[...].astype(f32)
    xhat, scale = norm_parts(mid_ref[...])
    g = g_ref[...].astype(f32)
    grad_mid = g + norm_back(grad, xhat, scale, vector(vec_ref, "gain_two"))
    gmid_ref[...] = grad_mid
    low = grad_mid.astype(bf16)
    gatt_ref[...] = mm(wo[...], low).astype(bf16)
    gwo_sum[...] += mm(low, att_ref[...], NT)
    sums_ref[0] += fold(low.astype(f32))
    sums_ref[1] += fold(grad * xhat)
    sums_ref[2] += fold(grad)
    sums_ref[3] += fold(g)

    @pl.when(i == pl.num_programs(0) - 1)
    def _():
        gwo_ref[...] = gwo_sum[...].astype(bf16)
        rows_ref[...] = row_sums([sums_ref[i] for i in range(4)])


def run_branch_back(gn, got, middle, g, att, w, vec):
    D, rows = att.shape
    cols = pl.BlockSpec((D, QT), lambda i: (0, i))
    shape = jax.ShapeDtypeStruct
    return pl.pallas_call(
        branch_back,
        grid=(rows // QT,),
        in_specs=[
            cols, cols, cols, cols, cols,
            whole((1, D, D), (3, 0, 0)),
            whole((D, LANES), (0, VEC_BLOCK)),
        ],
        out_specs=[cols, cols, whole((D, D)), whole((8, D))],
        out_shape=[
            shape((D, rows), f32),
            shape((D, rows), bf16),
            shape((D, D), bf16),
            shape((8, D), f32),
        ],
        scratch_shapes=[pltpu.VMEM((D, D), bf16), pltpu.VMEM((D, D), f32), pltpu.VMEM((4, D, LANES), f32)],
        name="branch_back",
        **kernel_params(9),
    )(gn, got, middle, g, att, w, vec)


def feed_forward(first, final, ahead, places, *refs):
    blocks, weights = len(places), 1 + max(p[0] for place in places for p in place)
    n2_in, g_in, refs = refs[0:2], refs[2:4], refs[4:]
    weights, refs = refs[:weights], refs[weights:]
    if not first:
        sums_in, refs = refs[:4], refs[4:]
    refs = refs[ahead:]
    sums_out, refs = refs[:4], refs[4:]
    dw_out, refs = refs[: 2 * blocks], refs[2 * blocks :]
    dub_out, refs = refs[:blocks], refs[blocks:]
    n2, g, up, dt, ub, up_t, down, act, gh, dw, sums, low, in_sem, out_sem = refs
    D, F = up.shape
    f, rows = F // blocks, n2.shape[2]

    arrivals = {}

    def fetch(name, source, target):
        copy = pltpu.make_async_copy(source, target, in_sem.at[len(arrivals)])
        copy.start()
        arrivals[name] = copy

    def weight(name, target, b, part):
        ref, at = places[b][part]
        fetch((name, b), weights[ref].at[:, at : at + f], target.at[:, b * f : (b + 1) * f])

    for b in range(blocks):
        weight("up", up, b, 0)
    fetch("n2", n2_in[0], n2.at[0])
    for b in range(blocks):
        weight("dt", dt, b, 1)
        ref, at = places[b][2]
        fetch(("ub", b), weights[ref].at[at : at + 16], ub.at[b])
    fetch("g", g_in[0], g.at[0])
    fetch("n2 other", n2_in[1], n2.at[1])
    fetch("g other", g_in[1], g.at[1])
    if not first:
        for i in range(4):
            fetch(("sum", i), sums_in[i], low.at[i])

    departures = []

    def send(source, target):
        copy = pltpu.make_async_copy(source, target, out_sem.at[len(departures)])
        copy.start()
        departures.append(copy)

    columns = []
    for b in range(blocks):
        arrivals["up", b].wait()
        up_t[b * f : (b + 1) * f, :] = up[:, b * f : (b + 1) * f].T
    for b in range(blocks):
        arrivals["dt", b].wait()
        down[b * f : (b + 1) * f, :] = dt[:, b * f : (b + 1) * f].T
        arrivals["ub", b].wait()
        column = ub[b, :, :f].astype(f32).T[:, 0:1]
        columns.append(jnp.broadcast_to(column, (f, LANES)))
    bias = jnp.concatenate([jnp.concatenate(columns, axis=0)] * (QT // LANES), axis=1)
    arrivals["n2"].wait()
    arrivals["g"].wait()

    chunks = [(half, at) for half in range(2) for at in range(0, rows, QT)]

    def front(chunk):
        half, at = chunk
        if half == 1 and at == 0:
            arrivals["n2 other"].wait()
            arrivals["g other"].wait()
        return mm(up_t[...], n2[half, :, at : at + QT]), mm(down[...], g[half, :, at : at + QT])

    dub = jnp.zeros((F, LANES), f32)
    ready = front(chunks[0])
    for i, (half, at) in enumerate(chunks):
        following = front(chunks[i + 1]) if i + 1 < len(chunks) else None
        hidden, grad_act = ready
        hidden = hidden + bias
        cdf, pdf = normal_cdf(hidden)
        act[half, :, at : at + QT] = (hidden * cdf).astype(bf16)
        grad_hidden = (grad_act * (cdf + hidden * pdf)).astype(bf16)
        gh[half, :, at : at + QT] = grad_hidden
        dub = dub + fold(grad_hidden.astype(f32))
        ready = following
    for b in range(blocks):
        dub_out[b][...] = row_sums([dub[b * f : (b + 1) * f]])
    for part, (left, right) in enumerate(((n2, gh), (g, act))):
        dw[part] = (mm(left[0], right[0], NT) + mm(left[1], right[1], NT)).astype(bf16)
        for b in range(blocks):
            send(dw.at[part, :, b * f : (b + 1) * f], dw_out[2 * b + part])
    if not first:
        for i in range(4):
            arrivals["sum", i].wait()
    for i, (left, right) in enumerate(((up, gh), (dt, act))):
        for half in (1, 0):
            total = mm(left[...], right[half])
            k = 2 * i + half
            if not first:
                total = total + low[k].astype(f32)
            if half == 1 or not final:
                low[k] = total.astype(bf16)
                send(low.at[k], sums_out[k])
            else:
                sums[i] = total
                send(sums.at[i], sums_out[k])
    for copy in departures:
        copy.wait()


def run_feed_forward(n2, g, blocks, sums, final=False, ahead=()):
    D, rows = n2[0].shape
    F = D
    first = sums is None
    weights, places = [], []
    for block in blocks:
        place = []
        for array, column in block:
            found = [i for i, w in enumerate(weights) if w is array]
            if not found:
                weights.append(array)
            place.append((found[0] if found else len(weights) - 1, column))
        places.append(place)
    sums = () if first else tuple(sums)
    count = len(blocks)
    shape = jax.ShapeDtypeStruct
    anywhere = pl.BlockSpec(memory_space=pl.ANY)
    vmem = pl.BlockSpec(memory_space=pltpu.VMEM)
    own_type = f32 if final else bf16
    outs = pl.pallas_call(
        functools.partial(feed_forward, first, final, len(ahead), places),
        in_specs=[anywhere] * (4 + len(weights) + len(sums) + len(ahead)),
        out_specs=[anywhere] * (4 + 2 * count) + [vmem] * count,
        out_shape=[shape((D, rows), t) for t in (own_type, bf16, own_type, bf16)]
        + [shape((D, F), bf16)] * (2 * count)
        + [shape((8, F), f32)] * count,
        scratch_shapes=[
            pltpu.VMEM((2, D, rows), bf16),
            pltpu.VMEM((2, D, rows), bf16),
            pltpu.VMEM((D, count * F), bf16),
            pltpu.VMEM((D, count * F), bf16),
            pltpu.VMEM((count, 16, D), bf16),
            pltpu.VMEM((count * F, D), bf16),
            pltpu.VMEM((count * F, D), bf16),
            pltpu.VMEM((2, count * F, rows), bf16),
            pltpu.VMEM((2, count * F, rows), bf16),
            pltpu.VMEM((2, D, count * F), bf16),
            pltpu.VMEM((2, D, rows), f32),
            pltpu.VMEM((4, D, rows), bf16),
            pltpu.SemaphoreType.DMA((3 * count + 8,)),
            pltpu.SemaphoreType.DMA((2 * count + 4,)),
        ],
        name="feed_forward",
        **kernel_params(14 * count),
    )(*n2, *g, *weights, *sums, *ahead)
    grads = [(*outs[4 + 2 * b : 6 + 2 * b], outs[4 + 2 * count + b]) for b in range(count)]
    return outs[:4], grads


def z_rotate(x, k):
    n = lax.axis_size("narrow")
    return lax.ppermute(x, "narrow", [(i, (i + k) % n) for i in range(n)])


def z_gather(x):
    n, me = lax.axis_size("narrow"), lax.axis_index("narrow")
    stack = jnp.stack([x] + [z_rotate(x, k) for k in range(1, n)])
    return [lax.dynamic_index_in_dim(stack, lax.rem(me - j + n, n), 0, False) for j in range(n)]


def z_scatter(pieces):
    n, me = lax.axis_size("narrow"), lax.axis_index("narrow")
    piece = lambda k: lax.dynamic_index_in_dim(pieces, lax.rem(me + k, n), 0, False)
    return [piece(0)] + [z_rotate(piece(k), k) for k in range(1, n)]


def add(*terms):
    return sum(t.astype(f32) for t in terms)


def swap(x, mask):
    n = lax.axis_size("wide")
    return lax.ppermute(x, "wide", [(i, i ^ mask) for i in range(n)])


def wide_sum(x):
    bit = 1
    while bit < lax.axis_size("wide"):
        x = x + swap(x, bit)
        bit *= 2
    return x


CORE, X, Y = 1, 2, 4


def after(deps, *values):
    n = len(values)
    tied = pl.pallas_call(
        lambda *refs: None,
        in_specs=[pl.BlockSpec(memory_space=pl.ANY)] * (n + len(deps)),
        out_specs=[pl.BlockSpec(memory_space=pl.ANY)] * n,
        out_shape=[jax.ShapeDtypeStruct(v.shape, v.dtype) for v in values],
        input_output_aliases={i: i for i in range(n)},
        name="tie",
    )(*values, *deps)
    return tied if n > 1 else tied[0]


def high_bits():
    bits, bit = [], 8
    while bit < lax.axis_size("wide"):
        bits.append(bit)
        bit *= 2
    return bits


def shards(
    tokens_in,
    ln1_gain,
    ln1_shift,
    w_qkv,
    qv_bias,
    w_out,
    out_bias,
    ln2_gain,
    ln2_shift,
    w_up,
    up_bias,
    w_down,
    down_bias,
    segment_ids,
    out_grad,
    predicted,
    labels,
):
    nn, me = lax.axis_size("narrow"), lax.axis_index("narrow")
    nw, mw = lax.axis_size("wide"), lax.axis_index("wide")
    part, tok = tokens_in.shape
    D = part * nn
    quarter = tok // nn
    halo = LONGEST
    span = quarter + 2 * halo
    high = high_bits()
    dw = w_qkv.shape[1]
    across = lambda x: lax.all_to_all(x, "narrow", 0, 0, tiled=True)

    position = jnp.arange(tok, dtype=jnp.int32)
    chunk = segment_ids * (tok // SEQ) + position // SEQ
    big = jnp.int32(2**30)
    chunk = jnp.concatenate([jnp.full((halo,), -1, jnp.int32), chunk, jnp.full((halo,), big, jnp.int32)])
    chunk = lax.dynamic_slice_in_dim(chunk, me * quarter, span, 0)
    chunk_own = chunk[halo : halo + quarter]
    tiles = quarter // QT
    edges = chunk_own.reshape(tiles, QT)
    low = jnp.sum((chunk[None] < edges[:, :1]).astype(jnp.int32), axis=1) // KT
    top = (jnp.sum((chunk[None] <= edges[:, -1:]).astype(jnp.int32), axis=1) + KT - 1) // KT
    small = (top - low <= 4).astype(jnp.int32)
    starts = jnp.minimum(low, span // KT - jnp.where(small == 1, 4, 6))
    segk = jnp.broadcast_to(chunk[:, None], (span, LANES))
    segq = jnp.broadcast_to(chunk_own[None], (8, quarter))

    vectors = [ln1_gain, ln1_shift, qv_bias, out_bias, ln2_gain, ln2_shift, down_bias]
    piece = run_pack(w_qkv, w_out, vectors, nn)
    vec = across(piece).reshape(D, -1)
    up_own = across(after((vec,), jnp.stack([w_up] * nn))).reshape(D, -1)
    units = up_bias.shape[0]
    bias_rows = jnp.pad(up_bias[None], ((0, 15), (0, D - units)))
    attn_own = after((vec,), jnp.concatenate([vec[:, : 4 * dw].T, bias_rows], axis=0))
    count, height = 1, 4 * dw + 16
    for bit in high:
        attn_own = jnp.concatenate([attn_own, swap(attn_own, bit)], axis=0)
        count *= 2
    cut = attn_own.shape[0] // 2 // 16 * 16
    from_x, from_y = swap(attn_own, X), swap(attn_own, Y)
    from_xy = swap(from_y[:cut], X), swap(from_x[cut:], Y)
    grad_blocks = jnp.stack([out_grad[:, j * quarter : (j + 1) * quarter] for j in range(nn)])
    padded = jnp.pad(tokens_in, ((0, 0), (halo, halo)))
    blocks = jnp.stack([padded[:, j * quarter : j * quarter + span] for j in range(nn)])
    blocks = after((starts, small, segk, segq, up_own, *from_xy, grad_blocks), blocks)
    x_low = across(blocks).reshape(D, span)
    dt_blocks = after((x_low,), jnp.stack([w_down.T] * nn))
    dt_own = across(dt_blocks).reshape(D, -1)
    bias_of = lambda a: jnp.concatenate(
        [a[j * height + 4 * dw : (j + 1) * height, :units] for j in range(count)], axis=1
    )
    if dw % 16 == 0:
        pieces = [attn_own, from_x, from_y, *from_xy]
        pieces += [swap(piece, CORE) for piece in pieces]
        parts = []
        for far in (0, 1):
            for i, mask in enumerate((0, X, Y)):
                parts += [(i + 5 * far, c * dw, dw, c, mask | far * CORE) for c in range(4)]
            for c in range(4):
                for first, last in ((c * dw, min((c + 1) * dw, cut)), (max(c * dw, cut), (c + 1) * dw)):
                    assert last <= first or last - first == dw
                    if last > first:
                        piece, start = (3, first) if last <= cut else (4, first - cut)
                        parts.append((piece + 5 * far, start, dw, c, (X | Y) | far * CORE))
        ub_own, ub_x, ub_y = (attn_own, 4 * dw), (from_x, 4 * dw), (from_y, 4 * dw)
        ub_xy = from_xy[1], 4 * dw - cut
    else:
        from_xy = jnp.concatenate(from_xy, axis=0)
        ub_own, ub_x, ub_y, ub_xy = ((bias_of(a), 0) for a in (attn_own, from_x, from_y, from_xy))
        half = jnp.concatenate([attn_own, from_x, from_y, from_xy], axis=0)
        half = half.reshape(-1, height, D)[:, : 4 * dw].reshape(-1, 4, dw, D)
        every = jnp.concatenate([half, swap(half, CORE)], axis=0)
        bits = high + [X, Y, CORE]
        place = lambda m: sum(((m // bit) % 2) << i for i, bit in enumerate(bits))
        every = [lax.dynamic_index_in_dim(every, place(mw ^ w), 0, True) for w in range(nw)]
        pieces = [jnp.concatenate(every, axis=0).transpose(1, 0, 2, 3).reshape(4 * D, D)]
        parts = [(0, c * D, D, c, 0) for c in range(4)]
    member = jnp.reshape(mw if dw % 16 == 0 else mw * 0, (1,)).astype(jnp.int32)

    for bit in high:
        up_own = jnp.concatenate([up_own, swap(up_own, bit)], axis=1)
    F = up_own.shape[1]
    up_x, up_y = swap(up_own, X), swap(up_own, Y)
    normed, qt, kt, vt, k, v, w_attn = run_project(x_low, vec, member, pieces, parts, (up_x, up_y))
    groups = D // LANES
    forward_in = starts, small, qt, k, vt, segk, segq
    att, lse = run_forward(*forward_in, (0, 1))

    dt_own = after((att,), dt_own)
    grad_cols = across(after((dt_own,), grad_blocks)).reshape(D, quarter)
    for bit in high:
        dt_own = jnp.concatenate([dt_own, swap(dt_own, bit)], axis=1)
    dt_x, dt_y = swap(dt_own, X), swap(dt_own, Y)
    up_xy = swap(up_y, X)
    att, lse = run_forward(*forward_in, (1, 3), (att, lse), (up_xy,))
    dt_x = after((att,), dt_x)
    dt_xy = swap(dt_x, Y)
    att, lse = run_forward(*forward_in, (3, groups), (att, lse))
    grad_cols = after((att,), grad_cols)
    grad_pair = grad_cols, swap(grad_cols, CORE)
    middle, normed_two = run_branch(att, w_attn, x_low, vec)

    normed_two = after((dt_xy,), normed_two)
    n2_pair = normed_two, swap(normed_two, CORE)
    blocks = [((up_xy, 0), (dt_xy, 0), ub_xy), ((up_x, 0), (dt_x, 0), ub_x)]
    sums, ((up_gxy, dt_gxy, ub_gxy), (up_gx, dt_gx, ub_gx)) = run_feed_forward(n2_pair, grad_pair, blocks, None)
    up_got_xy, dt_got_xy = swap(up_gxy, X), swap(dt_gxy, Y)
    up_got_x = swap(up_gx, X)
    blocks = [((up_y, 0), (dt_y, 0), ub_y)]
    sums, ((up_gy, dt_gy, ub_gy),) = run_feed_forward(n2_pair, grad_pair, blocks, sums)
    dt_got_y = swap(dt_gy, Y)
    up_gy, dt_gx = add(up_gy, up_got_xy).astype(bf16), add(dt_gx, dt_got_xy).astype(bf16)
    up_got_y, dt_got_x = swap(up_gy, Y), swap(dt_gx, X)
    blocks = [((up_own, 0), (dt_own, 0), ub_own)]
    sums, ((up_g, dt_g, ub_g),) = run_feed_forward(n2_pair, grad_pair, blocks, sums, True, (up_gy, dt_gx))
    gn_sum, gn_other, out_sum, out_other = sums
    gn_got, out_got = swap(gn_other, CORE), swap(out_other, CORE)

    layer = (middle + (out_sum + out_got.astype(f32) + vec[:, VEC_LAST : VEC_LAST + 1].astype(f32))).astype(bf16)
    layer_out = across(layer.reshape(nn, part, quarter)).transpose(1, 0, 2).reshape(part, tok)

    gn_got = after((layer,), gn_got)
    grad_mid, grad_att, grad_wo_t, sums_two = run_branch_back(
        gn_sum, gn_got, middle, grad_cols, att, w_attn, vec
    )
    back_in = starts, small, qt, kt, k, v, grad_att, att, lse, segk, segq
    back_a = run_backward(*back_in, (0, 3))
    up_got_x, up_got_y, dt_got_x, dt_got_y = after((back_a[0],), up_got_x, up_got_y, dt_got_x, dt_got_y)
    up_g, dt_g = add(up_g, up_got_x, up_got_y), add(dt_g, dt_got_x, dt_got_y)
    for bit in reversed(high):
        half = up_g.shape[1] // 2
        up_g = up_g[:, :half] + swap(up_g[:, half:].astype(bf16), bit).astype(f32)
        dt_g = dt_g[:, :half] + swap(dt_g[:, half:].astype(bf16), bit).astype(f32)
    ud_g = jnp.concatenate([up_g, dt_g], axis=1).astype(bf16)
    ud_grad = z_scatter(ud_g.reshape(nn, part, -1))
    dqt, dk, dv = run_backward(*back_in, (3, groups), back_a, (ud_g, layer_out))
    masks = [0]
    for bit in high:
        masks = masks + [m ^ bit for m in masks]
    masks = [m ^ b for b in (0, X, Y, X | Y) for m in masks]
    direct = masks if dw % 16 == 0 else []
    *grad_w, qv_rows = run_project_weights(
        normed, dqt, dk, dv, grad_wo_t, member, direct, dw, ud_grad[1:2]
    )
    if not direct:
        grad_w = grad_w[0].reshape(4, nw, dw, D).transpose(1, 0, 2, 3)
        pick = lambda masks: jnp.concatenate(
            [lax.dynamic_index_in_dim(grad_w, mw ^ m, 0, True) for m in masks], axis=0
        )
        grad_w = pick(masks), pick([m ^ CORE for m in masks])
    attn_g, got = grad_w[0], swap(grad_w[1], CORE)
    grad_in, sums_one, half = run_project_back(
        x_low, dqt, dk, dv, w_attn, grad_mid, vec, attn_g, got, ()
    )
    vector_rows = jnp.concatenate([sums_one[:2], qv_rows[:2], sums_two[:4]])
    ud_grad = add(*ud_grad[:2], *(after((sums_one,), piece) for piece in ud_grad[2:]))
    up_grad, down_grad = ud_grad[:, :units], ud_grad[:, units:].T
    grad_in = across(grad_in.reshape(nn, part, span)).astype(f32)
    tokens_grad = sum(
        jnp.pad(grad_in[j], ((0, 0), (j * quarter, tok - (j + 1) * quarter))) for j in range(nn)
    )[:, halo : halo + tok]

    g0, gx, gy, gxy = (half[i * count : (i + 1) * count] for i in range(4))
    gy_low = add(gy[:, :2], swap(gxy[:, :2], X)).astype(bf16)
    gx_high = add(gx[:, 2:], swap(gxy[:, 2:], Y)).astype(bf16)
    gx = jnp.concatenate([gx[:, :2], gx_high], axis=1)
    gy = jnp.concatenate([gy_low, gy[:, 2:]], axis=1)
    ub_g, ub_gx, ub_gy, ub_gxy = (rows[0] for rows in after((gx, gy), ub_g, ub_gx, ub_gy, ub_gxy))
    ub_g = ub_g + swap(ub_gx, X) + swap(ub_gy, Y) + swap(ub_gxy, X | Y)
    for bit in reversed(high):
        cut = ub_g.shape[0] // 2
        ub_g = ub_g[:cut] + swap(ub_g[cut:], bit)
    ub_g = jnp.pad(ub_g[None], ((0, 0), (0, D - units)))
    vector_rows = after((gx, gy), vector_rows)
    g0 = add(g0, swap(gx, X), swap(gy, Y))
    for bit in reversed(high):
        cut = g0.shape[0] // 2
        g0 = g0[:cut] + swap(g0[cut:].astype(bf16), bit).astype(f32)
    g0 = g0[0].astype(bf16).reshape(4 * dw, D).T.reshape(nn, part, 4 * dw)
    attn_grad = add(*z_scatter(g0))
    qkv_grad = attn_grad[:, : 3 * dw].T.reshape(3, dw, part)
    out_weight_grad = attn_grad[:, 3 * dw :]

    class_ids = jnp.arange(CLASSES, dtype=jnp.int32)
    label_hits = labels[:, None] == class_ids
    counts = jnp.stack(
        [
            jnp.sum(((predicted[:, None] == class_ids) & label_hits).astype(f32), axis=0),
            jnp.sum(label_hits.astype(f32), axis=0),
        ]
    )
    counts = jnp.pad(counts.reshape(1, -1), ((0, 0), (0, D - counts.size)))
    sums = wide_sum(jnp.concatenate([vector_rows, counts]))
    counts = sums[8, : 2 * CLASSES].reshape(2, CLASSES)
    sums = after((g0,), jnp.concatenate([sums[:8], ub_g]))
    sums = sums + sum(z_rotate(sums, r) for r in range(1, nn))
    ub_g = sums[8, :units]
    sums = lax.dynamic_slice_in_dim(sums[:8], me * part, part, 1)
    gain_one_g, shift_one_g, q_bias_g, v_bias_g, out_bias_g, gain_two_g, shift_two_g, down_bias_g = sums
    tallies = counts.astype(jnp.int32)
    accuracy = jnp.sum(counts[0]) / jnp.maximum(jnp.sum(counts[1]), 1.0)
    return (
        layer_out,
        tokens_grad,
        gain_one_g,
        shift_one_g,
        qkv_grad,
        jnp.stack([q_bias_g, v_bias_g]),
        out_weight_grad,
        out_bias_g,
        gain_two_g,
        shift_two_g,
        up_grad,
        ub_g,
        down_grad,
        down_bias_g,
        tallies,
        accuracy,
    )


def solution(mesh):
    return jax.shard_map(
        shards,
        mesh=mesh,
        in_specs=(
            P("narrow", "wide"),
            P("narrow"),
            P("narrow"),
            P(None, "wide", "narrow"),
            P(None, "narrow"),
            P("narrow", "wide"),
            P("narrow"),
            P("narrow"),
            P("narrow"),
            P("narrow", "wide"),
            P("wide"),
            P("wide", "narrow"),
            P("narrow"),
            P("wide"),
            P("narrow", "wide"),
            P("wide"),
            P("wide"),
        ),
        out_specs=(
            P("narrow", "wide"),
            P("narrow", "wide"),
            P("narrow"),
            P("narrow"),
            P(None, "wide", "narrow"),
            P(None, "narrow"),
            P("narrow", "wide"),
            P("narrow"),
            P("narrow"),
            P("narrow"),
            P("narrow", "wide"),
            P("wide"),
            P("wide", "narrow"),
            P("narrow"),
            P(),
            P(),
        ),
        check_vma=False,
    )
```
